32 devices in a mesh: dp: 8 (over y, x, core), seq: 4 (over z).
Axes of the slice: x: 2, y: 2, z: 4, core: 2. Of those that a mesh axis runs over, the one named last changes fastest.
Arguments:
- x_short: bfloat16 [16, 512, 512], P('dp', 'seq'), may hold values from -6 to 6
- order_short: int32 [512], P('seq'), may hold values from 0 to 511, as said below
- x_long: bfloat16 [24, 1024, 512], P('dp', 'seq'), may hold values from -6 to 6
- order_long: int32 [1024], P('seq'), may hold values from 0 to 1023, as said below
- w_query: bfloat16 [512, 512], replicated, may hold values from -0.25 to 0.25
- w_key: bfloat16 [512, 512], replicated, may hold values from -0.25 to 0.25
- w_value: bfloat16 [512, 512], replicated, may hold values from -0.25 to 0.25
- w_out: bfloat16 [512, 512], replicated, may hold values from -2 to 2
- b_out: float32 [512], replicated, may hold values from -2 to 2
- alphas: float32 [2], replicated, may hold values from 0.5 to 1.5
- w_up: bfloat16 [512, 2048], replicated, may hold values from -0.25 to 0.25
- b_up: float32 [2048], replicated, may hold values from -3 to 3
- w_down: bfloat16 [2048, 512], replicated, may hold values from -0.125 to 0.125
- b_down: float32 [512], replicated, may hold values from -2 to 2
- cot_short: bfloat16 [16, 512, 512], P('dp', 'seq'), may hold values from -6 to 6
- cot_long: bfloat16 [24, 1024, 512], P('dp', 'seq'), may hold values from -6 to 6
Outputs:
- out_short: bfloat16 [16, 512, 512], P('dp', 'seq')
- out_long: bfloat16 [24, 1024, 512], P('dp', 'seq')
- dx_short: float32 [16, 512, 512], P('dp', 'seq')
- dx_long: float32 [24, 1024, 512], P('dp', 'seq')
- g_query: float32 [512, 512], replicated
- g_key: float32 [512, 512], replicated
- g_value: float32 [512, 512], replicated
- g_out: float32 [512, 512], replicated
- g_bout: float32 [512], replicated
- g_alphas: float32 [2], replicated
- g_up: float32 [512, 2048], replicated
- g_bup: float32 [2048], replicated
- g_down: float32 [2048, 512], replicated
- g_bdown: float32 [512], replicated
The draws below stay inside these ranges and needn't reach their ends.
Inputs may be any that keep to these rules, and one draw needn't show every extreme that they name: A permutation of paired runs: stored row j of every short sequence is the token at position order_short[j]. Positions fall into 2 * 4 runs of 512 // (2 * 4) consecutive positions; the k-th block of 512 // 4 stored rows holds in its first half the run c and in its second half the run 2 * 4 - 1 - c, for some c that differs from block to block; within a half the rows may be in any order. The same for the long sequences: stored row j is the token at position order_long[j], with runs of 1024 // (2 * 4) positions paired as above.
All inputs are finite; a program needn't handle non-finite values.
Results may differ from the reference program's by a relative error of at most 0.012.
The reference program's roundings to bfloat16 on the way count: a program that leaves them out, or rounds other values in their place, can miss the bound.
Values may be sent and summed in bfloat16 or wider, within the bound.
No kernel may reach another device: no remote copies, remote signals or barrier semaphores. Data moves between devices by JAX's collectives and lax.ppermute only.
A program may use at most 256 MiB of HBM per device.

```python
import math
import jax
import jax.numpy as jnp
from jax import lax

D = 512
HEADS = 8
HEAD_DIM = 64
FF = 2048
LA = 512
LB = 1024
NSA = 16
NSB = 24
N_SEQ = 4


def paired_runs_order(key, length):
    pieces = 2 * N_SEQ
    run_len = length // pieces
    pairing = jax.random.permutation(jax.random.fold_in(key, 1), N_SEQ).astype(jnp.int32)
    blocks = []
    for member in range(N_SEQ):
        first = pairing[member]
        for half, which in enumerate((first, pieces - 1 - first)):
            inside = jax.random.permutation(jax.random.fold_in(key, 100 + 2 * member + half), run_len).astype(jnp.int32)
            blocks.append(which * run_len + inside)
    return jnp.concatenate(blocks).astype(jnp.int32)


def draw_order_short(key, part):
    key = jax.random.fold_in(key, 11)
    return paired_runs_order(key, LA)


def draw_order_long(key, part):
    key = jax.random.fold_in(key, 23)
    return paired_runs_order(key, LB)


def block_scale(stream_key, extent, cuts, low, top_value):
    def one(dim, shards_of):
        heights = jax.random.uniform(jax.random.fold_in(jax.random.fold_in(stream_key, 6), dim), (shards_of,), jnp.float32, low / len(cuts), top_value / len(cuts))
        return jnp.repeat(jnp.exp(heights), extent[dim] // shards_of).reshape((-1,) + (1,) * (len(extent) - dim - 1))

    factor_of = one(*cuts[0])
    for cut in cuts[1:]:
        factor_of = factor_of * one(*cut)
    return factor_of


def scatter_about(own_key, extent, scale, bound, cuts=(), dtype=jnp.bfloat16):
    factor_of = block_scale(own_key, extent, cuts, -0.22, 0.18) if cuts else 1.0
    result = jax.random.normal(own_key, extent, jnp.float32) * scale * factor_of
    return jnp.minimum(jnp.maximum(result, -bound), bound).astype(dtype)


def setup_inputs(seed: int = 0) -> dict:
    seeds = jax.random.split(jax.random.key(seed), 17)
    return {
        "x_short": scatter_about(seeds[0], (NSA, LA, D), 1.0, 6.0, ((0, 8), (1, 4))),
        "order_short": draw_order_short(jax.random.fold_in(seeds[16], 71), 0),
        "x_long": scatter_about(seeds[2], (NSB, LB, D), 1.0, 6.0, ((0, 8), (1, 4))),
        "order_long": draw_order_long(jax.random.fold_in(seeds[16], 71), 0),
        "w_query": scatter_about(seeds[4], (D, D), D ** -0.5, 0.25),
        "w_key": scatter_about(seeds[5], (D, D), D ** -0.5, 0.25),
        "w_value": scatter_about(seeds[6], (D, D), D ** -0.5, 0.25),
        "w_out": scatter_about(seeds[7], (D, D), (D // 64) ** -0.5, 2.0),
        "b_out": scatter_about(seeds[8], (D,), 0.3, 2.0, (), jnp.float32),
        "alphas": jnp.clip(jax.random.uniform(seeds[9], (2,), jnp.float32, 0.5, 1.5), 0.5, 1.5),
        "w_up": scatter_about(seeds[10], (D, FF), D ** -0.5, 0.25),
        "b_up": scatter_about(seeds[11], (FF,), 0.5, 3.0, (), jnp.float32),
        "w_down": scatter_about(seeds[12], (FF, D), FF ** -0.5, 0.125),
        "b_down": scatter_about(seeds[13], (D,), 0.3, 2.0, (), jnp.float32),
        "cot_short": scatter_about(seeds[14], (NSA, LA, D), 1.0, 6.0, ((0, 8), (1, 4))),
        "cot_long": scatter_about(seeds[15], (NSB, LB, D), 1.0, 6.0, ((0, 8), (1, 4))),
    }


highest = lax.Precision.HIGHEST

@jax.custom_vjp
def low(v):
    return lax.optimization_barrier(v.astype(jnp.bfloat16)).astype(jnp.float32)

@jax.custom_vjp
def low_back(v):
    return v

def low_keep(v):
    return (low(v), None)

def low_pass(kept, grad):
    return (grad,)

def back_keep(v):
    return (v, None)

def back_low(kept, grad):
    return (low(grad),)
low.defvjp(low_keep, low_pass)
low_back.defvjp(back_keep, back_low)

def layer_block(seq_block, positions, params):
    w_query, w_key, w_value, w_out, b_out, alphas, w_up, b_up, w_down, b_down = params
    number_seqs, length, model_width = seq_block.shape
    flat_rows = seq_block.reshape(number_seqs * length, model_width)

    def project(weight):
        product = jnp.dot(flat_rows, weight, precision=highest)
        return low_back(low(product)).reshape(number_seqs, length, HEADS, HEAD_DIM)
    queries = project(w_query)
    key_rows = project(w_key)
    value_rows = project(w_value)
    scores = jnp.einsum('bqhe,bkhe->bhqk', queries, key_rows, precision=highest) * HEAD_DIM ** (-0.5)
    allowed = positions[:, None] >= positions[None, :]
    scores = low_back(jnp.where(allowed, scores, -1e+30))
    soft_weights = low(jax.nn.softmax(scores, axis=-1))
    attended = jnp.einsum('bhqk,bkhe->bqhe', soft_weights, value_rows, precision=highest)
    attended = low_back(low(attended.reshape(number_seqs * length, model_width)))
    branch = low_back(jnp.dot(attended, w_out, precision=highest) + b_out)
    middle = flat_rows + alphas[0] * branch
    hidden = low_back(jnp.dot(low(middle), w_up, precision=highest) + b_up)
    active = low(jax.nn.gelu(hidden))
    feed_out = low_back(jnp.dot(active, w_down, precision=highest) + b_down)
    return (middle + alphas[1] * feed_out).reshape(number_seqs, length, model_width)

def run_group(seq_rows, positions, params):
    number_seqs = seq_rows.shape[0]
    together = math.gcd(number_seqs, max(1, 4096 // seq_rows.shape[1]))
    blocks = seq_rows.reshape(number_seqs // together, together, seq_rows.shape[1], seq_rows.shape[2])
    one_block = jax.checkpoint(lambda seq_block: layer_block(seq_block, positions, params))
    return lax.map(one_block, blocks).reshape(seq_rows.shape)

def reference(x_short, order_short, x_long, order_long, w_query, w_key, w_value, w_out, b_out, alphas, w_up, b_up, w_down, b_down, cot_short, cot_long):
    params = tuple((item.astype(jnp.float32) for item in (w_query, w_key, w_value, w_out, b_out, alphas, w_up, b_up, w_down, b_down)))

    def forward(short_in, long_in, *weights):
        return (run_group(short_in, order_short, weights), run_group(long_in, order_long, weights))
    results, backward = jax.vjp(forward, x_short.astype(jnp.float32), x_long.astype(jnp.float32), *params)
    grads = backward((cot_short.astype(jnp.float32), cot_long.astype(jnp.float32)))
    return (results[0].astype(jnp.bfloat16), results[1].astype(jnp.bfloat16), grads[0], grads[1], grads[2], grads[3], grads[4], grads[5], grads[6], grads[7], grads[8], grads[9], grads[10], grads[11])
```

```python
import functools
import jax
import jax.numpy as jnp
from jax import lax
from jax.sharding import PartitionSpec as P
from jax.experimental import pallas as pl
from jax.experimental.pallas import tpu as pltpu

BF = jnp.bfloat16
F32 = jnp.float32
HEADS = 8
HD = 64
D = 512
FF = 2048
T = 1024
SUB = 64
NSUB = T // SUB
QB = 256
NQ = T // QB


def dot(a, b, ca=1, cb=0):
    return lax.dot_general(a, b, (((ca,), (cb,)), ((), ())), preferred_element_type=F32)


def params(mb):
    return pltpu.CompilerParams(vmem_limit_bytes=mb * 1024 * 1024)


def attn_fwd_body(dst, bias, c0, c1, c2, c3, mask, w, wt, xs, qh, kh, vh, qt, kt, vt, ot, att, lse, sem):
    copies = []
    for s in range(NSUB):
        src = (c0, c1, c2, c3)[s // 4].at[pl.ds((s % 4) * SUB, SUB)]
        copies.append(pltpu.make_async_copy(src, xs.at[pl.ds(pl.multiple_of(dst[s] * SUB, SUB), SUB)], sem.at[s]))
    for c in copies:
        c.start()
    for c in copies:
        c.wait()

    def proj(i, carry):
        rows = pl.ds(pl.multiple_of(i * QB, QB), QB)
        x = xs[rows, :]
        qkv = dot(x, w[...]).astype(BF)
        qkvt = dot(wt[...], x, 1, 1).astype(BF)
        for h in range(HEADS):
            qh[h, rows, :] = qkv[:, h * HD:(h + 1) * HD] * BF(0.125)
            kh[h, rows, :] = qkv[:, D + h * HD:D + (h + 1) * HD]
            vh[h, rows, :] = qkv[:, 2 * D + h * HD:2 * D + (h + 1) * HD]
        qt[:, rows] = qkvt[:D] * BF(0.125)
        kt[:, rows] = qkvt[D:2 * D]
        vt[:, rows] = qkvt[2 * D:]
        return carry

    lax.fori_loop(0, NQ, proj, 0)

    def head(h, carry):
        hr = pl.ds(pl.multiple_of(h * HD, HD), HD)
        for i in range(NQ):
            cols = pl.ds(i * QB, QB)
            q = qt[hr, cols]
            tiles, tops = [], []
            for j in range(i + 1):
                s = dot(kh[h, pl.ds(j * QB, QB), :], q)
                if j == i:
                    s = s + mask[i]
                    tops.append(jnp.max(s, axis=0, keepdims=True))
                else:
                    tops.append(jnp.max(s, axis=0, keepdims=True) + bias[i * NQ + j])
                tiles.append(s)
            m = functools.reduce(jnp.maximum, tops)
            total, o = None, None
            for j in range(i + 1):
                mj = m if j == i else m - bias[i * NQ + j]
                e = jnp.exp(tiles[j] - mj)
                t = jnp.sum(e, axis=0, keepdims=True)
                total = t if total is None else total + t
                p = dot(vt[hr, pl.ds(j * QB, QB)], e.astype(BF))
                o = p if o is None else o + p
            o = o * (1.0 / total)
            ot[hr, cols] = o
            lse[h, :, cols] = m + jnp.log(total)
        return carry

    lax.fori_loop(0, HEADS, head, 0)
    for i in range(NQ):
        rows = pl.ds(i * QB, QB)
        att[rows, :] = ot[:, rows].T.astype(BF)


def attn_fwd(dst, bias, chunks, mask, w, wt):
    s = jax.ShapeDtypeStruct
    hb = s((HEADS, T, HD), BF)
    tb = s((D, T), BF)
    anyspec = pl.BlockSpec(memory_space=pl.ANY)
    smem = pl.BlockSpec(memory_space=pltpu.SMEM)
    vmem = pl.BlockSpec(memory_space=pltpu.VMEM)
    return pl.pallas_call(
        attn_fwd_body,
        out_shape=(s((T, D), BF), hb, hb, hb, tb, tb, tb, s((D, T), F32), s((T, D), BF), s((HEADS, 1, T), F32)),
        in_specs=[smem, smem] + [anyspec] * 4 + [vmem] * 3,
        out_specs=(vmem,) * 10,
        scratch_shapes=[pltpu.SemaphoreType.DMA((NSUB,))],
        compiler_params=params(40),
        cost_estimate=pl.CostEstimate(flops=12_000_000_000, bytes_accessed=16_000_000, transcendentals=5_000_000),
        name="attn_fwd",
    )(dst, bias, *chunks, mask, w, wt)


FB = 256
NF = FF // FB
SLOTS = 32
R1 = 304
R2 = 96


def scatter_rows(dst, rows_ref, outs, sem):
    copies = []
    for s in range(NSUB):
        to = outs[s // 4].at[pl.ds((s % 4) * SUB, SUB)]
        copies.append(pltpu.make_async_copy(rows_ref.at[pl.ds(pl.multiple_of(dst[s] * SUB, SUB), SUB)], to, sem.at[s]))
    for c in copies:
        c.start()
    return copies


def gather_rows(dst, ins, rows_ref, sem):
    copies = []
    for s in range(NSUB):
        src = ins[s // 4].at[pl.ds((s % 4) * SUB, SUB)]
        copies.append(pltpu.make_async_copy(src, rows_ref.at[pl.ds(pl.multiple_of(dst[s] * SUB, SUB), SUB)], sem.at[s]))
    for c in copies:
        c.start()
    return copies


def put_slot(me, keep, send, part, s, row, rows, val):
    slot = jnp.bitwise_xor(s, me[part])
    at = pl.ds(row, rows)

    @pl.when(slot < SLOTS // 2)
    def _():
        keep[part, slot, at, :] = val

    @pl.when(slot >= SLOTS // 2)
    def _():
        send[part, slot - SLOTS // 2, at, :] = val


def top_row(vals):
    rows = lax.broadcasted_iota(jnp.int32, (16, 128), 0)
    return jnp.where(rows == 0, jnp.broadcast_to(vals, (16, 128)), 0.0).astype(BF)


def ffn_body(n_dev, dst, me, alphas, c0, c1, c2, c3, xs, att, ot, w_out, b_out, w_up, b_up, w_down, b_down,
             o0, o1, o2, o3, gm_out, doh, dott, inner, keep, send,
             cot, branch, middle, low, gfeed, feed, gm, out_rows, sem, sem2):
    f = pl.program_id(0)
    a0, a1 = alphas[0], alphas[1]

    @pl.when(f == 0)
    def _():
        copies = gather_rows(dst, (c0, c1, c2, c3), cot, sem)
        br = dot(att[...], w_out[...]) + b_out[...]
        branch[...] = br
        mid = xs[...].astype(F32) + a0 * br
        middle[...] = mid
        low[...] = mid.astype(BF)
        for c in copies:
            c.wait()
        g = cot[...].astype(F32)
        gfeed[...] = (a1 * g).astype(BF)
        gm[...] = g
        feed[...] = jnp.broadcast_to(b_down[...], feed.shape)

    hidden = dot(low[...], w_up[...]) + b_up[...]
    c = 0.7978845608028654
    h2 = hidden * hidden
    th = jnp.tanh(hidden * (c + (c * 0.044715) * h2))
    half = 0.5 + 0.5 * th
    active = (hidden * half).astype(BF)
    slope = half + (0.5 * hidden) * (1.0 - th * th) * (c + (3 * c * 0.044715) * h2)
    feed[...] += dot(active, w_down[...])
    grad_h = (dot(gfeed[...], w_down[...], 1, 1) * slope).astype(BF)
    bu = jnp.sum(grad_h.astype(F32), axis=0, keepdims=True)
    gd = dot(active, gfeed[...], 0, 0)
    gu = dot(low[...], grad_h, 0, 0)
    gm[...] += dot(grad_h, w_up[...], 1, 1)
    for b in range(2):
        for a in range(2):
            put_slot(me, keep, send, 0, 4 * f + 2 * b + a, 0, 256,
                     gu[a * 256:(a + 1) * 256, b * 128:(b + 1) * 128].astype(BF))
        put_slot(me, keep, send, 0, 2 * f + b, 288, 16, top_row(bu[:, b * 128:(b + 1) * 128]))
    for lb in range(4):
        put_slot(me, keep, send, 1, lb * 8 + f, 0, 256, gd[:, lb * 128:(lb + 1) * 128].astype(BF))

    @pl.when(f == NF - 1)
    def _():
        out_rows[...] = (middle[...] + a1 * feed[...]).astype(BF)
        copies = scatter_rows(dst, out_rows, (o0, o1, o2, o3), sem2)
        g = cot[...].astype(F32)
        s1 = jnp.sum(feed[...] * g)
        s0 = jnp.sum(branch[...] * gm[...])
        bd = jnp.sum(gfeed[...].astype(F32), axis=0, keepdims=True)
        gm_out[...] = gm[...]
        gb = (a0 * gm[...]).astype(BF)
        bo = jnp.sum(gb.astype(F32), axis=0, keepdims=True)
        go = dot(att[...], gb, 0, 0)
        da = dot(gb, w_out[...], 1, 1).astype(BF)
        for h in range(HEADS):
            doh[h] = da[:, h * HD:(h + 1) * HD]
        dt = dot(w_out[...], gb, 1, 1).astype(BF)
        dott[...] = dt
        for h in range(HEADS):
            hs = slice(h * HD, (h + 1) * HD)
            inner[h] = jnp.sum(ot[hs, :] * dt[hs, :].astype(F32), axis=0, keepdims=True)
        for s in range(SLOTS):
            lb, a = s // 8, s % 8
            for part in range(2):
                r0 = a * 64 + part * 32
                put_slot(me, keep, send, part, s, 256, 32, go[r0:r0 + 32, lb * 128:(lb + 1) * 128].astype(BF))
        for b in range(4):
            put_slot(me, keep, send, 0, 16 + b, 288, 16, top_row(bd[:, b * 128:(b + 1) * 128]))
            put_slot(me, keep, send, 0, 20 + b, 288, 16, top_row(bo[:, b * 128:(b + 1) * 128]))
        zero = jnp.zeros((16, 128), BF)
        for s in range(24, SLOTS):
            put_slot(me, keep, send, 0, s, 288, 16, zero)
        nr = (n_dev + 127) // 128
        row = lax.broadcasted_iota(jnp.int32, (SLOTS, 128), 0)
        lane = lax.broadcasted_iota(jnp.int32, (SLOTS, 128), 1)
        mine_row, mine_lane = me[2] // 128, me[2] % 128
        small = jnp.zeros((SLOTS, 128), F32)
        for k, total in enumerate((s0, s1)):
            rest = jnp.full((SLOTS, 128), total, F32)
            for t in range(3):
                piece = rest.astype(BF).astype(F32)
                rest = rest - piece
                here = (row == (3 * k + t) * nr + mine_row) & (lane == mine_lane)
                small = jnp.where(here, piece, small)
        for s in range(SLOTS):
            put_slot(me, keep, send, 1, s, 288, 16, top_row(small[s:s + 1]))
        for c in copies:
            c.wait()


def ffn(n_dev, dst, me, alphas, cots, xs, att, ot, w_out, b_out, w_up, b_up, w_down, b_down):
    s = jax.ShapeDtypeStruct
    anyspec = pl.BlockSpec(memory_space=pl.ANY)
    smem = pl.BlockSpec(memory_space=pltpu.SMEM)
    vmem = pl.BlockSpec(memory_space=pltpu.VMEM)
    v = pltpu.VMEM
    half = s((2, SLOTS // 2, R1, 128), BF)
    return pl.pallas_call(
        functools.partial(ffn_body, n_dev),
        grid=(NF,),
        out_shape=(s((256, D), BF),) * 4 + (s((T, D), F32), s((HEADS, T, HD), BF), s((D, T), BF),
                                            s((HEADS, 1, T), F32), half, half),
        in_specs=[smem, smem, smem] + [anyspec] * 4 + [vmem] * 5 + [
            pl.BlockSpec((D, FB), lambda f: (0, f)),
            pl.BlockSpec((1, FB), lambda f: (0, f)),
            pl.BlockSpec((FB, D), lambda f: (f, 0)),
            vmem,
        ],
        out_specs=(anyspec,) * 4 + (vmem,) * 6,
        scratch_shapes=[v((T, D), BF), v((T, D), F32), v((T, D), F32), v((T, D), BF), v((T, D), BF), v((T, D), F32),
                        v((T, D), F32), v((T, D), BF), pltpu.SemaphoreType.DMA((NSUB,)), pltpu.SemaphoreType.DMA((NSUB,))],
        compiler_params=params(56),
        cost_estimate=pl.CostEstimate(flops=15_000_000_000, bytes_accessed=20_000_000, transcendentals=2_000_000),
        name="ffn",
    )(dst, me, alphas, *cots, xs, att, ot, w_out, b_out, w_up, b_up, w_down, b_down)


def attn_bwd_body(dst, me, bias, mask, xs, gm, qh, kh, vh, qt, kt, doh, dott, lse, inner, w,
                  d0, d1, d2, d3, keep, send, grads, dx_rows, sem):
    def pair(hp, carry):
        dq2, dk2, dv2 = [], [], []
        for sub in range(2):
            h = hp * 2 + sub
            hr = pl.ds(pl.multiple_of(h * HD, HD), HD)
            dk = [None] * NQ
            dv = [None] * NQ
            dq = []
            for i in range(NQ):
                cols = pl.ds(i * QB, QB)
                q, do = qt[hr, cols], dott[hr, cols]
                q_rows, do_rows = qh[h, cols, :], doh[h, cols, :]
                ls, inn = lse[h, :, cols], inner[h, :, cols]
                acc = None
                for j in range(i + 1):
                    rows = pl.ds(j * QB, QB)
                    s = dot(kh[h, rows, :], q)
                    if j == i:
                        p = jnp.exp(s + mask[i] - ls)
                    else:
                        p = jnp.exp(s - (ls - bias[i * NQ + j]))
                    dp = dot(vh[h, rows, :], do)
                    ds = (p * (dp - inn)).astype(BF)
                    gv = dot(p.astype(BF), do_rows)
                    gk = dot(ds, q_rows)
                    gq = dot(kt[hr, rows], ds)
                    dv[j] = gv if dv[j] is None else dv[j] + gv
                    dk[j] = gk if dk[j] is None else dk[j] + gk
                    acc = gq if acc is None else acc + gq
                dq.append((acc * 0.125).T.astype(BF))
            dq2.append(jnp.concatenate(dq, axis=0))
            dk2.append(jnp.concatenate(dk, axis=0).astype(BF))
            dv2.append(jnp.concatenate(dv, axis=0).astype(BF))
        for n, two in enumerate((dq2, dk2, dv2)):
            lanes = pl.ds(pl.multiple_of(n * D + hp * 128, 128), 128)
            grads[:, lanes] = jnp.concatenate(two, axis=1)
        return carry

    lax.fori_loop(0, HEADS // 2, pair, 0)
    dx_rows[...] = (gm[...] + dot(grads[...], w[...], 1, 1)).astype(BF)
    copies = scatter_rows(dst, dx_rows, (d0, d1, d2, d3), sem)
    for n in range(3):
        g = dot(xs[...], grads[:, n * D:(n + 1) * D], 0, 0)
        for s in range(SLOTS):
            lb, a = s // 8, s % 8
            for part in range(2):
                r0 = a * 64 + part * 32
                put_slot(me, keep, send, part, s, n * 32, 32, g[r0:r0 + 32, lb * 128:(lb + 1) * 128].astype(BF))
    for c in copies:
        c.wait()


def attn_bwd(dst, me, bias, mask, xs, gm, qh, kh, vh, qt, kt, doh, dott, lse, inner, w):
    s = jax.ShapeDtypeStruct
    anyspec = pl.BlockSpec(memory_space=pl.ANY)
    smem = pl.BlockSpec(memory_space=pltpu.SMEM)
    vmem = pl.BlockSpec(memory_space=pltpu.VMEM)
    half = s((2, SLOTS // 2, R2, 128), BF)
    return pl.pallas_call(
        attn_bwd_body,
        out_shape=(s((256, D), BF),) * 4 + (half, half),
        in_specs=[smem] * 3 + [vmem] * 13,
        out_specs=(anyspec,) * 4 + (vmem,) * 2,
        scratch_shapes=[pltpu.VMEM((T, 3 * D), BF), pltpu.VMEM((T, D), BF), pltpu.SemaphoreType.DMA((NSUB,))],
        compiler_params=params(56),
        cost_estimate=pl.CostEstimate(flops=18_000_000_000, bytes_accessed=20_000_000, transcendentals=5_000_000),
        name="attn_bwd",
    )(dst, me, bias, mask, xs, gm, qh, kh, vh, qt, kt, doh, dott, lse, inner, w)


def pick_half(slot, own, other):
    return jnp.where(slot < SLOTS // 2, own[0, 0].astype(F32), other[0, 0].astype(F32))


def finish_dense_body(slots, own_a, other_a, own_b, other_b, up, down, out, small):
    s = pl.program_id(0)
    a = pick_half(slots[0, s], own_a, other_a)
    b = pick_half(slots[1, s], own_b, other_b)
    up[...] = a[:256]
    down[...] = b[:256]
    out[0:32] = a[256:288]
    out[32:64] = b[256:288]
    small[0, 0:8] = a[288:296]
    small[0, 8:16] = b[288:296]


def finish_qkv_body(slots, own_a, other_a, own_b, other_b, gq, gk, gv):
    s = pl.program_id(0)
    a = pick_half(slots[0, s], own_a, other_a)
    b = pick_half(slots[1, s], own_b, other_b)
    for n, g in enumerate((gq, gk, gv)):
        g[0:32] = a[n * 32:n * 32 + 32]
        g[32:64] = b[n * 32:n * 32 + 32]


def finish(body, slots, own, other, rows, out_shape, out_specs, name):
    def block(part):
        return pl.BlockSpec((1, 1, rows, 128), lambda s, slots: (part, slots[part, s] % (SLOTS // 2), 0, 0))

    return pl.pallas_call(
        body,
        grid_spec=pltpu.PrefetchScalarGridSpec(
            num_scalar_prefetch=1,
            grid=(SLOTS,),
            in_specs=[block(0), block(0), block(1), block(1)],
            out_specs=out_specs,
        ),
        out_shape=out_shape,
        compiler_params=params(16),
        name=name,
    )(slots, own, other, own, other)


def pairs(size, bit):
    return [(a, a ^ bit) for a in range(size)]


def add(a, b):
    return (a.astype(F32) + b.astype(F32)).astype(BF)


def sum_shards(n_dp, n_seq, keep, send):
    def dp(v, bit):
        return lax.ppermute(v, "dp", pairs(n_dp, bit))

    def seq(v, bit):
        return lax.ppermute(v, "seq", pairs(n_seq, bit))

    got = dp(send, 1)
    a, b = add(keep[0], got[0]), add(keep[1], got[1])
    ga, gb = dp(a[8:], 2), dp(b[8:], 4)
    a, b = add(a[:8], ga), add(b[:8], gb)
    ga, gb = dp(a[4:], 4), dp(b[4:], 2)
    ab = jnp.stack([add(a[:4], ga), add(b[:4], gb)])
    ab = ab.reshape((2, 2, 2) + ab.shape[2:])
    ab = add(ab[:, :, 0], seq(ab[:, :, 1], 1))
    ab = add(ab[:, 0], seq(ab[:, 1], 2))
    bit = 8
    while bit < n_dp:
        ab = add(ab, dp(ab, bit))
        bit *= 2
    ab = jnp.stack([ab, seq(ab, 2)], axis=1)
    ab = jnp.stack([ab, seq(ab, 1)], axis=2)
    ab = ab.reshape((2, 4) + ab.shape[3:])
    a, b = ab[0], ab[1]
    a, b = jnp.concatenate([a, dp(a, 4)]), jnp.concatenate([b, dp(b, 2)])
    ab = jnp.stack([jnp.concatenate([a, dp(a, 2)]), jnp.concatenate([b, dp(b, 4)])])
    return ab, dp(ab, 1)


def per_device(n_dp, n_seq, x_short, order_short, x_long, order_long, w_query, w_key, w_value, w_out, b_out, alphas,
               w_up, b_up, w_down, b_down, cot_short, cot_long):
    i = lax.axis_index("seq")
    d = lax.axis_index("dp")
    n_dev = n_dp * n_seq

    def exchange(parts):
        got = [lax.dynamic_index_in_dim(parts, i, 0, False)]
        for k in range(1, n_seq):
            mine = lax.dynamic_index_in_dim(parts, jnp.bitwise_xor(i, k), 0, False)
            got.append(lax.ppermute(mine, "seq", pairs(n_seq, k)))
        return got

    def rows_of(short, long):
        return jnp.concatenate([short.reshape(1, 256, D), long])

    def home(got, dtype):
        def chunk(j):
            k = jnp.bitwise_xor(i, j)
            v = jnp.where(k < 2, jnp.where(k == 0, got[0], got[1]), jnp.where(k == 2, got[2], got[3]))
            return v.astype(dtype)
        return chunk(0).reshape(2, 128, D), jnp.stack([chunk(j) for j in range(1, n_seq)])

    def give_back(mine):
        return [mine[0]] + [lax.ppermute(mine[k], "seq", pairs(n_seq, k)) for k in range(1, n_seq)]

    xs = exchange(rows_of(x_short, x_long))
    pos_short = jnp.concatenate([order_short, order_short + 512])
    pos = exchange(jnp.stack([pos_short, order_long, order_long, order_long]).reshape(4, 2, 128))
    cots = exchange(rows_of(cot_short, cot_long))

    is_short = i == 0
    sub = jnp.stack(pos).reshape(NSUB, SUB)
    low = jnp.min(sub, axis=1)
    dst = jnp.where(is_short, low // SUB, 2 * (low // 128) + jnp.arange(NSUB) % 2).astype(jnp.int32)
    place = dst[None, :] == jnp.arange(NSUB)[:, None]
    sorted_pos = jnp.sum(jnp.where(place[:, :, None], sub[None], 0), axis=1).reshape(NQ, QB)
    mask = jnp.where(sorted_pos[:, :, None] <= sorted_pos[:, None, :], 0.0, -1e30).astype(F32)
    group = jnp.arange(NQ) // 2
    bias = jnp.where(is_short & (group[:, None] != group[None, :]), -1e30, 0.0).astype(F32).reshape(-1)
    c, bx, by = d & 1, (d >> 1) & 1, (d >> 2) & 1
    me = jnp.stack([c * 16 + bx * 8 + by * 4 + i, c * 16 + by * 8 + bx * 4 + i, d * n_seq + i]).astype(jnp.int32)
    slots = jnp.bitwise_xor(me[:2, None], jnp.arange(SLOTS, dtype=jnp.int32)[None, :])

    w = jnp.concatenate([w_query, w_key, w_value], axis=1)
    rows, qh, kh, vh, qt, kt, vt, ot, att, lse = attn_fwd(dst, bias, xs, mask, w, w.T)
    o0, o1, o2, o3, gm, doh, dott, inner, keep, send = ffn(
        n_dev, dst, me, alphas, cots, rows, att, ot, w_out, b_out.reshape(1, D), w_up, b_up.reshape(1, FF),
        w_down, b_down.reshape(1, D))
    outs = give_back((o0, o1, o2, o3))
    d0, d1, d2, d3, keep2, send2 = attn_bwd(dst, me, bias, mask, rows, gm, qh, kh, vh, qt, kt, doh, dott, lse, inner, w)
    dxs = give_back((d0, d1, d2, d3))
    out_short, out_long = home(outs, BF)
    dx_short, dx_long = home(dxs, F32)
    own1, other1 = sum_shards(n_dp, n_seq, keep, send)
    own2, other2 = sum_shards(n_dp, n_seq, keep2, send2)

    s = jax.ShapeDtypeStruct
    wide = pl.BlockSpec((64, 128), lambda s, slots: (s % 8, s // 8))
    g_up, g_down, g_out, small = finish(
        finish_dense_body, slots, own1, other1, R1,
        (s((D, FF), F32), s((FF, D), F32), s((D, D), F32), s((SLOTS, 16, 128), F32)),
        (pl.BlockSpec((256, 128), lambda s, slots: (s % 2, s // 2)),
         pl.BlockSpec((256, 128), lambda s, slots: (s % 8, s // 8)),
         wide,
         pl.BlockSpec((1, 16, 128), lambda s, slots: (s, 0, 0))), "finish_dense")
    g_query, g_key, g_value = finish(
        finish_qkv_body, slots, own2, other2, R2, (s((D, D), F32),) * 3, (wide,) * 3, "finish_qkv")
    flat = small[:24, 0].reshape(-1)
    nr = (n_dev + 127) // 128
    g_alphas = jnp.sum(small[:6 * nr, 8].reshape(2, 3 * nr * 128), axis=1)
    return (out_short, out_long, dx_short, dx_long, g_query, g_key, g_value, g_out, flat[2560:3072], g_alphas,
            g_up, flat[:2048], g_down, flat[2048:2560])


def solution(mesh):
    split = P("dp", "seq", None)
    whole = P()
    return jax.shard_map(
        functools.partial(per_device, mesh.shape["dp"], mesh.shape["seq"]),
        mesh=mesh,
        in_specs=(split, P("seq"), split, P("seq")) + (whole,) * 10 + (split, split),
        out_specs=(split,) * 4 + (whole,) * 10,
        check_vma=False,
    )
```

```python
import functools
import jax
import jax.numpy as jnp
from jax import lax
from jax.sharding import PartitionSpec as P
from jax.experimental import pallas as pl
from jax.experimental.pallas import tpu as pltpu

BF = jnp.bfloat16
F32 = jnp.float32
HEADS = 8
HD = 64
D = 512
FF = 2048
T = 1024
SUB = 64
NSUB = T // SUB
QB = 256
NQ = T // QB


def dot(a, b, ca=1, cb=0):
    return lax.dot_general(a, b, (((ca,), (cb,)), ((), ())), preferred_element_type=F32)


def params(mb):
    return pltpu.CompilerParams(vmem_limit_bytes=mb * 1024 * 1024)


def one_head(pair, h):
    row = lax.broadcasted_iota(jnp.int32, pair.shape, 0)
    return jnp.where((row >= HD) == (h == 1), pair, jnp.zeros_like(pair))


def attn_fwd_body(me, c0, c1, c2, c3, w, wt, xs, q_out, k_out, v_out, qt, kt, ot, att, lse, mask, dst, bias,
                  vt):
    chunks = (c0, c1, c2, c3)
    is_short = me[4] == 0
    runs = jnp.concatenate([chunks[n][256:272, :128].astype(F32)[:4] for n in range(4)], axis=0)
    spot = runs[:, :SUB] * 32.0 + runs[:, SUB:2 * SUB]
    lowest = jnp.min(spot, axis=1, keepdims=True).astype(jnp.int32)
    odd = lax.broadcasted_iota(jnp.int32, (NSUB, 1), 0) & 1
    to = jnp.where(is_short, lowest >> 6, 2 * (lowest >> 7) + odd)
    for s in range(NSUB):
        dst[s] = jnp.max(to[s:s + 1, :])
    gather_rows(dst, chunks, xs)
    for a in range(NQ):
        for b in range(NQ):
            bias[a * NQ + b] = jnp.where(is_short, 0.0 if a // 2 == b // 2 else -1e30, 0.0)
    place = (lax.broadcasted_iota(jnp.int32, (NSUB, NSUB), 1) == to).astype(BF)
    by_run = 32.0 * dot(place, runs[:, :SUB].astype(BF), 0, 0) + dot(place, runs[:, SUB:2 * SUB].astype(BF), 0, 0)
    for a in range(NQ):
        row = jnp.concatenate([by_run[4 * a + b:4 * a + b + 1, :] for b in range(4)], axis=1)
        across = jnp.broadcast_to(row, (QB, QB))
        mask[a] = jnp.where(across.T <= across, 0.0, -1e30)
    for i in range(NQ):
        rows = pl.ds(i * QB, QB)
        x = xs[rows, :]
        qkv = dot(x, w[...]).astype(BF)
        qkvt = dot(wt[...], x, 1, 1).astype(BF)
        q_out[rows, :] = qkv[:, :D] * BF(0.125)
        k_out[rows, :] = qkv[:, D:2 * D]
        v_out[rows, :] = qkv[:, 2 * D:]
        qt[:, rows] = qkvt[:D] * BF(0.125)
        kt[:, rows] = qkvt[D:2 * D]
        vt[:, rows] = qkvt[2 * D:]

    def pair(hp, carry):
        wide = pl.ds(pl.multiple_of(hp * 2 * HD, 2 * HD), 2 * HD)
        for i in range(NQ):
            cols = pl.ds(i * QB, QB)
            both = qt[wide, cols]
            for h in range(2):
                hr = pl.ds(pl.multiple_of(hp * 2 * HD + h * HD, HD), HD)
                q = one_head(both, h)
                tiles, tops = [], []
                for j in range(i + 1):
                    s = dot(k_out[pl.ds(j * QB, QB), wide], q)
                    if j == i:
                        s = s + mask[i]
                        tops.append(jnp.max(s, axis=0, keepdims=True))
                    else:
                        tops.append(jnp.max(s, axis=0, keepdims=True) + bias[i * NQ + j])
                    tiles.append(s)
                m = functools.reduce(jnp.maximum, tops)
                total, o = None, None
                for j in range(i + 1):
                    mj = m if j == i else m - bias[i * NQ + j]
                    e = jnp.exp(tiles[j] - mj)
                    t = jnp.sum(e, axis=0, keepdims=True)
                    total = t if total is None else total + t
                    p = dot(vt[hr, pl.ds(j * QB, QB)], e.astype(BF))
                    o = p if o is None else o + p
                o = o * (1.0 / total)
                ot[hr, cols] = o
                lse[hp * 2 + h, :, cols] = m + jnp.log(total)
        return carry

    lax.fori_loop(0, HEADS // 2, pair, 0)
    for i in range(NQ):
        rows = pl.ds(i * QB, QB)
        att[rows, :] = ot[:, rows].astype(BF).T


def attn_fwd(me, chunks, w, wt):
    s = jax.ShapeDtypeStruct
    rows, cols = s((T, D), BF), s((D, T), BF)
    smem = pl.BlockSpec(memory_space=pltpu.SMEM)
    vmem = pl.BlockSpec(memory_space=pltpu.VMEM)
    return pl.pallas_call(
        attn_fwd_body,
        out_shape=(rows, rows, rows, rows, cols, cols, s((D, T), F32), rows, s((HEADS, 1, T), F32),
                   s((NQ, QB, QB), F32), s((NSUB,), jnp.int32), s((NQ * NQ,), F32)),
        in_specs=[smem] + [vmem] * 6,
        out_specs=(vmem,) * 10 + (smem,) * 2,
        scratch_shapes=[pltpu.VMEM((D, T), BF)],
        compiler_params=params(24),
        cost_estimate=pl.CostEstimate(flops=1500000000, bytes_accessed=2000000, transcendentals=0),
        name="attn_fwd",
    )(me, *chunks, w, wt)


FB = 512
NF = FF // FB
SLOTS = 32
HALF = SLOTS // 2
TOKEN = jax.ShapeDtypeStruct((8, 128), F32)
R1 = 592
R2 = 192


def scatter_rows(dst, rows_ref, put):
    for s in range(NSUB):
        at = pl.ds(pl.multiple_of(dst[s] * SUB, SUB), SUB)
        put(s // 4, (s % 4) * SUB, rows_ref[at, :])


def gather_rows(dst, ins, rows_ref):
    for s in range(NSUB):
        to = pl.ds(pl.multiple_of(dst[s] * SUB, SUB), SUB)
        rows_ref[to, :] = ins[s // 4][(s % 4) * SUB:(s % 4 + 1) * SUB, :]


def put_slot(me, keep, send, s, row, rows, val):
    at = pl.ds(row, rows)

    @pl.when(s // HALF == me[0])
    def _():
        keep[jnp.bitwise_xor(s % HALF, me[1]), at, :] = val

    @pl.when(s // HALF != me[0])
    def _():
        send[jnp.bitwise_xor(s % HALF, me[2]), at, :] = val


def top_rows(first, second):
    rows = lax.broadcasted_iota(jnp.int32, (16, 128), 0)
    first, second = jnp.broadcast_to(first, (16, 128)), jnp.broadcast_to(second, (16, 128))
    return jnp.where(rows == 0, first, jnp.where(rows == 1, second, 0.0)).astype(BF)


def ffn_body(n_dev, dst, me, alphas, c0, c1, c2, c3, xs, att, ot, w_out, b_out, w_up, b_up, w_down, b_down,
             o0, o1, o2, o3, gm, do_out, dott, inner, keep, send,
             cot, branch, middle, low, low_t, gfeed, gfeed_t, feed, bias_up):
    f = pl.program_id(0)
    a0, a1 = alphas[0], alphas[1]

    @pl.when(f == 0)
    def _():
        gather_rows(dst, (c0, c1, c2, c3), cot)
        br = dot(att[...], w_out[...]) + b_out[...]
        branch[...] = br
        mid = xs[...].astype(F32) + a0 * br
        middle[...] = mid
        low[...] = mid.astype(BF)
        low_t[...] = low[...].T
        g = cot[...].astype(F32)
        gfeed[...] = (a1 * g).astype(BF)
        gfeed_t[...] = gfeed[...].T
        gm[...] = g
        feed[...] = jnp.broadcast_to(b_down[...], feed.shape)

    hidden = dot(low[...], w_up[...]) + b_up[...]
    c = 0.7978845608028654
    h2 = hidden * hidden
    th = jnp.tanh(hidden * (c + (c * 0.044715) * h2))
    half = 0.5 + 0.5 * th
    active = (hidden * half).astype(BF)
    slope = half + (0.5 * hidden) * (1.0 - th * th) * (c + (3 * c * 0.044715) * h2)
    feed[...] += dot(active, w_down[...])
    grad_h = (dot(gfeed[...], w_down[...], 1, 1) * slope).astype(BF)
    bu = jnp.sum(grad_h.astype(F32), axis=0, keepdims=True)
    gd = dot(gfeed_t[...], active).astype(BF).T
    gu = dot(low_t[...], grad_h)
    gm[...] += dot(grad_h, w_up[...], 1, 1)
    for b in range(FB // 128):
        for a in range(2):
            put_slot(me, keep, send, (FB // 64) * f + 2 * b + a, 0, 256,
                     gu[a * 256:(a + 1) * 256, b * 128:(b + 1) * 128].astype(BF))
        bias_up[(FB // 128) * f + b] = bu[:, b * 128:(b + 1) * 128]
    for lb in range(4):
        for a in range(FB // 256):
            put_slot(me, keep, send, lb * 8 + (FB // 256) * f + a, 256, 256,
                     gd[a * 256:(a + 1) * 256, lb * 128:(lb + 1) * 128])

    @pl.when(f == NF - 1)
    def _():
        low[...] = (middle[...] + a1 * feed[...]).astype(BF)
        def put(k, row, val):
            (o0, o1, o2, o3)[k][row:row + SUB, :] = val

        scatter_rows(dst, low, put)
        g = cot[...].astype(F32)
        s1 = jnp.sum(feed[...] * g)
        s0 = jnp.sum(branch[...] * gm[...])
        bd = jnp.sum(gfeed[...].astype(F32), axis=0, keepdims=True)
        gb = (a0 * gm[...]).astype(BF)
        bo = jnp.sum(gb.astype(F32), axis=0, keepdims=True)
        go = dot(att[...], gb, 0, 0)
        do_out[...] = dot(gb, w_out[...], 1, 1).astype(BF)
        dt = dot(w_out[...], gb, 1, 1).astype(BF)
        dott[...] = dt
        for h in range(HEADS):
            hs = slice(h * HD, (h + 1) * HD)
            inner[h] = jnp.sum(ot[hs, :] * dt[hs, :].astype(F32), axis=0, keepdims=True)
        nr = (n_dev + 127) // 128
        row = lax.broadcasted_iota(jnp.int32, (SLOTS, 128), 0)
        lane = lax.broadcasted_iota(jnp.int32, (SLOTS, 128), 1)
        mine_row, mine_lane = me[3] // 128, me[3] % 128
        small = jnp.zeros((SLOTS, 128), F32)
        for k, total in enumerate((s0, s1)):
            rest = jnp.full((SLOTS, 128), total, F32)
            for t in range(3):
                piece = rest.astype(BF).astype(F32)
                rest = rest - piece
                here = (row == (3 * k + t) * nr + mine_row) & (lane == mine_lane)
                small = jnp.where(here, piece, small)
        zero = jnp.zeros((1, 128), F32)
        for s in range(SLOTS):
            lb, a = s // 8, s % 8
            put_slot(me, keep, send, s, 512, 64, go[a * 64:a * 64 + 64, lb * 128:(lb + 1) * 128].astype(BF))
            if s < 16:
                first = bias_up[s]
            elif s < 24:
                first = (bd if s < 20 else bo)[:, (s % 4) * 128:(s % 4 + 1) * 128]
            else:
                first = zero
            put_slot(me, keep, send, s, 576, 16, top_rows(first, small[s:s + 1]))


def ffn(n_dev, dst, me, alphas, cots, xs, att, ot, w_out, b_out, w_up, b_up, w_down, b_down):
    s = jax.ShapeDtypeStruct
    anyspec = pl.BlockSpec(memory_space=pl.ANY)
    smem = pl.BlockSpec(memory_space=pltpu.SMEM)
    vmem = pl.BlockSpec(memory_space=pltpu.VMEM)
    v = pltpu.VMEM
    half = s((HALF, R1, 128), BF)
    return pl.pallas_call(
        functools.partial(ffn_body, n_dev),
        grid=(NF,),
        out_shape=(s((256, D), BF),) * 4 + (s((T, D), F32), s((T, D), BF), s((D, T), BF),
                                            s((HEADS, 1, T), F32), half, half),
        in_specs=[smem, smem, smem] + [vmem] * 9 + [
            pl.BlockSpec((D, FB), lambda f: (0, f)),
            pl.BlockSpec((1, FB), lambda f: (0, f)),
            pl.BlockSpec((FB, D), lambda f: (f, 0)),
            vmem,
        ],
        out_specs=(vmem,) * 10,
        scratch_shapes=[v((T, D), BF), v((T, D), F32), v((T, D), F32), v((T, D), BF), v((D, T), BF), v((T, D), BF),
                        v((D, T), BF), v((T, D), F32), v((16, 1, 128), F32)],
        compiler_params=params(40),
        cost_estimate=pl.CostEstimate(flops=1875000000, bytes_accessed=2500000, transcendentals=0),
        name="ffn",
    )(dst, me, alphas, *cots, xs, att, ot, w_out, b_out, w_up, b_up, w_down, b_down)


def attn_bwd_body(bias, mask, q_in, k_in, v_in, qt, kt, do_in, dott, lse, inner, after, dqo, dko, dvo, token):
    token[...] = jnp.zeros_like(token)
    dq2, dk2, dv2 = [], [], []
    for h in range(2):
        hr = pl.ds(h * HD, HD)
        dk = [None] * NQ
        dv = [None] * NQ
        dq = []
        for i in range(NQ):
            cols = pl.ds(i * QB, QB)
            q, do = one_head(qt[:, cols], h), one_head(dott[:, cols], h)
            q_rows, do_rows = q_in[cols, :], do_in[cols, :]
            ls, inn = lse[h, :, cols], inner[h, :, cols]
            acc = None
            for j in range(i + 1):
                rows = pl.ds(j * QB, QB)
                s = dot(k_in[rows, :], q)
                if j == i:
                    p = jnp.exp(s + mask[i] - ls)
                else:
                    p = jnp.exp(s - (ls - bias[i * NQ + j]))
                dp = dot(v_in[rows, :], do)
                ds = (p * (dp - inn)).astype(BF)
                gv = dot(p.astype(BF), do_rows)
                gk = dot(ds, q_rows)
                gq = dot(kt[hr, rows], ds)
                dv[j] = gv if dv[j] is None else dv[j] + gv
                dk[j] = gk if dk[j] is None else dk[j] + gk
                acc = gq if acc is None else acc + gq
            dq.append(acc * 0.125)
        dq2.append(dq)
        dk2.append(dk)
        dv2.append(dv)
    right = lax.broadcasted_iota(jnp.int32, (QB, 2 * HD), 1) >= HD
    for i in range(NQ):
        rows = pl.ds(i * QB, QB)
        dqo[rows, :] = jnp.concatenate([dq2[0][i], dq2[1][i]], axis=0).astype(BF).T
        dko[rows, :] = jnp.where(right, dk2[1][i], dk2[0][i]).astype(BF)
        dvo[rows, :] = jnp.where(right, dv2[1][i], dv2[0][i]).astype(BF)


def attn_bwd(hp, bias, mask, q, k, v, qt, kt, do, dott, lse, inner, after):
    s = jax.ShapeDtypeStruct
    smem = pl.BlockSpec(memory_space=pltpu.SMEM)
    vmem = pl.BlockSpec(memory_space=pltpu.VMEM)
    tall = pl.BlockSpec((T, 2 * HD), lambda g: (0, hp))
    wide = pl.BlockSpec((2 * HD, T), lambda g: (hp, 0))
    line = pl.BlockSpec((2, 1, T), lambda g: (hp, 0, 0))
    return pl.pallas_call(
        attn_bwd_body,
        grid=(1,),
        out_shape=(s((T, 2 * HD), BF),) * 3 + (TOKEN,),
        in_specs=[smem, vmem, tall, tall, tall, wide, wide, tall, wide, line, line, pl.BlockSpec(memory_space=pl.ANY)],
        out_specs=(vmem,) * 4,
        compiler_params=params(20),
        cost_estimate=pl.CostEstimate(flops=625000000, bytes_accessed=625000, transcendentals=0),
        name="attn_bwd%d" % hp,
    )(bias, mask, q, k, v, qt, kt, do, dott, lse, inner, after)


def attn_dense_body(dst, me, xs, gm, w, *refs):
    parts, (d_out, keep, send, token, dx_rows) = refs[:12], refs[-5:]
    token[...] = jnp.zeros_like(token)
    grads = [jnp.concatenate([parts[3 * hp + n][...] for hp in range(4)], axis=1) for n in range(3)]
    dx = gm[...]
    for n in range(3):
        dx = dx + dot(grads[n], w[:, n * D:(n + 1) * D], 1, 1)
    dx_rows[...] = dx.astype(BF)

    def put(k, row, val):
        d_out[jnp.bitwise_xor(me[4], k), row:row + SUB, :] = val

    scatter_rows(dst, dx_rows, put)
    for n in range(3):
        g = dot(xs[...], grads[n], 0, 0)
        for s in range(SLOTS):
            lb, a = s // 8, s % 8
            put_slot(me, keep, send, s, n * 64, 64, g[a * 64:a * 64 + 64, lb * 128:(lb + 1) * 128].astype(BF))


def attn_dense(dst, me, xs, gm, w, grads, after=()):
    s = jax.ShapeDtypeStruct
    anyspec = pl.BlockSpec(memory_space=pl.ANY)
    smem = pl.BlockSpec(memory_space=pltpu.SMEM)
    vmem = pl.BlockSpec(memory_space=pltpu.VMEM)
    half = s((HALF, R2, 128), BF)
    return pl.pallas_call(
        attn_dense_body,
        out_shape=(s((4, 256, D), BF), half, half, TOKEN),
        in_specs=[smem] * 2 + [vmem] * 15 + [anyspec] * len(after),
        out_specs=(vmem,) * 4,
        scratch_shapes=[pltpu.VMEM((T, D), BF)],
        compiler_params=params(32),
        cost_estimate=pl.CostEstimate(flops=400000000, bytes_accessed=1125000, transcendentals=0),
        name="attn_dense",
    )(dst, me, xs, gm, w, *grads, *after)


PIECES = ((2, 256, 0), (8, 256, 256), (8, 64, 512), (8, 64, R1), (8, 64, R1 + 64), (8, 64, R1 + 128))
SMALL = 576


def finish_body(part, me, own, other, *refs):
    n = len(PIECES)
    stages, small_stage, sem = refs[-n - 2:-2], refs[-2], refs[-1]
    outs, token = refs[-2 * n - 4:-n - 3], refs[-n - 3]
    token[...] = jnp.zeros_like(token)

    def each(slot, depth):
        copies = []
        for which, src in enumerate((own, other)):
            core = me[0] if which == 0 else 1 - me[0]
            s = core * HALF + jnp.bitwise_xor(slot + 8 * part, me[1 + which])
            for k, (tall, rows, row) in enumerate(PIECES):
                stages[k][depth, which] = src[slot, row:row + rows, :].astype(F32)
                to = outs[k].at[pl.ds(pl.multiple_of((s % tall) * rows, rows), rows),
                                pl.ds(pl.multiple_of((s // tall) * 128, 128), 128)]
                copies.append(pltpu.make_async_copy(stages[k].at[depth, which], to, sem.at[depth, which, k]))
            small_stage[depth, which] = src[slot, SMALL:SMALL + 16, :].astype(F32)[:8]
            to = outs[n].at[pl.ds(pl.multiple_of(s * 8, 8), 8)]
            copies.append(pltpu.make_async_copy(small_stage.at[depth, which], to, sem.at[depth, which, n]))
        return copies

    pending = [None] * 4
    for slot in range(8):
        depth = slot % 4
        if pending[depth] is not None:
            for c in pending[depth]:
                c.wait()
        pending[depth] = each(slot, depth)
        for c in pending[depth]:
            c.start()
    for group in pending:
        for c in group:
            c.wait()


def finish(part, me, got, before, after):
    anyspec = pl.BlockSpec(memory_space=pl.ANY)
    vmem = pl.BlockSpec(memory_space=pltpu.VMEM)
    s = jax.ShapeDtypeStruct
    n = len(PIECES)
    square = s((D, D), F32)
    *out, token = pl.pallas_call(
        functools.partial(finish_body, part),
        out_shape=(s((D, FF), F32), s((FF, D), F32), square, square, square, square, s((SLOTS * 8, 128), F32), TOKEN),
        in_specs=[pl.BlockSpec(memory_space=pltpu.SMEM)] + [vmem] * 2 + [anyspec] * (len(before) + len(after)),
        out_specs=(anyspec,) * (n + 1) + (vmem,),
        scratch_shapes=[pltpu.VMEM((4, 2, rows, 128), F32) for _, rows, _ in PIECES]
        + [pltpu.VMEM((4, 2, 8, 128), F32), pltpu.SemaphoreType.DMA((4, 2, n + 1))],
        input_output_aliases={3 + k: k for k in range(len(before))},
        compiler_params=params(20),
        cost_estimate=pl.CostEstimate(flops=1_000_000, bytes_accessed=10_000_000, transcendentals=0),
        name="finish%d" % part,
    )(me, *got, *before, *after)
    return tuple(out), token


def pairs(size, bit):
    return [(a, a ^ bit) for a in range(size)]


def add(a, b):
    return (a.astype(F32) + b.astype(F32)).astype(BF)


def halve_body(keep_lo, keep_hi, got_lo, got_hi, *refs):
    lo, hi, token = refs[-3:]
    lo[...] = add(keep_lo[...], got_lo[...])
    hi[...] = add(keep_hi[...], got_hi[...])
    token[...] = jnp.zeros_like(token)


def halve(keep, got, after=()):
    m, rows = keep.shape[0] // 2, keep.shape[1]
    steps = max(1, m // 2)
    lo = pl.BlockSpec((m // steps, rows, 128), lambda g: (g, 0, 0))
    hi = pl.BlockSpec((m // steps, rows, 128), lambda g: (g + steps, 0, 0))
    half = jax.ShapeDtypeStruct((m, rows, 128), BF)
    return pl.pallas_call(
        halve_body,
        grid=(steps,),
        out_shape=(half, half, TOKEN),
        in_specs=[lo, hi, lo, hi] + [pl.BlockSpec(memory_space=pl.ANY)] * len(after),
        out_specs=(lo, lo, pl.BlockSpec(memory_space=pltpu.VMEM)),
        compiler_params=params(12),
        cost_estimate=pl.CostEstimate(flops=m * rows * 32, bytes_accessed=m * rows * 200, transcendentals=0),
        name="halve%d_%d" % (m, rows),
    )(keep, keep, got, got, *after)


def plus_body(a, b, *refs):
    out, token = refs[-2:]
    out[...] = add(a[...], b[...])
    token[...] = jnp.zeros_like(token)


def plus(a, b, after=(), twist=0):
    rows = a.shape[1]
    one = pl.BlockSpec((1, rows, 128), lambda g: (g, 0, 0))
    other = pl.BlockSpec((1, rows, 128), lambda g: (jnp.bitwise_xor(g, twist), 0, 0))
    return pl.pallas_call(
        plus_body,
        grid=(a.shape[0],),
        out_shape=(jax.ShapeDtypeStruct(a.shape, BF), TOKEN),
        in_specs=[one, other] + [pl.BlockSpec(memory_space=pl.ANY)] * len(after),
        out_specs=(one, pl.BlockSpec(memory_space=pltpu.VMEM)),
        compiler_params=params(8),
        cost_estimate=pl.CostEstimate(flops=a.shape[0] * rows * 32, bytes_accessed=a.shape[0] * rows * 100, transcendentals=0),
        name="plus%d_%d" % (a.shape[0], rows),
    )(a, b, *after)


def join_body(n, *refs):
    out, token = refs[-2:]
    row = 0
    for a, b in zip(refs[0:2 * n:2], refs[1:2 * n:2]):
        m, rows = a.shape[:2]
        out[:m, row:row + rows] = a[...]
        out[m:, row:row + rows] = b[...]
        row += rows
    token[...] = jnp.zeros_like(token)


def join(parts, after=()):
    m, rows = parts[0].shape[0], sum(p.shape[1] for p in parts[::2])
    vmem = pl.BlockSpec(memory_space=pltpu.VMEM)
    return pl.pallas_call(
        functools.partial(join_body, len(parts) // 2),
        out_shape=(jax.ShapeDtypeStruct((2 * m, rows, 128), BF), TOKEN),
        in_specs=[vmem] * len(parts) + [pl.BlockSpec(memory_space=pl.ANY)] * len(after),
        out_specs=(vmem, vmem),
        compiler_params=params(12),
        cost_estimate=pl.CostEstimate(flops=1000, bytes_accessed=m * rows * 100, transcendentals=0),
        name="join%d_%d" % (m, rows),
    )(*parts, *after)


def pos_rows(v):
    left = lax.broadcasted_iota(jnp.int32, (1, 128), 1) < SUB
    out = []
    for r in range(v.shape[0]):
        high, rest = v[r:r + 1] >> 5, v[r:r + 1] & 31
        out.append(jnp.where(left, high, pltpu.roll(rest, SUB, 1)))
        out.append(jnp.where(left, pltpu.roll(high, SUB, 1), rest))
    return jnp.concatenate(out, axis=0)


def pick_body(with_pos, me, short, long, *refs):
    outs, sem = refs[-5:-1], refs[-1]
    waits = []
    for k in range(4):
        j = jnp.bitwise_xor(me[4], k)
        to = outs[k].at[pl.ds(0, 256)]

        @pl.when(j == 0)
        def _():
            pltpu.make_async_copy(short, to, sem.at[k]).start()

        @pl.when(j > 0)
        def _():
            pltpu.make_async_copy(long.at[jnp.maximum(j - 1, 0)], to, sem.at[k]).start()

        waits.append(pltpu.make_async_copy(short, to, sem.at[k]))
    if with_pos:
        of_short = pos_rows(jnp.concatenate([refs[0][...], refs[0][...] + 512], axis=0))
        of_long = pos_rows(refs[1][...])
        for k in range(4):
            tile = jnp.where(jnp.bitwise_xor(me[4], k) == 0, of_short, of_long).astype(F32)
            tile = jnp.concatenate([tile, jnp.zeros((12, 128), F32)], axis=0).astype(BF)
            outs[k][256:272, :] = jnp.concatenate([tile, jnp.zeros((16, D - 128), BF)], axis=1)
    for c in waits:
        c.wait()


def pick(me, short, long, pos=(), after=()):
    anyspec = pl.BlockSpec(memory_space=pl.ANY)
    vmem = pl.BlockSpec(memory_space=pltpu.VMEM)
    out = jax.ShapeDtypeStruct((272 if pos else 256, D), BF)
    return pl.pallas_call(
        functools.partial(pick_body, bool(pos)),
        out_shape=(out,) * 4,
        in_specs=[pl.BlockSpec(memory_space=pltpu.SMEM)] + [anyspec] * 2 + [vmem] * len(pos) + [anyspec] * len(after),
        out_specs=(vmem,) * 4,
        scratch_shapes=[pltpu.SemaphoreType.DMA((4,))],
        compiler_params=params(56 if pos else 8),
        cost_estimate=pl.CostEstimate(flops=1000, bytes_accessed=500_000, transcendentals=0),
        name="pick%d" % len(pos),
    )(me, short.reshape(256, D), long, *pos, *after)


class Sums:
    def __init__(self, n_dp, n_seq):
        self.n_dp, self.n_seq = n_dp, n_seq
        self.core = pairs(n_dp, 1)
        self.first = [(a, a ^ (4 if a & 1 else 2)) for a in range(n_dp)]
        self.second = [(a, a ^ (2 if a & 1 else 4)) for a in range(n_dp)]

    def dp(self, v, perm):
        return lax.ppermute(v, "dp", perm)

    def seq(self, v, bit):
        return lax.ppermute(v, "seq", pairs(self.n_seq, bit))

    def rest(self, v):
        bit = 8
        while bit < self.n_dp:
            v = add(v, self.dp(v, pairs(self.n_dp, bit)))
            bit *= 2
        return v


def tie(a, b):
    return lax.optimization_barrier((a, b))


def per_device(n_dp, n_seq, x_short, order_short, x_long, order_long, w_query, w_key, w_value, w_out, b_out, alphas,
               w_up, b_up, w_down, b_down, cot_short, cot_long):
    i = lax.axis_index("seq")
    d = lax.axis_index("dp")
    n_dev = n_dp * n_seq

    def give_back(mine):
        return [mine[0]] + [lax.ppermute(mine[k], "seq", pairs(n_seq, k)) for k in range(1, n_seq)]

    def home(got):
        def chunk(j):
            k = jnp.bitwise_xor(i, j)
            v = jnp.where(k < 2, jnp.where(k == 0, got[0], got[1]), jnp.where(k == 2, got[2], got[3]))
            return v
        return chunk(0).reshape(2, 128, D), jnp.stack([chunk(j) for j in range(1, n_seq)])

    def give_back(mine):
        return [mine[0]] + [lax.ppermute(mine[k], "seq", pairs(n_seq, k)) for k in range(1, n_seq)]

    c, bx, by = d & 1, (d >> 1) & 1, (d >> 2) & 1
    z = (i & 1) * 2 + (i >> 1)
    x_first, y_first = bx * 8 + by * 4 + z, by * 8 + bx * 4 + z
    at = jnp.arange(8)
    me = jnp.where(at == 0, c, jnp.where(at == 1, jnp.where(c == 0, x_first, y_first), jnp.where(
        at == 2, jnp.where(c == 0, y_first, x_first), jnp.where(at == 3, d * n_seq + i, i)))).astype(jnp.int32)
    xs = give_back(pick(me, x_short, x_long, (order_short.reshape(1, 128), order_long.reshape(2, 128))))
    cots = give_back(pick(me, cot_short, cot_long, (), (xs[2],)))

    w = jnp.concatenate([w_query, w_key, w_value], axis=1)
    rows, q, k, v_rows, qt, kt, ot, att, lse, mask, dst, bias = attn_fwd(me, xs, w, w.T)
    o0, o1, o2, o3, gm, do, dott, inner, keep, send = ffn(
        n_dev, dst, me, alphas, cots, rows, att, ot, w_out, b_out.reshape(1, D), w_up, b_up.reshape(1, FF),
        w_down, b_down.reshape(1, D))
    net = Sums(n_dp, n_seq)

    def bwd(hp, after):
        *g, token = attn_bwd(hp, bias, mask, q, k, v_rows, qt, kt, do, dott, lse, inner, after)
        return g, token

    got = net.dp(send, net.core)
    outs = give_back((o0, o1, o2, o3))
    g0, token = bwd(0, lse)
    lo, hi, token = halve(keep, got, (token,))
    got = net.dp(hi, net.first)
    g1, token = bwd(1, token)
    g2, token = bwd(2, token)
    g3, token = bwd(3, token)
    lo, hi, token = halve(lo, got, (token,))
    got = net.dp(hi, net.second)
    d_rows, keep2, send2, token = attn_dense(
        dst, me, rows, gm, w, g0 + g1 + g2 + g3, (token,) + tuple(outs[1:]))
    out_short, out_long = home(outs)
    lo, hi, token = halve(lo, got, (token, out_short, out_long))
    got = net.seq(hi, 1)
    got2 = net.dp(send2, net.core)
    lo2, hi2, token = halve(keep2, got2, (token,))
    got2 = net.dp(hi2, net.first)
    lo, hi, token = halve(lo, got, (token,))
    got = net.seq(hi, 2)
    lo2, hi2, token = halve(lo2, got2, (token,))
    got2 = net.dp(hi2, net.second)
    v, token = plus(lo, got, (token,))
    v = net.rest(v)
    got = net.seq(v, 2)
    v, token = join((v, got), (token,))
    got = net.seq(v, 1)
    u, token = plus(lo2, got2, (token,))
    v, token = join((v, got), (token,))
    got = net.dp(v, net.second)
    (u, d_rows), _ = tie((u, d_rows), token)
    got2 = net.seq(u, 1)
    dxs = lax.all_to_all(d_rows, "seq", 0, 0)
    u, token = plus(u, got2, (token,), 2)
    got2 = net.seq(u, 2)
    u, token = plus(u, got2, (token,), 1)
    u = net.rest(u)
    got2 = net.dp(u, net.second)
    v, token = join((v, got, u, got2), (token,))
    far = net.dp(v, net.first)
    near = net.dp(v, net.core)
    dx_short, dx_long = dxs[0].reshape(2, 128, D).astype(F32), dxs[1:].astype(F32)
    first, token = finish(0, me, (v, near), (), (token, dx_short, dx_long))
    far, _ = tie(far, token)
    (g_up, g_down, g_out, g_query, g_key, g_value, small), _ = finish(
        1, me, (far, net.dp(far, net.core)), first, (token,))
    small = small.reshape(SLOTS, 8, 128)
    flat = small[:24, 0].reshape(-1)
    nr = (n_dev + 127) // 128
    g_alphas = jnp.sum(small[:6 * nr, 1].reshape(2, 3 * nr * 128), axis=1)
    return (out_short, out_long, dx_short, dx_long, g_query, g_key, g_value, g_out, flat[2560:3072], g_alphas,
            g_up, flat[:2048], g_down, flat[2048:2560])


def solution(mesh):
    split = P("dp", "seq", None)
    whole = P()
    return jax.shard_map(
        functools.partial(per_device, mesh.shape["dp"], mesh.shape["seq"]),
        mesh=mesh,
        in_specs=(split, P("seq"), split, P("seq")) + (whole,) * 10 + (split, split),
        out_specs=(split,) * 4 + (whole,) * 10,
        check_vma=False,
    )
```

```python
import functools
import jax
import jax.numpy as jnp
from jax import lax
from jax.sharding import PartitionSpec as P
from jax.experimental import pallas as pl
from jax.experimental.pallas import tpu as pltpu

BF = jnp.bfloat16
F32 = jnp.float32
HEADS = 8
HD = 64
D = 512
FF = 2048
T = 1024
SUB = 64
NSUB = T // SUB
QB = 256
NQ = T // QB


def dot(a, b, ca=1, cb=0):
    return lax.dot_general(a, b, (((ca,), (cb,)), ((), ())), preferred_element_type=F32)


def params(mb):
    return pltpu.CompilerParams(vmem_limit_bytes=mb * 1024 * 1024)


def one_head(pair, h):
    row = lax.broadcasted_iota(jnp.int32, pair.shape, 0)
    return jnp.where((row >= HD) == (h == 1), pair, jnp.zeros_like(pair))


def attn_fwd_body(me, c0, c1, c2, c3, w, wt, xs, q_out, k_out, v_out, qt, kt, ot, att, lse, mask, dst, bias,
                  vt):
    chunks = (c0, c1, c2, c3)
    is_short = me[4] == 0
    runs = jnp.concatenate([chunks[n][256:272, :128].astype(F32)[:4] for n in range(4)], axis=0)
    spot = runs[:, :SUB] * 32.0 + runs[:, SUB:2 * SUB]
    lowest = jnp.min(spot, axis=1, keepdims=True).astype(jnp.int32)
    odd = lax.broadcasted_iota(jnp.int32, (NSUB, 1), 0) & 1
    to = jnp.where(is_short, lowest >> 6, 2 * (lowest >> 7) + odd)
    for s in range(NSUB):
        dst[s] = jnp.max(to[s:s + 1, :])
    gather_rows(dst, chunks, xs)
    for a in range(NQ):
        for b in range(NQ):
            bias[a * NQ + b] = jnp.where(is_short, 0.0 if a // 2 == b // 2 else -1e30, 0.0)
    place = (lax.broadcasted_iota(jnp.int32, (NSUB, NSUB), 1) == to).astype(BF)
    by_run = 32.0 * dot(place, runs[:, :SUB].astype(BF), 0, 0) + dot(place, runs[:, SUB:2 * SUB].astype(BF), 0, 0)
    for a in range(NQ):
        row = jnp.concatenate([by_run[4 * a + b:4 * a + b + 1, :] for b in range(4)], axis=1)
        across = jnp.broadcast_to(row, (QB, QB))
        mask[a] = jnp.where(across.T <= across, 0.0, -1e30)
    for i in range(NQ):
        rows = pl.ds(i * QB, QB)
        x = xs[rows, :]
        qkv = dot(x, w[...]).astype(BF)
        qkvt = dot(wt[...], x, 1, 1).astype(BF)
        q_out[rows, :] = qkv[:, :D] * BF(0.125)
        k_out[rows, :] = qkv[:, D:2 * D]
        v_out[rows, :] = qkv[:, 2 * D:]
        qt[:, rows] = qkvt[:D] * BF(0.125)
        kt[:, rows] = qkvt[D:2 * D]
        vt[:, rows] = qkvt[2 * D:]

    def pair(hp, carry):
        wide = pl.ds(pl.multiple_of(hp * 2 * HD, 2 * HD), 2 * HD)
        for i in range(NQ):
            cols = pl.ds(i * QB, QB)
            both = qt[wide, cols]
            for h in range(2):
                hr = pl.ds(pl.multiple_of(hp * 2 * HD + h * HD, HD), HD)
                q = one_head(both, h)
                tiles, tops = [], []
                for j in range(i + 1):
                    s = dot(k_out[pl.ds(j * QB, QB), wide], q)
                    if j == i:
                        s = s + mask[i]
                        tops.append(jnp.max(s, axis=0, keepdims=True))
                    else:
                        tops.append(jnp.max(s, axis=0, keepdims=True) + bias[i * NQ + j])
                    tiles.append(s)
                m = functools.reduce(jnp.maximum, tops)
                total, o = None, None
                for j in range(i + 1):
                    mj = m if j == i else m - bias[i * NQ + j]
                    e = jnp.exp(tiles[j] - mj)
                    t = jnp.sum(e, axis=0, keepdims=True)
                    total = t if total is None else total + t
                    p = dot(vt[hr, pl.ds(j * QB, QB)], e.astype(BF))
                    o = p if o is None else o + p
                o = o * (1.0 / total)
                ot[hr, cols] = o
                lse[hp * 2 + h, :, cols] = m + jnp.log(total)
        return carry

    lax.fori_loop(0, HEADS // 2, pair, 0)
    for i in range(NQ):
        rows = pl.ds(i * QB, QB)
        att[rows, :] = ot[:, rows].astype(BF).T


def attn_fwd(me, chunks, w, wt):
    s = jax.ShapeDtypeStruct
    rows, cols = s((T, D), BF), s((D, T), BF)
    smem = pl.BlockSpec(memory_space=pltpu.SMEM)
    vmem = pl.BlockSpec(memory_space=pltpu.VMEM)
    return pl.pallas_call(
        attn_fwd_body,
        out_shape=(rows, rows, rows, rows, cols, cols, s((D, T), F32), rows, s((HEADS, 1, T), F32),
                   s((NQ, QB, QB), F32), s((NSUB,), jnp.int32), s((NQ * NQ,), F32)),
        in_specs=[smem] + [vmem] * 6,
        out_specs=(vmem,) * 10 + (smem,) * 2,
        scratch_shapes=[pltpu.VMEM((D, T), BF)],
        compiler_params=params(24),
        cost_estimate=pl.CostEstimate(flops=1500000000, bytes_accessed=2000000, transcendentals=0),
        name="attn_fwd",
    )(me, *chunks, w, wt)


FB = 512
NF = FF // FB
SLOTS = 32
HALF = SLOTS // 2
TOKEN = jax.ShapeDtypeStruct((8, 128), F32)
R1 = 592
R2 = 192


def scatter_rows(dst, rows_ref, put):
    for s in range(NSUB):
        at = pl.ds(pl.multiple_of(dst[s] * SUB, SUB), SUB)
        put(s // 4, (s % 4) * SUB, rows_ref[at, :])


def gather_rows(dst, ins, rows_ref):
    for s in range(NSUB):
        to = pl.ds(pl.multiple_of(dst[s] * SUB, SUB), SUB)
        rows_ref[to, :] = ins[s // 4][(s % 4) * SUB:(s % 4 + 1) * SUB, :]


def put_slot(me, keep, send, s, row, rows, val):
    at = pl.ds(row, rows)

    @pl.when(s // HALF == me[0])
    def _():
        keep[jnp.bitwise_xor(s % HALF, me[1]), at, :] = val

    @pl.when(s // HALF != me[0])
    def _():
        send[jnp.bitwise_xor(s % HALF, me[2]), at, :] = val


def top_rows(first, second):
    rows = lax.broadcasted_iota(jnp.int32, (16, 128), 0)
    first, second = jnp.broadcast_to(first, (16, 128)), jnp.broadcast_to(second, (16, 128))
    return jnp.where(rows == 0, first, jnp.where(rows == 1, second, 0.0)).astype(BF)


def ffn_body(n_dev, dst, me, alphas, c0, c1, c2, c3, xs, att, ot, w_out, b_out, w_up, b_up, w_down, b_down,
             o0, o1, o2, o3, gm, do_out, dott, inner, keep, send,
             cot, branch, middle, low, low_t, gfeed, gfeed_t, feed, bias_up):
    f = pl.program_id(0)
    a0, a1 = alphas[0], alphas[1]

    @pl.when(f == 0)
    def _():
        gather_rows(dst, (c0, c1, c2, c3), cot)
        br = dot(att[...], w_out[...]) + b_out[...]
        branch[...] = br
        mid = xs[...].astype(F32) + a0 * br
        middle[...] = mid
        low[...] = mid.astype(BF)
        low_t[...] = low[...].T
        g = cot[...].astype(F32)
        gfeed[...] = (a1 * g).astype(BF)
        gfeed_t[...] = gfeed[...].T
        gm[...] = g
        feed[...] = jnp.broadcast_to(b_down[...], feed.shape)

    hidden = dot(low[...], w_up[...]) + b_up[...]
    c = 0.7978845608028654
    h2 = hidden * hidden
    th = jnp.tanh(hidden * (c + (c * 0.044715) * h2))
    half = 0.5 + 0.5 * th
    active = (hidden * half).astype(BF)
    slope = half + (0.5 * hidden) * (1.0 - th * th) * (c + (3 * c * 0.044715) * h2)
    feed[...] += dot(active, w_down[...])
    grad_h = (dot(gfeed[...], w_down[...], 1, 1) * slope).astype(BF)
    bu = jnp.sum(grad_h.astype(F32), axis=0, keepdims=True)
    gd = dot(gfeed_t[...], active).astype(BF).T
    gu = dot(low_t[...], grad_h)
    gm[...] += dot(grad_h, w_up[...], 1, 1)
    for b in range(FB // 128):
        for a in range(2):
            put_slot(me, keep, send, (FB // 64) * f + 2 * b + a, 0, 256,
                     gu[a * 256:(a + 1) * 256, b * 128:(b + 1) * 128].astype(BF))
        bias_up[(FB // 128) * f + b] = bu[:, b * 128:(b + 1) * 128]
    for lb in range(4):
        for a in range(FB // 256):
            put_slot(me, keep, send, lb * 8 + (FB // 256) * f + a, 256, 256,
                     gd[a * 256:(a + 1) * 256, lb * 128:(lb + 1) * 128])

    @pl.when(f == NF - 1)
    def _():
        low[...] = (middle[...] + a1 * feed[...]).astype(BF)
        def put(k, row, val):
            (o0, o1, o2, o3)[k][row:row + SUB, :] = val

        scatter_rows(dst, low, put)
        g = cot[...].astype(F32)
        s1 = jnp.sum(feed[...] * g)
        s0 = jnp.sum(branch[...] * gm[...])
        bd = jnp.sum(gfeed[...].astype(F32), axis=0, keepdims=True)
        gb = (a0 * gm[...]).astype(BF)
        bo = jnp.sum(gb.astype(F32), axis=0, keepdims=True)
        go = dot(att[...], gb, 0, 0)
        do_out[...] = dot(gb, w_out[...], 1, 1).astype(BF)
        dt = dot(w_out[...], gb, 1, 1).astype(BF)
        dott[...] = dt
        for h in range(HEADS):
            hs = slice(h * HD, (h + 1) * HD)
            inner[h] = jnp.sum(ot[hs, :] * dt[hs, :].astype(F32), axis=0, keepdims=True)
        nr = (n_dev + 127) // 128
        row = lax.broadcasted_iota(jnp.int32, (SLOTS, 128), 0)
        lane = lax.broadcasted_iota(jnp.int32, (SLOTS, 128), 1)
        mine_row, mine_lane = me[3] // 128, me[3] % 128
        small = jnp.zeros((SLOTS, 128), F32)
        for k, total in enumerate((s0, s1)):
            rest = jnp.full((SLOTS, 128), total, F32)
            for t in range(3):
                piece = rest.astype(BF).astype(F32)
                rest = rest - piece
                here = (row == (3 * k + t) * nr + mine_row) & (lane == mine_lane)
                small = jnp.where(here, piece, small)
        zero = jnp.zeros((1, 128), F32)
        for s in range(SLOTS):
            lb, a = s // 8, s % 8
            put_slot(me, keep, send, s, 512, 64, go[a * 64:a * 64 + 64, lb * 128:(lb + 1) * 128].astype(BF))
            if s < 16:
                first = bias_up[s]
            elif s < 24:
                first = (bd if s < 20 else bo)[:, (s % 4) * 128:(s % 4 + 1) * 128]
            else:
                first = zero
            put_slot(me, keep, send, s, 576, 16, top_rows(first, small[s:s + 1]))


def ffn(n_dev, dst, me, alphas, cots, xs, att, ot, w_out, b_out, w_up, b_up, w_down, b_down):
    s = jax.ShapeDtypeStruct
    anyspec = pl.BlockSpec(memory_space=pl.ANY)
    smem = pl.BlockSpec(memory_space=pltpu.SMEM)
    vmem = pl.BlockSpec(memory_space=pltpu.VMEM)
    v = pltpu.VMEM
    half = s((HALF, R1, 128), BF)
    return pl.pallas_call(
        functools.partial(ffn_body, n_dev),
        grid=(NF,),
        out_shape=(s((256, D), BF),) * 4 + (s((T, D), F32), s((T, D), BF), s((D, T), BF),
                                            s((HEADS, 1, T), F32), half, half),
        in_specs=[smem, smem, smem] + [vmem] * 9 + [
            pl.BlockSpec((D, FB), lambda f: (0, f)),
            pl.BlockSpec((1, FB), lambda f: (0, f)),
            pl.BlockSpec((FB, D), lambda f: (f, 0)),
            vmem,
        ],
        out_specs=(vmem,) * 10,
        scratch_shapes=[v((T, D), BF), v((T, D), F32), v((T, D), F32), v((T, D), BF), v((D, T), BF), v((T, D), BF),
                        v((D, T), BF), v((T, D), F32), v((16, 1, 128), F32)],
        compiler_params=params(33),
        cost_estimate=pl.CostEstimate(flops=1875000000, bytes_accessed=2500000, transcendentals=0),
        name="ffn",
    )(dst, me, alphas, *cots, xs, att, ot, w_out, b_out, w_up, b_up, w_down, b_down)


def attn_bwd_body(bias, mask, q_in, k_in, v_in, qt, kt, do_in, dott, lse, inner, after, dqo, dko, dvo, token):
    token[...] = jnp.zeros_like(token)
    dq2, dk2, dv2 = [], [], []
    for h in range(2):
        hr = pl.ds(h * HD, HD)
        dk = [None] * NQ
        dv = [None] * NQ
        dq = []
        for i in range(NQ):
            cols = pl.ds(i * QB, QB)
            q, do = one_head(qt[:, cols], h), one_head(dott[:, cols], h)
            q_rows, do_rows = q_in[cols, :], do_in[cols, :]
            ls, inn = lse[h, :, cols], inner[h, :, cols]
            acc = None
            for j in range(i + 1):
                rows = pl.ds(j * QB, QB)
                s = dot(k_in[rows, :], q)
                if j == i:
                    p = jnp.exp(s + mask[i] - ls)
                else:
                    p = jnp.exp(s - (ls - bias[i * NQ + j]))
                dp = dot(v_in[rows, :], do)
                ds = (p * (dp - inn)).astype(BF)
                gv = dot(p.astype(BF), do_rows)
                gk = dot(ds, q_rows)
                gq = dot(kt[hr, rows], ds)
                dv[j] = gv if dv[j] is None else dv[j] + gv
                dk[j] = gk if dk[j] is None else dk[j] + gk
                acc = gq if acc is None else acc + gq
            dq.append(acc * 0.125)
        dq2.append(dq)
        dk2.append(dk)
        dv2.append(dv)
    right = lax.broadcasted_iota(jnp.int32, (QB, 2 * HD), 1) >= HD
    for i in range(NQ):
        rows = pl.ds(i * QB, QB)
        dqo[rows, :] = jnp.concatenate([dq2[0][i], dq2[1][i]], axis=0).astype(BF).T
        dko[rows, :] = jnp.where(right, dk2[1][i], dk2[0][i]).astype(BF)
        dvo[rows, :] = jnp.where(right, dv2[1][i], dv2[0][i]).astype(BF)


def attn_bwd(hp, bias, mask, q, k, v, qt, kt, do, dott, lse, inner, after):
    s = jax.ShapeDtypeStruct
    smem = pl.BlockSpec(memory_space=pltpu.SMEM)
    vmem = pl.BlockSpec(memory_space=pltpu.VMEM)
    tall = pl.BlockSpec((T, 2 * HD), lambda g: (0, hp))
    wide = pl.BlockSpec((2 * HD, T), lambda g: (hp, 0))
    line = pl.BlockSpec((2, 1, T), lambda g: (hp, 0, 0))
    return pl.pallas_call(
        attn_bwd_body,
        grid=(1,),
        out_shape=(s((T, 2 * HD), BF),) * 3 + (TOKEN,),
        in_specs=[smem, vmem, tall, tall, tall, wide, wide, tall, wide, line, line, pl.BlockSpec(memory_space=pl.ANY)],
        out_specs=(vmem,) * 4,
        compiler_params=params(20),
        cost_estimate=pl.CostEstimate(flops=625000000, bytes_accessed=625000, transcendentals=0),
        name="attn_bwd%d" % hp,
    )(bias, mask, q, k, v, qt, kt, do, dott, lse, inner, after)


def attn_dense_body(dst, me, xs, gm, w, *refs):
    parts, (d_out, keep, send, token, dx_rows) = refs[:12], refs[-5:]
    token[...] = jnp.zeros_like(token)
    grads = [jnp.concatenate([parts[3 * hp + n][...] for hp in range(4)], axis=1) for n in range(3)]
    dx = gm[...]
    for n in range(3):
        dx = dx + dot(grads[n], w[:, n * D:(n + 1) * D], 1, 1)
    dx_rows[...] = dx.astype(BF)

    def put(k, row, val):
        d_out[jnp.bitwise_xor(me[4], k), row:row + SUB, :] = val

    scatter_rows(dst, dx_rows, put)
    for n in range(3):
        g = dot(xs[...], grads[n], 0, 0)
        for s in range(SLOTS):
            lb, a = s // 8, s % 8
            put_slot(me, keep, send, s, n * 64, 64, g[a * 64:a * 64 + 64, lb * 128:(lb + 1) * 128].astype(BF))


def attn_dense(dst, me, xs, gm, w, grads, after=()):
    s = jax.ShapeDtypeStruct
    anyspec = pl.BlockSpec(memory_space=pl.ANY)
    smem = pl.BlockSpec(memory_space=pltpu.SMEM)
    vmem = pl.BlockSpec(memory_space=pltpu.VMEM)
    half = s((HALF, R2, 128), BF)
    return pl.pallas_call(
        attn_dense_body,
        out_shape=(s((4, 256, D), BF), half, half, TOKEN),
        in_specs=[smem] * 2 + [vmem] * 15 + [anyspec] * len(after),
        out_specs=(vmem,) * 4,
        scratch_shapes=[pltpu.VMEM((T, D), BF)],
        compiler_params=params(32),
        cost_estimate=pl.CostEstimate(flops=400000000, bytes_accessed=1125000, transcendentals=0),
        name="attn_dense",
    )(dst, me, xs, gm, w, *grads, *after)


DENSE = ((2, 256, 0), (8, 256, 256), (8, 64, 512))
QKV = ((8, 64, 0), (8, 64, 64), (8, 64, 128))
SMALL = 576


def finish_body(pieces, small, part, me, own, other, *refs):
    n = len(pieces)
    n_out = n + small
    stages, sem = refs[-n_out - 1:-1], refs[-1]
    outs, token = refs[-2 * n_out - 2:-n_out - 2], refs[-n_out - 2]
    token[...] = jnp.zeros_like(token)

    def each(slot, depth):
        copies = []
        for which, src in enumerate((own, other)):
            core = me[0] if which == 0 else 1 - me[0]
            s = core * HALF + jnp.bitwise_xor(slot + 8 * part, me[1 + which])
            for k, (tall, rows, row) in enumerate(pieces):
                stages[k][depth, which] = src[slot, row:row + rows, :].astype(F32)
                to = outs[k].at[pl.ds(pl.multiple_of((s % tall) * rows, rows), rows),
                                pl.ds(pl.multiple_of((s // tall) * 128, 128), 128)]
                copies.append(pltpu.make_async_copy(stages[k].at[depth, which], to, sem.at[depth, which, k]))
            if small:
                stages[n][depth, which] = src[slot, SMALL:SMALL + 16, :].astype(F32)[:8]
                to = outs[n].at[pl.ds(pl.multiple_of(s * 8, 8), 8)]
                copies.append(pltpu.make_async_copy(stages[n].at[depth, which], to, sem.at[depth, which, n]))
        return copies

    pending = [None] * 4
    for slot in range(8):
        depth = slot % 4
        if pending[depth] is not None:
            for c in pending[depth]:
                c.wait()
        pending[depth] = each(slot, depth)
        for c in pending[depth]:
            c.start()
    for group in pending:
        for c in group:
            c.wait()


def finish(pieces, part, me, got, before, after):
    anyspec = pl.BlockSpec(memory_space=pl.ANY)
    vmem = pl.BlockSpec(memory_space=pltpu.VMEM)
    s = jax.ShapeDtypeStruct
    square = s((D, D), F32)
    small = pieces is DENSE
    shapes = (s((D, FF), F32), s((FF, D), F32), square, s((SLOTS * 8, 128), F32)) if small else (square,) * 3
    n = len(shapes)
    *out, token = pl.pallas_call(
        functools.partial(finish_body, pieces, int(small), part),
        out_shape=shapes + (TOKEN,),
        in_specs=[pl.BlockSpec(memory_space=pltpu.SMEM)] + [vmem] * 2 + [anyspec] * (len(before) + len(after)),
        out_specs=(anyspec,) * n + (vmem,),
        scratch_shapes=[pltpu.VMEM((4, 2, rows, 128), F32) for _, rows, _ in pieces]
        + [pltpu.VMEM((4, 2, 8, 128), F32)] * small + [pltpu.SemaphoreType.DMA((4, 2, n))],
        input_output_aliases={3 + k: k for k in range(len(before))},
        compiler_params=params(20),
        cost_estimate=pl.CostEstimate(flops=1_000_000, bytes_accessed=4_000_000, transcendentals=0),
        name="finish%d_%d" % (n, part),
    )(me, *got, *before, *after)
    return tuple(out), token


def pairs(size, bit):
    return [(a, a ^ bit) for a in range(size)]


def add(a, b):
    return (a.astype(F32) + b.astype(F32)).astype(BF)


def halve_body(keep_lo, keep_hi, got_lo, got_hi, *refs):
    lo, hi, token = refs[-3:]
    lo[...] = add(keep_lo[...], got_lo[...])
    hi[...] = add(keep_hi[...], got_hi[...])
    token[...] = jnp.zeros_like(token)


def halve(keep, got, after=()):
    m, rows = keep.shape[0] // 2, keep.shape[1]
    steps = max(1, m // 2)
    lo = pl.BlockSpec((m // steps, rows, 128), lambda g: (g, 0, 0))
    hi = pl.BlockSpec((m // steps, rows, 128), lambda g: (g + steps, 0, 0))
    half = jax.ShapeDtypeStruct((m, rows, 128), BF)
    return pl.pallas_call(
        halve_body,
        grid=(steps,),
        out_shape=(half, half, TOKEN),
        in_specs=[lo, hi, lo, hi] + [pl.BlockSpec(memory_space=pl.ANY)] * len(after),
        out_specs=(lo, lo, pl.BlockSpec(memory_space=pltpu.VMEM)),
        compiler_params=params(12),
        cost_estimate=pl.CostEstimate(flops=m * rows * 32, bytes_accessed=m * rows * 200, transcendentals=0),
        name="halve%d_%d" % (m, rows),
    )(keep, keep, got, got, *after)


def plus_body(a, b, *refs):
    out, token = refs[-2:]
    out[...] = add(a[...], b[...])
    token[...] = jnp.zeros_like(token)


def plus(a, b, after=(), twist=0):
    rows = a.shape[1]
    one = pl.BlockSpec((1, rows, 128), lambda g: (g, 0, 0))
    other = pl.BlockSpec((1, rows, 128), lambda g: (jnp.bitwise_xor(g, twist), 0, 0))
    return pl.pallas_call(
        plus_body,
        grid=(a.shape[0],),
        out_shape=(jax.ShapeDtypeStruct(a.shape, BF), TOKEN),
        in_specs=[one, other] + [pl.BlockSpec(memory_space=pl.ANY)] * len(after),
        out_specs=(one, pl.BlockSpec(memory_space=pltpu.VMEM)),
        compiler_params=params(8),
        cost_estimate=pl.CostEstimate(flops=a.shape[0] * rows * 32, bytes_accessed=a.shape[0] * rows * 100, transcendentals=0),
        name="plus%d_%d" % (a.shape[0], rows),
    )(a, b, *after)


def join_body(n, *refs):
    out, token = refs[-2:]
    row = 0
    for a, b in zip(refs[0:2 * n:2], refs[1:2 * n:2]):
        m, rows = a.shape[:2]
        out[:m, row:row + rows] = a[...]
        out[m:, row:row + rows] = b[...]
        row += rows
    token[...] = jnp.zeros_like(token)


def join(parts, after=()):
    m, rows = parts[0].shape[0], sum(p.shape[1] for p in parts[::2])
    vmem = pl.BlockSpec(memory_space=pltpu.VMEM)
    return pl.pallas_call(
        functools.partial(join_body, len(parts) // 2),
        out_shape=(jax.ShapeDtypeStruct((2 * m, rows, 128), BF), TOKEN),
        in_specs=[vmem] * len(parts) + [pl.BlockSpec(memory_space=pl.ANY)] * len(after),
        out_specs=(vmem, vmem),
        compiler_params=params(12),
        cost_estimate=pl.CostEstimate(flops=1000, bytes_accessed=m * rows * 100, transcendentals=0),
        name="join%d_%d" % (m, rows),
    )(*parts, *after)


def pos_rows(v):
    left = lax.broadcasted_iota(jnp.int32, (1, 128), 1) < SUB
    out = []
    for r in range(v.shape[0]):
        high, rest = v[r:r + 1] >> 5, v[r:r + 1] & 31
        out.append(jnp.where(left, high, pltpu.roll(rest, SUB, 1)))
        out.append(jnp.where(left, pltpu.roll(high, SUB, 1), rest))
    return jnp.concatenate(out, axis=0)


def pick_body(with_pos, me, short, long, *refs):
    outs, sem = refs[-5:-1], refs[-1]
    waits = []
    for k in range(4):
        j = jnp.bitwise_xor(me[4], k)
        to = outs[k].at[pl.ds(0, 256)]

        @pl.when(j == 0)
        def _():
            pltpu.make_async_copy(short, to, sem.at[k]).start()

        @pl.when(j > 0)
        def _():
            pltpu.make_async_copy(long.at[jnp.maximum(j - 1, 0)], to, sem.at[k]).start()

        waits.append(pltpu.make_async_copy(short, to, sem.at[k]))
    if with_pos:
        of_short = pos_rows(jnp.concatenate([refs[0][...], refs[0][...] + 512], axis=0))
        of_long = pos_rows(refs[1][...])
        for k in range(4):
            tile = jnp.where(jnp.bitwise_xor(me[4], k) == 0, of_short, of_long).astype(F32)
            tile = jnp.concatenate([tile, jnp.zeros((12, 128), F32)], axis=0).astype(BF)
            outs[k][256:272, :] = jnp.concatenate([tile, jnp.zeros((16, D - 128), BF)], axis=1)
    for c in waits:
        c.wait()


def pick(me, short, long, pos=(), after=()):
    anyspec = pl.BlockSpec(memory_space=pl.ANY)
    vmem = pl.BlockSpec(memory_space=pltpu.VMEM)
    out = jax.ShapeDtypeStruct((272 if pos else 256, D), BF)
    return pl.pallas_call(
        functools.partial(pick_body, bool(pos)),
        out_shape=(out,) * 4,
        in_specs=[pl.BlockSpec(memory_space=pltpu.SMEM)] + [anyspec] * 2 + [vmem] * len(pos) + [anyspec] * len(after),
        out_specs=(vmem,) * 4,
        scratch_shapes=[pltpu.SemaphoreType.DMA((4,))],
        compiler_params=params(56 if pos else 8),
        cost_estimate=pl.CostEstimate(flops=1000, bytes_accessed=500_000, transcendentals=0),
        name="pick%d" % len(pos),
    )(me, short.reshape(256, D), long, *pos, *after)


class Sums:
    def __init__(self, n_dp, n_seq):
        self.n_dp, self.n_seq = n_dp, n_seq
        self.core = pairs(n_dp, 1)
        self.first = [(a, a ^ (4 if a & 1 else 2)) for a in range(n_dp)]
        self.second = [(a, a ^ (2 if a & 1 else 4)) for a in range(n_dp)]

    def dp(self, v, perm):
        return lax.ppermute(v, "dp", perm)

    def seq(self, v, bit):
        return lax.ppermute(v, "seq", pairs(self.n_seq, bit))

    def rest(self, v):
        bit = 8
        while bit < self.n_dp:
            v = add(v, self.dp(v, pairs(self.n_dp, bit)))
            bit *= 2
        return v


def tie(a, b):
    return lax.optimization_barrier((a, b))


def per_device(n_dp, n_seq, x_short, order_short, x_long, order_long, w_query, w_key, w_value, w_out, b_out, alphas,
               w_up, b_up, w_down, b_down, cot_short, cot_long):
    i = lax.axis_index("seq")
    d = lax.axis_index("dp")
    n_dev = n_dp * n_seq

    def give_back(mine):
        return [mine[0]] + [lax.ppermute(mine[k], "seq", pairs(n_seq, k)) for k in range(1, n_seq)]

    def home(got):
        def chunk(j):
            k = jnp.bitwise_xor(i, j)
            v = jnp.where(k < 2, jnp.where(k == 0, got[0], got[1]), jnp.where(k == 2, got[2], got[3]))
            return v
        return chunk(0).reshape(2, 128, D), jnp.stack([chunk(j) for j in range(1, n_seq)])

    def give_back(mine):
        return [mine[0]] + [lax.ppermute(mine[k], "seq", pairs(n_seq, k)) for k in range(1, n_seq)]

    c, bx, by = d & 1, (d >> 1) & 1, (d >> 2) & 1
    z = (i & 1) * 2 + (i >> 1)
    x_first, y_first = bx * 8 + by * 4 + z, by * 8 + bx * 4 + z
    at = jnp.arange(8)
    me = jnp.where(at == 0, c, jnp.where(at == 1, jnp.where(c == 0, x_first, y_first), jnp.where(
        at == 2, jnp.where(c == 0, y_first, x_first), jnp.where(at == 3, d * n_seq + i, i)))).astype(jnp.int32)
    xs = give_back(pick(me, x_short, x_long, (order_short.reshape(1, 128), order_long.reshape(2, 128))))
    w = jnp.concatenate([w_query, w_key, w_value], axis=1)
    wt = w.T
    mine, *far = pick(me, cot_short, cot_long, (), (wt,))
    far, _ = tie(far, xs[1:])
    cots = give_back([mine] + far)
    rows, q, k, v_rows, qt, kt, ot, att, lse, mask, dst, bias = attn_fwd(me, xs, w, wt)
    o0, o1, o2, o3, gm, do, dott, inner, keep, send = ffn(
        n_dev, dst, me, alphas, cots, rows, att, ot, w_out, b_out.reshape(1, D), w_up, b_up.reshape(1, FF),
        w_down, b_down.reshape(1, D))
    net = Sums(n_dp, n_seq)

    def bwd(hp, after):
        *g, token = attn_bwd(hp, bias, mask, q, k, v_rows, qt, kt, do, dott, lse, inner, after)
        return g, token

    got = net.dp(send, net.core)
    outs = give_back((o0, o1, o2, o3))
    g0, token = bwd(0, lse)
    lo, hi, token = halve(keep, got, (token,))
    got = net.dp(hi, net.first)
    g1, token = bwd(1, token)
    g2, token = bwd(2, token)
    g3, token = bwd(3, token)
    lo, hi, token = halve(lo, got, (token,))
    got = net.dp(hi, net.second)
    d_rows, keep2, send2, token = attn_dense(
        dst, me, rows, gm, w, g0 + g1 + g2 + g3, (token,))
    out_short, out_long = home(outs)
    lo, hi, token = halve(lo, got, (token, out_short, out_long))
    got = net.seq(hi, 1)
    got2 = net.dp(send2, net.core)
    lo, hi, token = halve(lo, got, (token,))
    got = net.seq(hi, 2)
    lo2, hi2, token = halve(keep2, got2, (token,))
    got2 = net.dp(hi2, net.first)
    v, token = plus(lo, got, (token,))
    v = net.rest(v)
    got = net.seq(v, 2)
    lo2, hi2, token = halve(lo2, got2, (token,))
    got2 = net.dp(hi2, net.second)
    v, token = join((v, got), (token,))
    got = net.seq(v, 1)
    u, token = plus(lo2, got2, (token,))
    got2 = net.seq(u, 1)
    v, token = join((v, got), (token,))
    got = net.dp(v, net.second)
    u, token = plus(u, got2, (token,), 2)
    got2 = net.seq(u, 2)
    v, token = join((v, got), (token,))
    far = net.dp(v, net.first)
    near = net.dp(v, net.core)
    first, token = finish(DENSE, 0, me, (v, near), (), (token,))
    u, token = plus(u, got2, (token,), 1)
    u = net.rest(u)
    d_rows, _ = tie(d_rows, token)
    dxs = lax.all_to_all(d_rows, "seq", 0, 0)
    got2 = net.dp(u, net.second)
    u, token = join((u, got2), (token,))
    far2 = net.dp(u, net.first)
    near2 = net.dp(u, net.core)
    (g_up, g_down, g_out, small), token = finish(DENSE, 1, me, (far, net.dp(far, net.core)), first, (token,))
    first2, token = finish(QKV, 0, me, (u, near2), (), (token,))
    (g_query, g_key, g_value), token = finish(QKV, 1, me, (far2, net.dp(far2, net.core)), first2, (token,))
    dxs, _ = tie(dxs, token)
    dx_short, dx_long = dxs[0].reshape(2, 128, D).astype(F32), dxs[1:].astype(F32)
    small = small.reshape(SLOTS, 8, 128)
    flat = small[:24, 0].reshape(-1)
    nr = (n_dev + 127) // 128
    g_alphas = jnp.sum(small[:6 * nr, 1].reshape(2, 3 * nr * 128), axis=1)
    return (out_short, out_long, dx_short, dx_long, g_query, g_key, g_value, g_out, flat[2560:3072], g_alphas,
            g_up, flat[:2048], g_down, flat[2048:2560])


def solution(mesh):
    split = P("dp", "seq", None)
    whole = P()
    return jax.shard_map(
        functools.partial(per_device, mesh.shape["dp"], mesh.shape["seq"]),
        mesh=mesh,
        in_specs=(split, P("seq"), split, P("seq")) + (whole,) * 10 + (split, split),
        out_specs=(split,) * 4 + (whole,) * 10,
        check_vma=False,
    )
```

```python
import functools
import jax
import jax.numpy as jnp
from jax import lax
from jax.sharding import PartitionSpec as P
from jax.experimental import pallas as pl
from jax.experimental.pallas import tpu as pltpu

BF = jnp.bfloat16
F32 = jnp.float32
HEADS = 8
HD = 64
D = 512
FF = 2048
T = 1024
SUB = 64
NSUB = T // SUB
QB = 256
NQ = T // QB


def dot(a, b, ca=1, cb=0):
    return lax.dot_general(a, b, (((ca,), (cb,)), ((), ())), preferred_element_type=F32)


def params(mb):
    return pltpu.CompilerParams(vmem_limit_bytes=mb * 1024 * 1024)


def one_head(pair, h):
    row = lax.broadcasted_iota(jnp.int32, pair.shape, 0)
    return jnp.where((row >= HD) == (h == 1), pair, jnp.zeros_like(pair))


def attn_fwd_body(me, c0, c1, c2, c3, w, wt, xs, q_out, k_out, v_out, qt, kt, ot, att, lse, mask, dst, bias,
                  vt):
    chunks = (c0, c1, c2, c3)
    is_short = me[4] == 0
    runs = jnp.concatenate([chunks[n][256:272, :128].astype(F32)[:4] for n in range(4)], axis=0)
    spot = runs[:, :SUB] * 32.0 + runs[:, SUB:2 * SUB]
    lowest = jnp.min(spot, axis=1, keepdims=True).astype(jnp.int32)
    odd = lax.broadcasted_iota(jnp.int32, (NSUB, 1), 0) & 1
    to = jnp.where(is_short, lowest >> 6, 2 * (lowest >> 7) + odd)
    for s in range(NSUB):
        dst[s] = jnp.max(to[s:s + 1, :])
    gather_rows(dst, chunks, xs)
    for a in range(NQ):
        for b in range(NQ):
            bias[a * NQ + b] = jnp.where(is_short, 0.0 if a // 2 == b // 2 else -1e30, 0.0)
    place = (lax.broadcasted_iota(jnp.int32, (NSUB, NSUB), 1) == to).astype(BF)
    by_run = 32.0 * dot(place, runs[:, :SUB].astype(BF), 0, 0) + dot(place, runs[:, SUB:2 * SUB].astype(BF), 0, 0)
    for a in range(NQ):
        row = jnp.concatenate([by_run[4 * a + b:4 * a + b + 1, :] for b in range(4)], axis=1)
        across = jnp.broadcast_to(row, (QB, QB))
        mask[a] = jnp.where(across.T <= across, 0.0, -1e30)
    for i in range(NQ):
        rows = pl.ds(i * QB, QB)
        x = xs[rows, :]
        qkv = dot(x, w[...]).astype(BF)
        qkvt = dot(wt[...], x, 1, 1).astype(BF)
        q_out[rows, :] = qkv[:, :D] * BF(0.125)
        k_out[rows, :] = qkv[:, D:2 * D]
        v_out[rows, :] = qkv[:, 2 * D:]
        qt[:, rows] = qkvt[:D] * BF(0.125)
        kt[:, rows] = qkvt[D:2 * D]
        vt[:, rows] = qkvt[2 * D:]

    def pair(hp, carry):
        wide = pl.ds(pl.multiple_of(hp * 2 * HD, 2 * HD), 2 * HD)
        for i in range(NQ):
            cols = pl.ds(i * QB, QB)
            both = qt[wide, cols]
            for h in range(2):
                hr = pl.ds(pl.multiple_of(hp * 2 * HD + h * HD, HD), HD)
                q = one_head(both, h)
                tiles, tops = [], []
                for j in range(i + 1):
                    s = dot(k_out[pl.ds(j * QB, QB), wide], q)
                    if j == i:
                        s = s + mask[i]
                        tops.append(jnp.max(s, axis=0, keepdims=True))
                    else:
                        tops.append(jnp.max(s, axis=0, keepdims=True) + bias[i * NQ + j])
                    tiles.append(s)
                m = functools.reduce(jnp.maximum, tops)
                total, o = None, None
                for j in range(i + 1):
                    mj = m if j == i else m - bias[i * NQ + j]
                    e = jnp.exp(tiles[j] - mj)
                    t = jnp.sum(e, axis=0, keepdims=True)
                    total = t if total is None else total + t
                    p = dot(vt[hr, pl.ds(j * QB, QB)], e.astype(BF))
                    o = p if o is None else o + p
                o = o * (1.0 / total)
                ot[hr, cols] = o
                lse[hp * 2 + h, :, cols] = m + jnp.log(total)
        return carry

    lax.fori_loop(0, HEADS // 2, pair, 0)
    for i in range(NQ):
        rows = pl.ds(i * QB, QB)
        att[rows, :] = ot[:, rows].astype(BF).T


def attn_fwd(me, chunks, w, wt):
    s = jax.ShapeDtypeStruct
    rows, cols = s((T, D), BF), s((D, T), BF)
    smem = pl.BlockSpec(memory_space=pltpu.SMEM)
    vmem = pl.BlockSpec(memory_space=pltpu.VMEM)
    return pl.pallas_call(
        attn_fwd_body,
        out_shape=(rows, rows, rows, rows, cols, cols, s((D, T), F32), rows, s((HEADS, 1, T), F32),
                   s((NQ, QB, QB), F32), s((NSUB,), jnp.int32), s((NQ * NQ,), F32)),
        in_specs=[smem] + [vmem] * 6,
        out_specs=(vmem,) * 10 + (smem,) * 2,
        scratch_shapes=[pltpu.VMEM((D, T), BF)],
        compiler_params=params(24),
        cost_estimate=pl.CostEstimate(flops=1500000000, bytes_accessed=2000000, transcendentals=0),
        name="attn_fwd",
    )(me, *chunks, w, wt)


FB = 512
NF = FF // FB
SLOTS = 32
HALF = SLOTS // 2
TOKEN = jax.ShapeDtypeStruct((8, 128), F32)
R1 = 592
R2 = 192


def scatter_rows(dst, rows_ref, put):
    for s in range(NSUB):
        at = pl.ds(pl.multiple_of(dst[s] * SUB, SUB), SUB)
        put(s // 4, (s % 4) * SUB, rows_ref[at, :])


def gather_rows(dst, ins, rows_ref):
    for s in range(NSUB):
        to = pl.ds(pl.multiple_of(dst[s] * SUB, SUB), SUB)
        rows_ref[to, :] = ins[s // 4][(s % 4) * SUB:(s % 4 + 1) * SUB, :]


def put_slot(me, keep, send, s, row, rows, val):
    at = pl.ds(row, rows)

    @pl.when(s // HALF == me[0])
    def _():
        keep[jnp.bitwise_xor(s % HALF, me[1]), at, :] = val

    @pl.when(s // HALF != me[0])
    def _():
        send[jnp.bitwise_xor(s % HALF, me[2]), at, :] = val


def top_rows(first, second):
    rows = lax.broadcasted_iota(jnp.int32, (16, 128), 0)
    first, second = jnp.broadcast_to(first, (16, 128)), jnp.broadcast_to(second, (16, 128))
    return jnp.where(rows == 0, first, jnp.where(rows == 1, second, 0.0)).astype(BF)


def ffn_body(n_dev, dst, me, alphas, c0, c1, c2, c3, xs, att, ot, w_out, b_out, w_up, b_up, w_down, b_down,
             o0, o1, o2, o3, gm, do_out, dott, inner, keep, send,
             cot, branch, middle, low, low_t, gfeed, gfeed_t, feed, bias_up):
    f = pl.program_id(0)
    a0, a1 = alphas[0], alphas[1]

    @pl.when(f == 0)
    def _():
        gather_rows(dst, (c0, c1, c2, c3), cot)
        br = dot(att[...], w_out[...]) + b_out[...]
        branch[...] = br
        mid = xs[...].astype(F32) + a0 * br
        middle[...] = mid
        low[...] = mid.astype(BF)
        low_t[...] = low[...].T
        g = cot[...].astype(F32)
        gfeed[...] = (a1 * g).astype(BF)
        gfeed_t[...] = gfeed[...].T
        gm[...] = g
        feed[...] = jnp.broadcast_to(b_down[...], feed.shape)

    hidden = dot(low[...], w_up[...]) + b_up[...]
    c = 0.7978845608028654
    h2 = hidden * hidden
    th = jnp.tanh(hidden * (c + (c * 0.044715) * h2))
    half = 0.5 + 0.5 * th
    active = (hidden * half).astype(BF)
    slope = half + (0.5 * hidden) * (1.0 - th * th) * (c + (3 * c * 0.044715) * h2)
    feed[...] += dot(active, w_down[...])
    grad_h = (dot(gfeed[...], w_down[...], 1, 1) * slope).astype(BF)
    bu = jnp.sum(grad_h.astype(F32), axis=0, keepdims=True)
    gd = dot(gfeed_t[...], active).astype(BF).T
    gu = dot(low_t[...], grad_h)
    gm[...] += dot(grad_h, w_up[...], 1, 1)
    for b in range(FB // 128):
        for a in range(2):
            put_slot(me, keep, send, (FB // 64) * f + 2 * b + a, 0, 256,
                     gu[a * 256:(a + 1) * 256, b * 128:(b + 1) * 128].astype(BF))
        bias_up[(FB // 128) * f + b] = bu[:, b * 128:(b + 1) * 128]
    for lb in range(4):
        for a in range(FB // 256):
            put_slot(me, keep, send, lb * 8 + (FB // 256) * f + a, 256, 256,
                     gd[a * 256:(a + 1) * 256, lb * 128:(lb + 1) * 128])

    @pl.when(f == NF - 1)
    def _():
        low[...] = (middle[...] + a1 * feed[...]).astype(BF)
        def put(k, row, val):
            (o0, o1, o2, o3)[k][row:row + SUB, :] = val

        scatter_rows(dst, low, put)
        g = cot[...].astype(F32)
        s1 = jnp.sum(feed[...] * g)
        s0 = jnp.sum(branch[...] * gm[...])
        bd = jnp.sum(gfeed[...].astype(F32), axis=0, keepdims=True)
        gb = (a0 * gm[...]).astype(BF)
        bo = jnp.sum(gb.astype(F32), axis=0, keepdims=True)
        go = dot(att[...], gb, 0, 0)
        do_out[...] = dot(gb, w_out[...], 1, 1).astype(BF)
        dt = dot(w_out[...], gb, 1, 1).astype(BF)
        dott[...] = dt
        for h in range(HEADS):
            hs = slice(h * HD, (h + 1) * HD)
            inner[h] = jnp.sum(ot[hs, :] * dt[hs, :].astype(F32), axis=0, keepdims=True)
        nr = (n_dev + 127) // 128
        row = lax.broadcasted_iota(jnp.int32, (SLOTS, 128), 0)
        lane = lax.broadcasted_iota(jnp.int32, (SLOTS, 128), 1)
        mine_row, mine_lane = me[3] // 128, me[3] % 128
        small = jnp.zeros((SLOTS, 128), F32)
        for k, total in enumerate((s0, s1)):
            rest = jnp.full((SLOTS, 128), total, F32)
            for t in range(3):
                piece = rest.astype(BF).astype(F32)
                rest = rest - piece
                here = (row == (3 * k + t) * nr + mine_row) & (lane == mine_lane)
                small = jnp.where(here, piece, small)
        zero = jnp.zeros((1, 128), F32)
        for s in range(SLOTS):
            lb, a = s // 8, s % 8
            put_slot(me, keep, send, s, 512, 64, go[a * 64:a * 64 + 64, lb * 128:(lb + 1) * 128].astype(BF))
            if s < 16:
                first = bias_up[s]
            elif s < 24:
                first = (bd if s < 20 else bo)[:, (s % 4) * 128:(s % 4 + 1) * 128]
            else:
                first = zero
            put_slot(me, keep, send, s, 576, 16, top_rows(first, small[s:s + 1]))


def ffn(n_dev, dst, me, alphas, cots, xs, att, ot, w_out, b_out, w_up, b_up, w_down, b_down):
    s = jax.ShapeDtypeStruct
    anyspec = pl.BlockSpec(memory_space=pl.ANY)
    smem = pl.BlockSpec(memory_space=pltpu.SMEM)
    vmem = pl.BlockSpec(memory_space=pltpu.VMEM)
    v = pltpu.VMEM
    half = s((HALF, R1, 128), BF)
    return pl.pallas_call(
        functools.partial(ffn_body, n_dev),
        grid=(NF,),
        out_shape=(s((256, D), BF),) * 4 + (s((T, D), F32), s((T, D), BF), s((D, T), BF),
                                            s((HEADS, 1, T), F32), half, half),
        in_specs=[smem, smem, smem] + [vmem] * 9 + [
            pl.BlockSpec((D, FB), lambda f: (0, f)),
            pl.BlockSpec((1, FB), lambda f: (0, f)),
            pl.BlockSpec((FB, D), lambda f: (f, 0)),
            vmem,
        ],
        out_specs=(vmem,) * 10,
        scratch_shapes=[v((T, D), BF), v((T, D), F32), v((T, D), F32), v((T, D), BF), v((D, T), BF), v((T, D), BF),
                        v((D, T), BF), v((T, D), F32), v((16, 1, 128), F32)],
        compiler_params=params(40),
        cost_estimate=pl.CostEstimate(flops=1875000000, bytes_accessed=2500000, transcendentals=0),
        name="ffn",
    )(dst, me, alphas, *cots, xs, att, ot, w_out, b_out, w_up, b_up, w_down, b_down)


def attn_bwd_body(bias, mask, q_in, k_in, v_in, qt, kt, do_in, dott, lse, inner, after, dqo, dko, dvo, token):
    token[...] = jnp.zeros_like(token)
    dq2, dk2, dv2 = [], [], []
    for h in range(2):
        hr = pl.ds(h * HD, HD)
        dk = [None] * NQ
        dv = [None] * NQ
        dq = []
        for i in range(NQ):
            cols = pl.ds(i * QB, QB)
            q, do = one_head(qt[:, cols], h), one_head(dott[:, cols], h)
            q_rows, do_rows = q_in[cols, :], do_in[cols, :]
            ls, inn = lse[h, :, cols], inner[h, :, cols]
            acc = None
            for j in range(i + 1):
                rows = pl.ds(j * QB, QB)
                s = dot(k_in[rows, :], q)
                if j == i:
                    p = jnp.exp(s + mask[i] - ls)
                else:
                    p = jnp.exp(s - (ls - bias[i * NQ + j]))
                dp = dot(v_in[rows, :], do)
                ds = (p * (dp - inn)).astype(BF)
                gv = dot(p.astype(BF), do_rows)
                gk = dot(ds, q_rows)
                gq = dot(kt[hr, rows], ds)
                dv[j] = gv if dv[j] is None else dv[j] + gv
                dk[j] = gk if dk[j] is None else dk[j] + gk
                acc = gq if acc is None else acc + gq
            dq.append(acc * 0.125)
        dq2.append(dq)
        dk2.append(dk)
        dv2.append(dv)
    right = lax.broadcasted_iota(jnp.int32, (QB, 2 * HD), 1) >= HD
    for i in range(NQ):
        rows = pl.ds(i * QB, QB)
        dqo[rows, :] = jnp.concatenate([dq2[0][i], dq2[1][i]], axis=0).astype(BF).T
        dko[rows, :] = jnp.where(right, dk2[1][i], dk2[0][i]).astype(BF)
        dvo[rows, :] = jnp.where(right, dv2[1][i], dv2[0][i]).astype(BF)


def attn_bwd(hp, bias, mask, q, k, v, qt, kt, do, dott, lse, inner, after):
    s = jax.ShapeDtypeStruct
    smem = pl.BlockSpec(memory_space=pltpu.SMEM)
    vmem = pl.BlockSpec(memory_space=pltpu.VMEM)
    tall = pl.BlockSpec((T, 2 * HD), lambda g: (0, hp))
    wide = pl.BlockSpec((2 * HD, T), lambda g: (hp, 0))
    line = pl.BlockSpec((2, 1, T), lambda g: (hp, 0, 0))
    return pl.pallas_call(
        attn_bwd_body,
        grid=(1,),
        out_shape=(s((T, 2 * HD), BF),) * 3 + (TOKEN,),
        in_specs=[smem, vmem, tall, tall, tall, wide, wide, tall, wide, line, line, pl.BlockSpec(memory_space=pl.ANY)],
        out_specs=(vmem,) * 4,
        compiler_params=params(20),
        cost_estimate=pl.CostEstimate(flops=625000000, bytes_accessed=625000, transcendentals=0),
        name="attn_bwd%d" % hp,
    )(bias, mask, q, k, v, qt, kt, do, dott, lse, inner, after)


def attn_dense_body(dst, me, xs, gm, w, *refs):
    parts, (d_out, keep, send, token, dx_rows) = refs[:12], refs[-5:]
    token[...] = jnp.zeros_like(token)
    grads = [jnp.concatenate([parts[3 * hp + n][...] for hp in range(4)], axis=1) for n in range(3)]
    dx = gm[...]
    for n in range(3):
        dx = dx + dot(grads[n], w[:, n * D:(n + 1) * D], 1, 1)
    dx_rows[...] = dx.astype(BF)

    def put(k, row, val):
        d_out[jnp.bitwise_xor(me[4], k), row:row + SUB, :] = val

    scatter_rows(dst, dx_rows, put)
    for n in range(3):
        g = dot(xs[...], grads[n], 0, 0)
        for s in range(SLOTS):
            lb, a = s // 8, s % 8
            put_slot(me, keep, send, s, n * 64, 64, g[a * 64:a * 64 + 64, lb * 128:(lb + 1) * 128].astype(BF))


def attn_dense(dst, me, xs, gm, w, grads, after=()):
    s = jax.ShapeDtypeStruct
    anyspec = pl.BlockSpec(memory_space=pl.ANY)
    smem = pl.BlockSpec(memory_space=pltpu.SMEM)
    vmem = pl.BlockSpec(memory_space=pltpu.VMEM)
    half = s((HALF, R2, 128), BF)
    return pl.pallas_call(
        attn_dense_body,
        out_shape=(s((4, 256, D), BF), half, half, TOKEN),
        in_specs=[smem] * 2 + [vmem] * 15 + [anyspec] * len(after),
        out_specs=(vmem,) * 4,
        scratch_shapes=[pltpu.VMEM((T, D), BF)],
        compiler_params=params(32),
        cost_estimate=pl.CostEstimate(flops=400000000, bytes_accessed=1125000, transcendentals=0),
        name="attn_dense",
    )(dst, me, xs, gm, w, *grads, *after)


DENSE = ((2, 256, 0), (8, 256, 256), (8, 64, 512))
QKV = ((8, 64, 0), (8, 64, 64), (8, 64, 128))
SMALL = 576


def finish_body(pieces, small, part, me, own, other, *refs):
    n = len(pieces)
    n_out = n + small
    stages, sem = refs[-n_out - 1:-1], refs[-1]
    outs, token = refs[-2 * n_out - 2:-n_out - 2], refs[-n_out - 2]
    token[...] = jnp.zeros_like(token)

    def each(slot, depth):
        copies = []
        for which, src in enumerate((own, other)):
            core = me[0] if which == 0 else 1 - me[0]
            s = core * HALF + jnp.bitwise_xor(slot + 8 * part, me[1 + which])
            for k, (tall, rows, row) in enumerate(pieces):
                stages[k][depth, which] = src[slot, row:row + rows, :].astype(F32)
                to = outs[k].at[pl.ds(pl.multiple_of((s % tall) * rows, rows), rows),
                                pl.ds(pl.multiple_of((s // tall) * 128, 128), 128)]
                copies.append(pltpu.make_async_copy(stages[k].at[depth, which], to, sem.at[depth, which, k]))
            if small:
                stages[n][depth, which] = src[slot, SMALL:SMALL + 16, :].astype(F32)[:8]
                to = outs[n].at[pl.ds(pl.multiple_of(s * 8, 8), 8)]
                copies.append(pltpu.make_async_copy(stages[n].at[depth, which], to, sem.at[depth, which, n]))
        return copies

    pending = [None] * 4
    for slot in range(8):
        depth = slot % 4
        if pending[depth] is not None:
            for c in pending[depth]:
                c.wait()
        pending[depth] = each(slot, depth)
        for c in pending[depth]:
            c.start()
    for group in pending:
        for c in group:
            c.wait()


def finish(pieces, part, me, got, before, after):
    anyspec = pl.BlockSpec(memory_space=pl.ANY)
    vmem = pl.BlockSpec(memory_space=pltpu.VMEM)
    s = jax.ShapeDtypeStruct
    square = s((D, D), F32)
    small = pieces is DENSE
    shapes = (s((D, FF), F32), s((FF, D), F32), square, s((SLOTS * 8, 128), F32)) if small else (square,) * 3
    n = len(shapes)
    *out, token = pl.pallas_call(
        functools.partial(finish_body, pieces, int(small), part),
        out_shape=shapes + (TOKEN,),
        in_specs=[pl.BlockSpec(memory_space=pltpu.SMEM)] + [vmem] * 2 + [anyspec] * (len(before) + len(after)),
        out_specs=(anyspec,) * n + (vmem,),
        scratch_shapes=[pltpu.VMEM((4, 2, rows, 128), F32) for _, rows, _ in pieces]
        + [pltpu.VMEM((4, 2, 8, 128), F32)] * small + [pltpu.SemaphoreType.DMA((4, 2, n))],
        input_output_aliases={3 + k: k for k in range(len(before))},
        compiler_params=params(20),
        cost_estimate=pl.CostEstimate(flops=1_000_000, bytes_accessed=4_000_000, transcendentals=0),
        name="finish%d_%d" % (n, part),
    )(me, *got, *before, *after)
    return tuple(out), token


def pairs(size, bit):
    return [(a, a ^ bit) for a in range(size)]


def add(a, b):
    return (a.astype(F32) + b.astype(F32)).astype(BF)


def halve_body(keep_lo, keep_hi, got_lo, got_hi, *refs):
    lo, hi, token = refs[-3:]
    lo[...] = add(keep_lo[...], got_lo[...])
    hi[...] = add(keep_hi[...], got_hi[...])
    token[...] = jnp.zeros_like(token)


def halve(keep, got, after=()):
    m, rows = keep.shape[0] // 2, keep.shape[1]
    steps = max(1, m // 2)
    lo = pl.BlockSpec((m // steps, rows, 128), lambda g: (g, 0, 0))
    hi = pl.BlockSpec((m // steps, rows, 128), lambda g: (g + steps, 0, 0))
    half = jax.ShapeDtypeStruct((m, rows, 128), BF)
    return pl.pallas_call(
        halve_body,
        grid=(steps,),
        out_shape=(half, half, TOKEN),
        in_specs=[lo, hi, lo, hi] + [pl.BlockSpec(memory_space=pl.ANY)] * len(after),
        out_specs=(lo, lo, pl.BlockSpec(memory_space=pltpu.VMEM)),
        compiler_params=params(12),
        cost_estimate=pl.CostEstimate(flops=m * rows * 32, bytes_accessed=m * rows * 200, transcendentals=0),
        name="halve%d_%d" % (m, rows),
    )(keep, keep, got, got, *after)


def plus_body(a, b, *refs):
    out, token = refs[-2:]
    out[...] = add(a[...], b[...])
    token[...] = jnp.zeros_like(token)


def plus(a, b, after=(), twist=0):
    rows = a.shape[1]
    one = pl.BlockSpec((1, rows, 128), lambda g: (g, 0, 0))
    other = pl.BlockSpec((1, rows, 128), lambda g: (jnp.bitwise_xor(g, twist), 0, 0))
    return pl.pallas_call(
        plus_body,
        grid=(a.shape[0],),
        out_shape=(jax.ShapeDtypeStruct(a.shape, BF), TOKEN),
        in_specs=[one, other] + [pl.BlockSpec(memory_space=pl.ANY)] * len(after),
        out_specs=(one, pl.BlockSpec(memory_space=pltpu.VMEM)),
        compiler_params=params(8),
        cost_estimate=pl.CostEstimate(flops=a.shape[0] * rows * 32, bytes_accessed=a.shape[0] * rows * 100, transcendentals=0),
        name="plus%d_%d" % (a.shape[0], rows),
    )(a, b, *after)


def join_body(n, *refs):
    out, token = refs[-2:]
    row = 0
    for a, b in zip(refs[0:2 * n:2], refs[1:2 * n:2]):
        m, rows = a.shape[:2]
        out[:m, row:row + rows] = a[...]
        out[m:, row:row + rows] = b[...]
        row += rows
    token[...] = jnp.zeros_like(token)


def join(parts, after=()):
    m, rows = parts[0].shape[0], sum(p.shape[1] for p in parts[::2])
    vmem = pl.BlockSpec(memory_space=pltpu.VMEM)
    return pl.pallas_call(
        functools.partial(join_body, len(parts) // 2),
        out_shape=(jax.ShapeDtypeStruct((2 * m, rows, 128), BF), TOKEN),
        in_specs=[vmem] * len(parts) + [pl.BlockSpec(memory_space=pl.ANY)] * len(after),
        out_specs=(vmem, vmem),
        compiler_params=params(12),
        cost_estimate=pl.CostEstimate(flops=1000, bytes_accessed=m * rows * 100, transcendentals=0),
        name="join%d_%d" % (m, rows),
    )(*parts, *after)


def pos_rows(v):
    left = lax.broadcasted_iota(jnp.int32, (1, 128), 1) < SUB
    out = []
    for r in range(v.shape[0]):
        high, rest = v[r:r + 1] >> 5, v[r:r + 1] & 31
        out.append(jnp.where(left, high, pltpu.roll(rest, SUB, 1)))
        out.append(jnp.where(left, pltpu.roll(high, SUB, 1), rest))
    return jnp.concatenate(out, axis=0)


def pick_body(with_pos, me, short, long, *refs):
    outs, sem = refs[-5:-1], refs[-1]
    waits = []
    for k in range(4):
        j = jnp.bitwise_xor(me[4], k)
        to = outs[k].at[pl.ds(0, 256)]

        @pl.when(j == 0)
        def _():
            pltpu.make_async_copy(short, to, sem.at[k]).start()

        @pl.when(j > 0)
        def _():
            pltpu.make_async_copy(long.at[jnp.maximum(j - 1, 0)], to, sem.at[k]).start()

        waits.append(pltpu.make_async_copy(short, to, sem.at[k]))
    if with_pos:
        of_short = pos_rows(jnp.concatenate([refs[0][...], refs[0][...] + 512], axis=0))
        of_long = pos_rows(refs[1][...])
        for k in range(4):
            tile = jnp.where(jnp.bitwise_xor(me[4], k) == 0, of_short, of_long).astype(F32)
            tile = jnp.concatenate([tile, jnp.zeros((12, 128), F32)], axis=0).astype(BF)
            outs[k][256:272, :] = jnp.concatenate([tile, jnp.zeros((16, D - 128), BF)], axis=1)
    for c in waits:
        c.wait()


def pick(me, short, long, pos=(), after=()):
    anyspec = pl.BlockSpec(memory_space=pl.ANY)
    vmem = pl.BlockSpec(memory_space=pltpu.VMEM)
    out = jax.ShapeDtypeStruct((272 if pos else 256, D), BF)
    return pl.pallas_call(
        functools.partial(pick_body, bool(pos)),
        out_shape=(out,) * 4,
        in_specs=[pl.BlockSpec(memory_space=pltpu.SMEM)] + [anyspec] * 2 + [vmem] * len(pos) + [anyspec] * len(after),
        out_specs=(vmem,) * 4,
        scratch_shapes=[pltpu.SemaphoreType.DMA((4,))],
        compiler_params=params(56 if pos else 8),
        cost_estimate=pl.CostEstimate(flops=1000, bytes_accessed=500_000, transcendentals=0),
        name="pick%d" % len(pos),
    )(me, short.reshape(256, D), long, *pos, *after)


class Sums:
    def __init__(self, n_dp, n_seq):
        self.n_dp, self.n_seq = n_dp, n_seq
        self.core = pairs(n_dp, 1)
        self.first = [(a, a ^ (4 if a & 1 else 2)) for a in range(n_dp)]
        self.second = [(a, a ^ (2 if a & 1 else 4)) for a in range(n_dp)]

    def dp(self, v, perm):
        return lax.ppermute(v, "dp", perm)

    def seq(self, v, bit):
        return lax.ppermute(v, "seq", pairs(self.n_seq, bit))

    def rest(self, v):
        bit = 8
        while bit < self.n_dp:
            v = add(v, self.dp(v, pairs(self.n_dp, bit)))
            bit *= 2
        return v


def tie(a, b):
    return lax.optimization_barrier((a, b))


def per_device(n_dp, n_seq, x_short, order_short, x_long, order_long, w_query, w_key, w_value, w_out, b_out, alphas,
               w_up, b_up, w_down, b_down, cot_short, cot_long):
    i = lax.axis_index("seq")
    d = lax.axis_index("dp")
    n_dev = n_dp * n_seq

    def give_back(mine):
        return [mine[0]] + [lax.ppermute(mine[k], "seq", pairs(n_seq, k)) for k in range(1, n_seq)]

    def home(got):
        def chunk(j):
            k = jnp.bitwise_xor(i, j)
            v = jnp.where(k < 2, jnp.where(k == 0, got[0], got[1]), jnp.where(k == 2, got[2], got[3]))
            return v
        return chunk(0).reshape(2, 128, D), jnp.stack([chunk(j) for j in range(1, n_seq)])

    def give_back(mine):
        return [mine[0]] + [lax.ppermute(mine[k], "seq", pairs(n_seq, k)) for k in range(1, n_seq)]

    c, bx, by = d & 1, (d >> 1) & 1, (d >> 2) & 1
    z = (i & 1) * 2 + (i >> 1)
    x_first, y_first = bx * 8 + by * 4 + z, by * 8 + bx * 4 + z
    at = jnp.arange(8)
    me = jnp.where(at == 0, c, jnp.where(at == 1, jnp.where(c == 0, x_first, y_first), jnp.where(
        at == 2, jnp.where(c == 0, y_first, x_first), jnp.where(at == 3, d * n_seq + i, i)))).astype(jnp.int32)
    xs = give_back(pick(me, x_short, x_long, (order_short.reshape(1, 128), order_long.reshape(2, 128))))
    w = jnp.concatenate([w_query, w_key, w_value], axis=1)
    wt = w.T
    cots = give_back(pick(me, cot_short, cot_long, (), tuple(xs[1:])))
    rows, q, k, v_rows, qt, kt, ot, att, lse, mask, dst, bias = attn_fwd(me, xs, w, wt)
    o0, o1, o2, o3, gm, do, dott, inner, keep, send = ffn(
        n_dev, dst, me, alphas, cots, rows, att, ot, w_out, b_out.reshape(1, D), w_up, b_up.reshape(1, FF),
        w_down, b_down.reshape(1, D))
    net = Sums(n_dp, n_seq)

    def bwd(hp, after):
        *g, token = attn_bwd(hp, bias, mask, q, k, v_rows, qt, kt, do, dott, lse, inner, after)
        return g, token

    got = net.dp(send, net.core)
    outs = give_back((o0, o1, o2, o3))
    g0, token = bwd(0, lse)
    lo, hi, token = halve(keep, got, (token,))
    got = net.dp(hi, net.first)
    g1, token = bwd(1, token)
    g2, token = bwd(2, token)
    g3, token = bwd(3, token)
    lo, hi, token = halve(lo, got, (token,))
    got = net.dp(hi, net.second)
    d_rows, keep2, send2, token = attn_dense(
        dst, me, rows, gm, w, g0 + g1 + g2 + g3, (token,))
    out_short, out_long = home(outs)
    lo, hi, token = halve(lo, got, (token, out_short, out_long))
    got = net.seq(hi, 1)
    got2 = net.dp(send2, net.core)
    lo, hi, token = halve(lo, got, (token,))
    got = net.seq(hi, 2)
    lo2, hi2, token = halve(keep2, got2, (token,))
    got2 = net.dp(hi2, net.first)
    v, token = plus(lo, got, (token,))
    v = net.rest(v)
    got = net.seq(v, 2)
    lo2, hi2, token = halve(lo2, got2, (token,))
    got2 = net.dp(hi2, net.second)
    v, token = join((v, got), (token,))
    got = net.seq(v, 1)
    u, token = plus(lo2, got2, (token,))
    got2 = net.seq(u, 1)
    v, token = join((v, got), (token,))
    got = net.dp(v, net.second)
    u, token = plus(u, got2, (token,), 2)
    got2 = net.seq(u, 2)
    v, token = join((v, got), (token,))
    far = net.dp(v, net.first)
    near = net.dp(v, net.core)
    first, token = finish(DENSE, 0, me, (v, near), (), (token,))
    u, token = plus(u, got2, (token,), 1)
    u = net.rest(u)
    d_rows, _ = tie(d_rows, token)
    dxs = lax.all_to_all(d_rows, "seq", 0, 0)
    got2 = net.dp(u, net.second)
    u, token = join((u, got2), (token,))
    far2 = net.dp(u, net.first)
    near2 = net.dp(u, net.core)
    (g_up, g_down, g_out, small), token = finish(DENSE, 1, me, (far, net.dp(far, net.core)), first, (token,))
    first2, token = finish(QKV, 0, me, (u, near2), (), (token,))
    (g_query, g_key, g_value), token = finish(QKV, 1, me, (far2, net.dp(far2, net.core)), first2, (token,))
    dxs, _ = tie(dxs, token)
    dx_short, dx_long = dxs[0].reshape(2, 128, D).astype(F32), dxs[1:].astype(F32)
    small = small.reshape(SLOTS, 8, 128)
    flat = small[:24, 0].reshape(-1)
    nr = (n_dev + 127) // 128
    g_alphas = jnp.sum(small[:6 * nr, 1].reshape(2, 3 * nr * 128), axis=1)
    return (out_short, out_long, dx_short, dx_long, g_query, g_key, g_value, g_out, flat[2560:3072], g_alphas,
            g_up, flat[:2048], g_down, flat[2048:2560])


def solution(mesh):
    split = P("dp", "seq", None)
    whole = P()
    return jax.shard_map(
        functools.partial(per_device, mesh.shape["dp"], mesh.shape["seq"]),
        mesh=mesh,
        in_specs=(split, P("seq"), split, P("seq")) + (whole,) * 10 + (split, split),
        out_specs=(split,) * 4 + (whole,) * 10,
        check_vma=False,
    )
```

```python
import functools
import jax
import jax.numpy as jnp
from jax import lax
from jax.sharding import PartitionSpec as P
from jax.experimental import pallas as pl
from jax.experimental.pallas import tpu as pltpu

BF = jnp.bfloat16
F32 = jnp.float32
HEADS = 8
HD = 64
D = 512
FF = 2048
T = 1024
SUB = 64
NSUB = T // SUB
QB = 256
NQ = T // QB


def dot(a, b, ca=1, cb=0):
    return lax.dot_general(a, b, (((ca,), (cb,)), ((), ())), preferred_element_type=F32)


def params(mb):
    return pltpu.CompilerParams(vmem_limit_bytes=mb * 1024 * 1024)


def one_head(pair, h):
    row = lax.broadcasted_iota(jnp.int32, pair.shape, 0)
    return jnp.where((row >= HD) == (h == 1), pair, jnp.zeros_like(pair))


def attn_fwd_body(me, c0, c1, c2, c3, w, wt, xs, q_out, k_out, v_out, qt, kt, ot, att, lse, mask, dst, bias,
                  vt):
    chunks = (c0, c1, c2, c3)
    is_short = me[4] == 0
    runs = jnp.concatenate([chunks[n][256:272, :128].astype(F32)[:4] for n in range(4)], axis=0)
    spot = runs[:, :SUB] * 32.0 + runs[:, SUB:2 * SUB]
    lowest = jnp.min(spot, axis=1, keepdims=True).astype(jnp.int32)
    odd = lax.broadcasted_iota(jnp.int32, (NSUB, 1), 0) & 1
    to = jnp.where(is_short, lowest >> 6, 2 * (lowest >> 7) + odd)
    for s in range(NSUB):
        dst[s] = jnp.max(to[s:s + 1, :])
    gather_rows(dst, chunks, xs)
    for a in range(NQ):
        for b in range(NQ):
            bias[a * NQ + b] = jnp.where(is_short, 0.0 if a // 2 == b // 2 else -1e30, 0.0)
    place = (lax.broadcasted_iota(jnp.int32, (NSUB, NSUB), 1) == to).astype(BF)
    by_run = 32.0 * dot(place, runs[:, :SUB].astype(BF), 0, 0) + dot(place, runs[:, SUB:2 * SUB].astype(BF), 0, 0)
    for a in range(NQ):
        row = jnp.concatenate([by_run[4 * a + b:4 * a + b + 1, :] for b in range(4)], axis=1)
        across = jnp.broadcast_to(row, (QB, QB))
        mask[a] = jnp.where(across.T <= across, 0.0, -1e30)
    for i in range(NQ):
        rows = pl.ds(i * QB, QB)
        x = xs[rows, :]
        qkv = dot(x, w[...]).astype(BF)
        qkvt = dot(wt[...], x, 1, 1).astype(BF)
        q_out[rows, :] = qkv[:, :D] * BF(0.125)
        k_out[rows, :] = qkv[:, D:2 * D]
        v_out[rows, :] = qkv[:, 2 * D:]
        qt[:, rows] = qkvt[:D] * BF(0.125)
        kt[:, rows] = qkvt[D:2 * D]
        vt[:, rows] = qkvt[2 * D:]

    def pair(hp, carry):
        wide = pl.ds(pl.multiple_of(hp * 2 * HD, 2 * HD), 2 * HD)
        for i in range(NQ):
            cols = pl.ds(i * QB, QB)
            both = qt[wide, cols]
            for h in range(2):
                hr = pl.ds(pl.multiple_of(hp * 2 * HD + h * HD, HD), HD)
                q = one_head(both, h)
                tiles, tops = [], []
                for j in range(i + 1):
                    s = dot(k_out[pl.ds(j * QB, QB), wide], q)
                    if j == i:
                        s = s + mask[i]
                        tops.append(jnp.max(s, axis=0, keepdims=True))
                    else:
                        tops.append(jnp.max(s, axis=0, keepdims=True) + bias[i * NQ + j])
                    tiles.append(s)
                m = functools.reduce(jnp.maximum, tops)
                total, o = None, None
                for j in range(i + 1):
                    mj = m if j == i else m - bias[i * NQ + j]
                    e = jnp.exp(tiles[j] - mj)
                    t = jnp.sum(e, axis=0, keepdims=True)
                    total = t if total is None else total + t
                    p = dot(vt[hr, pl.ds(j * QB, QB)], e.astype(BF))
                    o = p if o is None else o + p
                o = o * (1.0 / total)
                ot[hr, cols] = o
                lse[hp * 2 + h, :, cols] = m + jnp.log(total)
        return carry

    lax.fori_loop(0, HEADS // 2, pair, 0)
    for i in range(NQ):
        rows = pl.ds(i * QB, QB)
        att[rows, :] = ot[:, rows].astype(BF).T


def attn_fwd(me, chunks, w, wt):
    s = jax.ShapeDtypeStruct
    rows, cols = s((T, D), BF), s((D, T), BF)
    smem = pl.BlockSpec(memory_space=pltpu.SMEM)
    vmem = pl.BlockSpec(memory_space=pltpu.VMEM)
    return pl.pallas_call(
        attn_fwd_body,
        out_shape=(rows, rows, rows, rows, cols, cols, s((D, T), F32), rows, s((HEADS, 1, T), F32),
                   s((NQ, QB, QB), F32), s((NSUB,), jnp.int32), s((NQ * NQ,), F32)),
        in_specs=[smem] + [vmem] * 6,
        out_specs=(vmem,) * 10 + (smem,) * 2,
        scratch_shapes=[pltpu.VMEM((D, T), BF)],
        compiler_params=params(24),
        cost_estimate=pl.CostEstimate(flops=1500000000, bytes_accessed=2000000, transcendentals=0),
        name="attn_fwd",
    )(me, *chunks, w, wt)


FB = 512
NF = FF // FB
SLOTS = 32
HALF = SLOTS // 2
TOKEN = jax.ShapeDtypeStruct((8, 128), F32)
R1 = 592
R2 = 192


def scatter_rows(dst, rows_ref, put):
    for s in range(NSUB):
        at = pl.ds(pl.multiple_of(dst[s] * SUB, SUB), SUB)
        put(s // 4, (s % 4) * SUB, rows_ref[at, :])


def gather_rows(dst, ins, rows_ref):
    for s in range(NSUB):
        to = pl.ds(pl.multiple_of(dst[s] * SUB, SUB), SUB)
        rows_ref[to, :] = ins[s // 4][(s % 4) * SUB:(s % 4 + 1) * SUB, :]


def put_slot(me, keep, send, s, row, rows, val):
    at = pl.ds(row, rows)

    @pl.when(s // HALF == me[0])
    def _():
        keep[jnp.bitwise_xor(s % HALF, me[1]), at, :] = val

    @pl.when(s // HALF != me[0])
    def _():
        send[jnp.bitwise_xor(s % HALF, me[2]), at, :] = val


def top_rows(first, second):
    rows = lax.broadcasted_iota(jnp.int32, (16, 128), 0)
    first, second = jnp.broadcast_to(first, (16, 128)), jnp.broadcast_to(second, (16, 128))
    return jnp.where(rows == 0, first, jnp.where(rows == 1, second, 0.0)).astype(BF)


def ffn_body(n_dev, dst, me, alphas, c0, c1, c2, c3, xs, att, ot, w_out, b_out, w_up, b_up, w_down, b_down,
             o0, o1, o2, o3, gm, do_out, dott, inner, keep, send,
             cot, branch, middle, low, low_t, gfeed, gfeed_t, feed, bias_up):
    f = pl.program_id(0)
    a0, a1 = alphas[0], alphas[1]

    @pl.when(f == 0)
    def _():
        gather_rows(dst, (c0, c1, c2, c3), cot)
        br = dot(att[...], w_out[...]) + b_out[...]
        branch[...] = br
        mid = xs[...].astype(F32) + a0 * br
        middle[...] = mid
        low[...] = mid.astype(BF)
        low_t[...] = low[...].T
        g = cot[...].astype(F32)
        gfeed[...] = (a1 * g).astype(BF)
        gfeed_t[...] = gfeed[...].T
        gm[...] = g
        feed[...] = jnp.broadcast_to(b_down[...], feed.shape)

    hidden = dot(low[...], w_up[...]) + b_up[...]
    c = 0.7978845608028654
    h2 = hidden * hidden
    th = jnp.tanh(hidden * (c + (c * 0.044715) * h2))
    half = 0.5 + 0.5 * th
    active = (hidden * half).astype(BF)
    slope = half + (0.5 * hidden) * (1.0 - th * th) * (c + (3 * c * 0.044715) * h2)
    feed[...] += dot(active, w_down[...])
    grad_h = (dot(gfeed[...], w_down[...], 1, 1) * slope).astype(BF)
    bu = jnp.sum(grad_h.astype(F32), axis=0, keepdims=True)
    gd = dot(gfeed_t[...], active).astype(BF).T
    gu = dot(low_t[...], grad_h)
    gm[...] += dot(grad_h, w_up[...], 1, 1)
    for b in range(FB // 128):
        for a in range(2):
            put_slot(me, keep, send, (FB // 64) * f + 2 * b + a, 0, 256,
                     gu[a * 256:(a + 1) * 256, b * 128:(b + 1) * 128].astype(BF))
        bias_up[(FB // 128) * f + b] = bu[:, b * 128:(b + 1) * 128]
    for lb in range(4):
        for a in range(FB // 256):
            put_slot(me, keep, send, lb * 8 + (FB // 256) * f + a, 256, 256,
                     gd[a * 256:(a + 1) * 256, lb * 128:(lb + 1) * 128])

    @pl.when(f == NF - 1)
    def _():
        low[...] = (middle[...] + a1 * feed[...]).astype(BF)
        def put(k, row, val):
            (o0, o1, o2, o3)[k][row:row + SUB, :] = val

        scatter_rows(dst, low, put)
        g = cot[...].astype(F32)
        s1 = jnp.sum(feed[...] * g)
        s0 = jnp.sum(branch[...] * gm[...])
        bd = jnp.sum(gfeed[...].astype(F32), axis=0, keepdims=True)
        gb = (a0 * gm[...]).astype(BF)
        bo = jnp.sum(gb.astype(F32), axis=0, keepdims=True)
        go = dot(att[...], gb, 0, 0)
        do_out[...] = dot(gb, w_out[...], 1, 1).astype(BF)
        dt = dot(w_out[...], gb, 1, 1).astype(BF)
        dott[...] = dt
        for h in range(HEADS):
            hs = slice(h * HD, (h + 1) * HD)
            inner[h] = jnp.sum(ot[hs, :] * dt[hs, :].astype(F32), axis=0, keepdims=True)
        nr = (n_dev + 127) // 128
        row = lax.broadcasted_iota(jnp.int32, (SLOTS, 128), 0)
        lane = lax.broadcasted_iota(jnp.int32, (SLOTS, 128), 1)
        mine_row, mine_lane = me[3] // 128, me[3] % 128
        small = jnp.zeros((SLOTS, 128), F32)
        for k, total in enumerate((s0, s1)):
            rest = jnp.full((SLOTS, 128), total, F32)
            for t in range(3):
                piece = rest.astype(BF).astype(F32)
                rest = rest - piece
                here = (row == (3 * k + t) * nr + mine_row) & (lane == mine_lane)
                small = jnp.where(here, piece, small)
        zero = jnp.zeros((1, 128), F32)
        for s in range(SLOTS):
            lb, a = s // 8, s % 8
            put_slot(me, keep, send, s, 512, 64, go[a * 64:a * 64 + 64, lb * 128:(lb + 1) * 128].astype(BF))
            if s < 16:
                first = bias_up[s]
            elif s < 24:
                first = (bd if s < 20 else bo)[:, (s % 4) * 128:(s % 4 + 1) * 128]
            else:
                first = zero
            put_slot(me, keep, send, s, 576, 16, top_rows(first, small[s:s + 1]))


def ffn(n_dev, dst, me, alphas, cots, xs, att, ot, w_out, b_out, w_up, b_up, w_down, b_down):
    s = jax.ShapeDtypeStruct
    anyspec = pl.BlockSpec(memory_space=pl.ANY)
    smem = pl.BlockSpec(memory_space=pltpu.SMEM)
    vmem = pl.BlockSpec(memory_space=pltpu.VMEM)
    v = pltpu.VMEM
    half = s((HALF, R1, 128), BF)
    return pl.pallas_call(
        functools.partial(ffn_body, n_dev),
        grid=(NF,),
        out_shape=(s((256, D), BF),) * 4 + (s((T, D), F32), s((T, D), BF), s((D, T), BF),
                                            s((HEADS, 1, T), F32), half, half),
        in_specs=[smem, smem, smem] + [vmem] * 9 + [
            pl.BlockSpec((D, FB), lambda f: (0, f)),
            pl.BlockSpec((1, FB), lambda f: (0, f)),
            pl.BlockSpec((FB, D), lambda f: (f, 0)),
            vmem,
        ],
        out_specs=(vmem,) * 10,
        scratch_shapes=[v((T, D), BF), v((T, D), F32), v((T, D), F32), v((T, D), BF), v((D, T), BF), v((T, D), BF),
                        v((D, T), BF), v((T, D), F32), v((16, 1, 128), F32)],
        compiler_params=params(40),
        cost_estimate=pl.CostEstimate(flops=1875000000, bytes_accessed=2500000, transcendentals=0),
        name="ffn",
    )(dst, me, alphas, *cots, xs, att, ot, w_out, b_out, w_up, b_up, w_down, b_down)


def attn_bwd_body(bias, mask, q_in, k_in, v_in, qt, kt, do_in, dott, lse, inner, after, dqo, dko, dvo, token):
    token[...] = jnp.zeros_like(token)
    dq2, dk2, dv2 = [], [], []
    for h in range(2):
        hr = pl.ds(h * HD, HD)
        dk = [None] * NQ
        dv = [None] * NQ
        dq = []
        for i in range(NQ):
            cols = pl.ds(i * QB, QB)
            q, do = one_head(qt[:, cols], h), one_head(dott[:, cols], h)
            q_rows, do_rows = q_in[cols, :], do_in[cols, :]
            ls, inn = lse[h, :, cols], inner[h, :, cols]
            acc = None
            for j in range(i + 1):
                rows = pl.ds(j * QB, QB)
                s = dot(k_in[rows, :], q)
                if j == i:
                    p = jnp.exp(s + mask[i] - ls)
                else:
                    p = jnp.exp(s - (ls - bias[i * NQ + j]))
                dp = dot(v_in[rows, :], do)
                ds = (p * (dp - inn)).astype(BF)
                gv = dot(p.astype(BF), do_rows)
                gk = dot(ds, q_rows)
                gq = dot(kt[hr, rows], ds)
                dv[j] = gv if dv[j] is None else dv[j] + gv
                dk[j] = gk if dk[j] is None else dk[j] + gk
                acc = gq if acc is None else acc + gq
            dq.append(acc * 0.125)
        dq2.append(dq)
        dk2.append(dk)
        dv2.append(dv)
    right = lax.broadcasted_iota(jnp.int32, (QB, 2 * HD), 1) >= HD
    for i in range(NQ):
        rows = pl.ds(i * QB, QB)
        dqo[rows, :] = jnp.concatenate([dq2[0][i], dq2[1][i]], axis=0).astype(BF).T
        dko[rows, :] = jnp.where(right, dk2[1][i], dk2[0][i]).astype(BF)
        dvo[rows, :] = jnp.where(right, dv2[1][i], dv2[0][i]).astype(BF)


def attn_bwd(hp, bias, mask, q, k, v, qt, kt, do, dott, lse, inner, after):
    s = jax.ShapeDtypeStruct
    smem = pl.BlockSpec(memory_space=pltpu.SMEM)
    vmem = pl.BlockSpec(memory_space=pltpu.VMEM)
    tall = pl.BlockSpec((T, 2 * HD), lambda g: (0, hp))
    wide = pl.BlockSpec((2 * HD, T), lambda g: (hp, 0))
    line = pl.BlockSpec((2, 1, T), lambda g: (hp, 0, 0))
    return pl.pallas_call(
        attn_bwd_body,
        grid=(1,),
        out_shape=(s((T, 2 * HD), BF),) * 3 + (TOKEN,),
        in_specs=[smem, vmem, tall, tall, tall, wide, wide, tall, wide, line, line, pl.BlockSpec(memory_space=pl.ANY)],
        out_specs=(vmem,) * 4,
        compiler_params=params(20),
        cost_estimate=pl.CostEstimate(flops=625000000, bytes_accessed=625000, transcendentals=0),
        name="attn_bwd%d" % hp,
    )(bias, mask, q, k, v, qt, kt, do, dott, lse, inner, after)


def attn_dense_body(dst, me, xs, gm, w, *refs):
    parts, (d_out, keep, send, token, dx_rows) = refs[:12], refs[-5:]
    token[...] = jnp.zeros_like(token)
    grads = [jnp.concatenate([parts[3 * hp + n][...] for hp in range(4)], axis=1) for n in range(3)]
    dx = gm[...]
    for n in range(3):
        dx = dx + dot(grads[n], w[:, n * D:(n + 1) * D], 1, 1)
    dx_rows[...] = dx.astype(BF)

    def put(k, row, val):
        d_out[jnp.bitwise_xor(me[4], k), row:row + SUB, :] = val

    scatter_rows(dst, dx_rows, put)
    for n in range(3):
        g = dot(xs[...], grads[n], 0, 0)
        for s in range(SLOTS):
            lb, a = s // 8, s % 8
            put_slot(me, keep, send, s, n * 64, 64, g[a * 64:a * 64 + 64, lb * 128:(lb + 1) * 128].astype(BF))


def attn_dense(dst, me, xs, gm, w, grads, after=()):
    s = jax.ShapeDtypeStruct
    anyspec = pl.BlockSpec(memory_space=pl.ANY)
    smem = pl.BlockSpec(memory_space=pltpu.SMEM)
    vmem = pl.BlockSpec(memory_space=pltpu.VMEM)
    half = s((HALF, R2, 128), BF)
    return pl.pallas_call(
        attn_dense_body,
        out_shape=(s((4, 256, D), BF), half, half, TOKEN),
        in_specs=[smem] * 2 + [vmem] * 15 + [anyspec] * len(after),
        out_specs=(vmem,) * 4,
        scratch_shapes=[pltpu.VMEM((T, D), BF)],
        compiler_params=params(32),
        cost_estimate=pl.CostEstimate(flops=400000000, bytes_accessed=1125000, transcendentals=0),
        name="attn_dense",
    )(dst, me, xs, gm, w, *grads, *after)


DENSE = ((2, 256, 0), (8, 256, 256), (8, 64, 512))
QKV = ((8, 64, 0), (8, 64, 64), (8, 64, 128))
SMALL = 576


def finish_body(pieces, small, part, me, own, other, *refs):
    n = len(pieces)
    n_out = n + small
    stages, sem = refs[-n_out - 1:-1], refs[-1]
    outs, token = refs[-2 * n_out - 2:-n_out - 2], refs[-n_out - 2]
    token[...] = jnp.zeros_like(token)

    def each(slot, depth):
        copies = []
        for which, src in enumerate((own, other)):
            core = me[0] if which == 0 else 1 - me[0]
            s = core * HALF + jnp.bitwise_xor(slot + 8 * part, me[1 + which])
            for k, (tall, rows, row) in enumerate(pieces):
                stages[k][depth, which] = src[slot, row:row + rows, :].astype(F32)
                to = outs[k].at[pl.ds(pl.multiple_of((s % tall) * rows, rows), rows),
                                pl.ds(pl.multiple_of((s // tall) * 128, 128), 128)]
                copies.append(pltpu.make_async_copy(stages[k].at[depth, which], to, sem.at[depth, which, k]))
            if small:
                stages[n][depth, which] = src[slot, SMALL:SMALL + 16, :].astype(F32)[:8]
                to = outs[n].at[pl.ds(pl.multiple_of(s * 8, 8), 8)]
                copies.append(pltpu.make_async_copy(stages[n].at[depth, which], to, sem.at[depth, which, n]))
        return copies

    pending = [None] * 4
    for slot in range(8):
        depth = slot % 4
        if pending[depth] is not None:
            for c in pending[depth]:
                c.wait()
        pending[depth] = each(slot, depth)
        for c in pending[depth]:
            c.start()
    for group in pending:
        for c in group:
            c.wait()


def finish(pieces, part, me, got, before, after):
    anyspec = pl.BlockSpec(memory_space=pl.ANY)
    vmem = pl.BlockSpec(memory_space=pltpu.VMEM)
    s = jax.ShapeDtypeStruct
    square = s((D, D), F32)
    small = pieces is DENSE
    shapes = (s((D, FF), F32), s((FF, D), F32), square, s((SLOTS * 8, 128), F32)) if small else (square,) * 3
    n = len(shapes)
    *out, token = pl.pallas_call(
        functools.partial(finish_body, pieces, int(small), part),
        out_shape=shapes + (TOKEN,),
        in_specs=[pl.BlockSpec(memory_space=pltpu.SMEM)] + [vmem] * 2 + [anyspec] * (len(before) + len(after)),
        out_specs=(anyspec,) * n + (vmem,),
        scratch_shapes=[pltpu.VMEM((4, 2, rows, 128), F32) for _, rows, _ in pieces]
        + [pltpu.VMEM((4, 2, 8, 128), F32)] * small + [pltpu.SemaphoreType.DMA((4, 2, n))],
        input_output_aliases={3 + k: k for k in range(len(before))},
        compiler_params=params(20),
        cost_estimate=pl.CostEstimate(flops=1_000_000, bytes_accessed=4_000_000, transcendentals=0),
        name="finish%d_%d" % (n, part),
    )(me, *got, *before, *after)
    return tuple(out), token


def pairs(size, bit):
    return [(a, a ^ bit) for a in range(size)]


def add(a, b):
    return (a.astype(F32) + b.astype(F32)).astype(BF)


def halve_body(keep_lo, keep_hi, got_lo, got_hi, *refs):
    lo, hi, token = refs[-3:]
    lo[...] = add(keep_lo[...], got_lo[...])
    hi[...] = add(keep_hi[...], got_hi[...])
    token[...] = jnp.zeros_like(token)


def halve(keep, got, after=()):
    m, rows = keep.shape[0] // 2, keep.shape[1]
    steps = max(1, m // 2)
    lo = pl.BlockSpec((m // steps, rows, 128), lambda g: (g, 0, 0))
    hi = pl.BlockSpec((m // steps, rows, 128), lambda g: (g + steps, 0, 0))
    half = jax.ShapeDtypeStruct((m, rows, 128), BF)
    return pl.pallas_call(
        halve_body,
        grid=(steps,),
        out_shape=(half, half, TOKEN),
        in_specs=[lo, hi, lo, hi] + [pl.BlockSpec(memory_space=pl.ANY)] * len(after),
        out_specs=(lo, lo, pl.BlockSpec(memory_space=pltpu.VMEM)),
        compiler_params=params(12),
        cost_estimate=pl.CostEstimate(flops=m * rows * 32, bytes_accessed=m * rows * 200, transcendentals=0),
        name="halve%d_%d" % (m, rows),
    )(keep, keep, got, got, *after)


def plus_body(a, b, *refs):
    out, token = refs[-2:]
    out[...] = add(a[...], b[...])
    token[...] = jnp.zeros_like(token)


def plus(a, b, after=(), twist=0):
    rows = a.shape[1]
    one = pl.BlockSpec((1, rows, 128), lambda g: (g, 0, 0))
    other = pl.BlockSpec((1, rows, 128), lambda g: (jnp.bitwise_xor(g, twist), 0, 0))
    return pl.pallas_call(
        plus_body,
        grid=(a.shape[0],),
        out_shape=(jax.ShapeDtypeStruct(a.shape, BF), TOKEN),
        in_specs=[one, other] + [pl.BlockSpec(memory_space=pl.ANY)] * len(after),
        out_specs=(one, pl.BlockSpec(memory_space=pltpu.VMEM)),
        compiler_params=params(8),
        cost_estimate=pl.CostEstimate(flops=a.shape[0] * rows * 32, bytes_accessed=a.shape[0] * rows * 100, transcendentals=0),
        name="plus%d_%d" % (a.shape[0], rows),
    )(a, b, *after)


def join_body(n, *refs):
    out, token = refs[-2:]
    row = 0
    for a, b in zip(refs[0:2 * n:2], refs[1:2 * n:2]):
        m, rows = a.shape[:2]
        out[:m, row:row + rows] = a[...]
        out[m:, row:row + rows] = b[...]
        row += rows
    token[...] = jnp.zeros_like(token)


def join(parts, after=()):
    m, rows = parts[0].shape[0], sum(p.shape[1] for p in parts[::2])
    vmem = pl.BlockSpec(memory_space=pltpu.VMEM)
    return pl.pallas_call(
        functools.partial(join_body, len(parts) // 2),
        out_shape=(jax.ShapeDtypeStruct((2 * m, rows, 128), BF), TOKEN),
        in_specs=[vmem] * len(parts) + [pl.BlockSpec(memory_space=pl.ANY)] * len(after),
        out_specs=(vmem, vmem),
        compiler_params=params(12),
        cost_estimate=pl.CostEstimate(flops=1000, bytes_accessed=m * rows * 100, transcendentals=0),
        name="join%d_%d" % (m, rows),
    )(*parts, *after)


def pos_rows(v):
    left = lax.broadcasted_iota(jnp.int32, (1, 128), 1) < SUB
    out = []
    for r in range(v.shape[0]):
        high, rest = v[r:r + 1] >> 5, v[r:r + 1] & 31
        out.append(jnp.where(left, high, pltpu.roll(rest, SUB, 1)))
        out.append(jnp.where(left, pltpu.roll(high, SUB, 1), rest))
    return jnp.concatenate(out, axis=0)


def pick_body(with_pos, me, short, long, *refs):
    outs, sem = refs[-5:-1], refs[-1]
    waits = []
    for k in range(4):
        j = jnp.bitwise_xor(me[4], k)
        to = outs[k].at[pl.ds(0, 256)]

        @pl.when(j == 0)
        def _():
            pltpu.make_async_copy(short, to, sem.at[k]).start()

        @pl.when(j > 0)
        def _():
            pltpu.make_async_copy(long.at[jnp.maximum(j - 1, 0)], to, sem.at[k]).start()

        waits.append(pltpu.make_async_copy(short, to, sem.at[k]))
    if with_pos:
        of_short = pos_rows(jnp.concatenate([refs[0][...], refs[0][...] + 512], axis=0))
        of_long = pos_rows(refs[1][...])
        for k in range(4):
            tile = jnp.where(jnp.bitwise_xor(me[4], k) == 0, of_short, of_long).astype(F32)
            tile = jnp.concatenate([tile, jnp.zeros((12, 128), F32)], axis=0).astype(BF)
            outs[k][256:272, :] = jnp.concatenate([tile, jnp.zeros((16, D - 128), BF)], axis=1)
    for c in waits:
        c.wait()


def pick(me, short, long, pos=(), after=()):
    anyspec = pl.BlockSpec(memory_space=pl.ANY)
    vmem = pl.BlockSpec(memory_space=pltpu.VMEM)
    out = jax.ShapeDtypeStruct((272 if pos else 256, D), BF)
    return pl.pallas_call(
        functools.partial(pick_body, bool(pos)),
        out_shape=(out,) * 4,
        in_specs=[pl.BlockSpec(memory_space=pltpu.SMEM)] + [anyspec] * 2 + [vmem] * len(pos) + [anyspec] * len(after),
        out_specs=(vmem,) * 4,
        scratch_shapes=[pltpu.SemaphoreType.DMA((4,))],
        compiler_params=params(56 if pos else 8),
        cost_estimate=pl.CostEstimate(flops=1000, bytes_accessed=500_000, transcendentals=0),
        name="pick%d" % len(pos),
    )(me, short.reshape(256, D), long, *pos, *after)


def widen_body(first, other, after, short, long):
    @pl.when(pl.program_id(0) == 0)
    def _():
        short[...] = first[0].astype(F32)

    long[...] = other[...].astype(F32)


def widen(rows, after):
    s = jax.ShapeDtypeStruct
    return pl.pallas_call(
        widen_body,
        grid=(3,),
        out_shape=(s((256, D), F32), s((3, 256, D), F32)),
        in_specs=[pl.BlockSpec((1, 256, D), lambda g: (0, 0, 0)), pl.BlockSpec((1, 256, D), lambda g: (g + 1, 0, 0)),
                  pl.BlockSpec(memory_space=pl.ANY)],
        out_specs=(pl.BlockSpec((256, D), lambda g: (0, 0)), pl.BlockSpec((1, 256, D), lambda g: (g, 0, 0))),
        compiler_params=params(8),
        cost_estimate=pl.CostEstimate(flops=1000, bytes_accessed=400_000, transcendentals=0),
        name="widen",
    )(rows, rows, after)


class Sums:
    def __init__(self, n_dp, n_seq):
        self.n_dp, self.n_seq = n_dp, n_seq
        self.core = pairs(n_dp, 1)
        self.first = [(a, a ^ (4 if a & 1 else 2)) for a in range(n_dp)]
        self.second = [(a, a ^ (2 if a & 1 else 4)) for a in range(n_dp)]

    def dp(self, v, perm):
        return lax.ppermute(v, "dp", perm)

    def seq(self, v, bit):
        return lax.ppermute(v, "seq", pairs(self.n_seq, bit))

    def rest(self, v):
        bit = 8
        while bit < self.n_dp:
            v = add(v, self.dp(v, pairs(self.n_dp, bit)))
            bit *= 2
        return v


def tie(a, b):
    return lax.optimization_barrier((a, b))


def per_device(n_dp, n_seq, x_short, order_short, x_long, order_long, w_query, w_key, w_value, w_out, b_out, alphas,
               w_up, b_up, w_down, b_down, cot_short, cot_long):
    i = lax.axis_index("seq")
    d = lax.axis_index("dp")
    n_dev = n_dp * n_seq

    def give_back(mine):
        return [mine[0]] + [lax.ppermute(mine[k], "seq", pairs(n_seq, k)) for k in range(1, n_seq)]

    def home(got):
        def chunk(j):
            k = jnp.bitwise_xor(i, j)
            v = jnp.where(k < 2, jnp.where(k == 0, got[0], got[1]), jnp.where(k == 2, got[2], got[3]))
            return v
        return chunk(0).reshape(2, 128, D), jnp.stack([chunk(j) for j in range(1, n_seq)])

    def give_back(mine):
        return [mine[0]] + [lax.ppermute(mine[k], "seq", pairs(n_seq, k)) for k in range(1, n_seq)]

    c, bx, by = d & 1, (d >> 1) & 1, (d >> 2) & 1
    z = (i & 1) * 2 + (i >> 1)
    x_first, y_first = bx * 8 + by * 4 + z, by * 8 + bx * 4 + z
    at = jnp.arange(8)
    me = jnp.where(at == 0, c, jnp.where(at == 1, jnp.where(c == 0, x_first, y_first), jnp.where(
        at == 2, jnp.where(c == 0, y_first, x_first), jnp.where(at == 3, d * n_seq + i, i)))).astype(jnp.int32)
    xs = give_back(pick(me, x_short, x_long, (order_short.reshape(1, 128), order_long.reshape(2, 128))))
    w = jnp.concatenate([w_query, w_key, w_value], axis=1)
    wt = w.T
    cots = give_back(pick(me, cot_short, cot_long, (), (wt,) + tuple(xs[1:])))
    rows, q, k, v_rows, qt, kt, ot, att, lse, mask, dst, bias = attn_fwd(me, xs, w, wt)
    o0, o1, o2, o3, gm, do, dott, inner, keep, send = ffn(
        n_dev, dst, me, alphas, cots, rows, att, ot, w_out, b_out.reshape(1, D), w_up, b_up.reshape(1, FF),
        w_down, b_down.reshape(1, D))
    net = Sums(n_dp, n_seq)

    def bwd(hp, after):
        *g, token = attn_bwd(hp, bias, mask, q, k, v_rows, qt, kt, do, dott, lse, inner, after)
        return g, token

    got = net.dp(send, net.core)
    outs = give_back((o0, o1, o2, o3))
    g0, token = bwd(0, lse)
    lo, hi, token = halve(keep, got, (token,))
    got = net.dp(hi, net.first)
    g1, token = bwd(1, token)
    g2, token = bwd(2, token)
    g3, token = bwd(3, token)
    lo, hi, token = halve(lo, got, (token,))
    got = net.dp(hi, net.second)
    d_rows, keep2, send2, token = attn_dense(
        dst, me, rows, gm, w, g0 + g1 + g2 + g3, (token,))
    out_short, out_long = home(outs)
    lo, hi, token = halve(lo, got, (token, out_short, out_long))
    got = net.seq(hi, 1)
    got2 = net.dp(send2, net.core)
    lo, hi, token = halve(lo, got, (token,))
    got = net.seq(hi, 2)
    lo2, hi2, token = halve(keep2, got2, (token,))
    got2 = net.dp(hi2, net.first)
    v, token = plus(lo, got, (token,))
    v = net.rest(v)
    got = net.seq(v, 2)
    lo2, hi2, token = halve(lo2, got2, (token,))
    got2 = net.dp(hi2, net.second)
    v, token = join((v, got), (token,))
    got = net.seq(v, 1)
    u, token = plus(lo2, got2, (token,))
    got2 = net.seq(u, 1)
    v, token = join((v, got), (token,))
    got = net.dp(v, net.second)
    u, token = plus(u, got2, (token,), 2)
    got2 = net.seq(u, 2)
    v, token = join((v, got), (token,))
    far = net.dp(v, net.first)
    near = net.dp(v, net.core)
    first, token = finish(DENSE, 0, me, (v, near), (), (token,))
    u, token = plus(u, got2, (token,), 1)
    u = net.rest(u)
    d_rows, _ = tie(d_rows, token)
    dxs = lax.all_to_all(d_rows, "seq", 0, 0)
    got2 = net.dp(u, net.second)
    u, token = join((u, got2), (token,))
    far2 = net.dp(u, net.first)
    near2 = net.dp(u, net.core)
    (g_up, g_down, g_out, small), token = finish(DENSE, 1, me, (far, net.dp(far, net.core)), first, (token,))
    first2, token = finish(QKV, 0, me, (u, near2), (), (token,))
    (g_query, g_key, g_value), token = finish(QKV, 1, me, (far2, net.dp(far2, net.core)), first2, (token,))
    dx_short, dx_long = widen(dxs, token)
    dx_short = dx_short.reshape(2, 128, D)
    small = small.reshape(SLOTS, 8, 128)
    flat = small[:24, 0].reshape(-1)
    nr = (n_dev + 127) // 128
    g_alphas = jnp.sum(small[:6 * nr, 1].reshape(2, 3 * nr * 128), axis=1)
    return (out_short, out_long, dx_short, dx_long, g_query, g_key, g_value, g_out, flat[2560:3072], g_alphas,
            g_up, flat[:2048], g_down, flat[2048:2560])


def solution(mesh):
    split = P("dp", "seq", None)
    whole = P()
    return jax.shard_map(
        functools.partial(per_device, mesh.shape["dp"], mesh.shape["seq"]),
        mesh=mesh,
        in_specs=(split, P("seq"), split, P("seq")) + (whole,) * 10 + (split, split),
        out_specs=(split,) * 4 + (whole,) * 10,
        check_vma=False,
    )
```

```python
import functools
import jax
import jax.numpy as jnp
from jax import lax
from jax.sharding import PartitionSpec as P
from jax.experimental import pallas as pl
from jax.experimental.pallas import tpu as pltpu

BF = jnp.bfloat16
F32 = jnp.float32
HEADS = 8
HD = 64
D = 512
FF = 2048
T = 1024
SUB = 64
NSUB = T // SUB
QB = 256
NQ = T // QB


def dot(a, b, ca=1, cb=0):
    return lax.dot_general(a, b, (((ca,), (cb,)), ((), ())), preferred_element_type=F32)


def params(mb):
    return pltpu.CompilerParams(vmem_limit_bytes=mb * 1024 * 1024)


def one_head(pair, h):
    row = lax.broadcasted_iota(jnp.int32, pair.shape, 0)
    return jnp.where((row >= HD) == (h == 1), pair, jnp.zeros_like(pair))


def attn_fwd_body(me, c0, c1, c2, c3, w, wt, xs, q_out, k_out, v_out, qt, kt, ot, att, lse, mask, dst, bias,
                  vt):
    chunks = (c0, c1, c2, c3)
    is_short = me[4] == 0
    runs = jnp.concatenate([chunks[n][256:272, :128].astype(F32)[:4] for n in range(4)], axis=0)
    spot = runs[:, :SUB] * 32.0 + runs[:, SUB:2 * SUB]
    lowest = jnp.min(spot, axis=1, keepdims=True).astype(jnp.int32)
    odd = lax.broadcasted_iota(jnp.int32, (NSUB, 1), 0) & 1
    to = jnp.where(is_short, lowest >> 6, 2 * (lowest >> 7) + odd)
    for s in range(NSUB):
        dst[s] = jnp.max(to[s:s + 1, :])
    gather_rows(dst, chunks, xs)
    for a in range(NQ):
        for b in range(NQ):
            bias[a * NQ + b] = jnp.where(is_short, 0.0 if a // 2 == b // 2 else -1e30, 0.0)
    place = (lax.broadcasted_iota(jnp.int32, (NSUB, NSUB), 1) == to).astype(BF)
    by_run = 32.0 * dot(place, runs[:, :SUB].astype(BF), 0, 0) + dot(place, runs[:, SUB:2 * SUB].astype(BF), 0, 0)
    for a in range(NQ):
        row = jnp.concatenate([by_run[4 * a + b:4 * a + b + 1, :] for b in range(4)], axis=1)
        across = jnp.broadcast_to(row, (QB, QB))
        mask[a] = jnp.where(across.T <= across, 0.0, -1e30)
    for i in range(NQ):
        rows = pl.ds(i * QB, QB)
        x = xs[rows, :]
        qkv = dot(x, w[...]).astype(BF)
        qkvt = dot(wt[...], x, 1, 1).astype(BF)
        q_out[rows, :] = qkv[:, :D] * BF(0.125)
        k_out[rows, :] = qkv[:, D:2 * D]
        v_out[rows, :] = qkv[:, 2 * D:]
        qt[:, rows] = qkvt[:D] * BF(0.125)
        kt[:, rows] = qkvt[D:2 * D]
        vt[:, rows] = qkvt[2 * D:]

    def pair(hp, carry):
        wide = pl.ds(pl.multiple_of(hp * 2 * HD, 2 * HD), 2 * HD)
        for i in range(NQ):
            cols = pl.ds(i * QB, QB)
            both = qt[wide, cols]
            for h in range(2):
                hr = pl.ds(pl.multiple_of(hp * 2 * HD + h * HD, HD), HD)
                q = one_head(both, h)
                tiles, tops = [], []
                for j in range(i + 1):
                    s = dot(k_out[pl.ds(j * QB, QB), wide], q)
                    if j == i:
                        s = s + mask[i]
                        tops.append(jnp.max(s, axis=0, keepdims=True))
                    else:
                        tops.append(jnp.max(s, axis=0, keepdims=True) + bias[i * NQ + j])
                    tiles.append(s)
                m = functools.reduce(jnp.maximum, tops)
                total, o = None, None
                for j in range(i + 1):
                    mj = m if j == i else m - bias[i * NQ + j]
                    e = jnp.exp(tiles[j] - mj)
                    t = jnp.sum(e, axis=0, keepdims=True)
                    total = t if total is None else total + t
                    p = dot(vt[hr, pl.ds(j * QB, QB)], e.astype(BF))
                    o = p if o is None else o + p
                o = o * (1.0 / total)
                ot[hr, cols] = o
                lse[hp * 2 + h, :, cols] = m + jnp.log(total)
        return carry

    lax.fori_loop(0, HEADS // 2, pair, 0)
    for i in range(NQ):
        rows = pl.ds(i * QB, QB)
        att[rows, :] = ot[:, rows].astype(BF).T


def attn_fwd(me, chunks, w, wt):
    s = jax.ShapeDtypeStruct
    rows, cols = s((T, D), BF), s((D, T), BF)
    smem = pl.BlockSpec(memory_space=pltpu.SMEM)
    vmem = pl.BlockSpec(memory_space=pltpu.VMEM)
    return pl.pallas_call(
        attn_fwd_body,
        out_shape=(rows, rows, rows, rows, cols, cols, s((D, T), F32), rows, s((HEADS, 1, T), F32),
                   s((NQ, QB, QB), F32), s((NSUB,), jnp.int32), s((NQ * NQ,), F32)),
        in_specs=[smem] + [vmem] * 6,
        out_specs=(vmem,) * 10 + (smem,) * 2,
        scratch_shapes=[pltpu.VMEM((D, T), BF)],
        compiler_params=params(24),
        cost_estimate=pl.CostEstimate(flops=1500000000, bytes_accessed=2000000, transcendentals=0),
        name="attn_fwd",
    )(me, *chunks, w, wt)


FB = 512
NF = FF // FB
SLOTS = 32
HALF = SLOTS // 2
TOKEN = jax.ShapeDtypeStruct((8, 128), F32)
R1 = 592
R2 = 192


def scatter_rows(dst, rows_ref, put):
    for s in range(NSUB):
        at = pl.ds(pl.multiple_of(dst[s] * SUB, SUB), SUB)
        put(s // 4, (s % 4) * SUB, rows_ref[at, :])


def gather_rows(dst, ins, rows_ref):
    for s in range(NSUB):
        to = pl.ds(pl.multiple_of(dst[s] * SUB, SUB), SUB)
        rows_ref[to, :] = ins[s // 4][(s % 4) * SUB:(s % 4 + 1) * SUB, :]


def put_slot(me, keep, send, s, row, rows, val):
    at = pl.ds(row, rows)

    @pl.when(s // HALF == me[0])
    def _():
        keep[jnp.bitwise_xor(s % HALF, me[1]), at, :] = val

    @pl.when(s // HALF != me[0])
    def _():
        send[jnp.bitwise_xor(s % HALF, me[2]), at, :] = val


def top_rows(first, second):
    rows = lax.broadcasted_iota(jnp.int32, (16, 128), 0)
    first, second = jnp.broadcast_to(first, (16, 128)), jnp.broadcast_to(second, (16, 128))
    return jnp.where(rows == 0, first, jnp.where(rows == 1, second, 0.0)).astype(BF)


def ffn_body(n_dev, dst, me, alphas, c0, c1, c2, c3, xs, att, ot, w_out, b_out, w_up, b_up, w_down, b_down,
             o0, o1, o2, o3, gm, do_out, dott, inner, keep, send,
             cot, branch, middle, low, low_t, gfeed, gfeed_t, feed, bias_up):
    f = pl.program_id(0)
    a0, a1 = alphas[0], alphas[1]

    @pl.when(f == 0)
    def _():
        gather_rows(dst, (c0, c1, c2, c3), cot)
        br = dot(att[...], w_out[...]) + b_out[...]
        branch[...] = br
        mid = xs[...].astype(F32) + a0 * br
        middle[...] = mid
        low[...] = mid.astype(BF)
        low_t[...] = low[...].T
        g = cot[...].astype(F32)
        gfeed[...] = (a1 * g).astype(BF)
        gfeed_t[...] = gfeed[...].T
        gm[...] = g
        feed[...] = jnp.broadcast_to(b_down[...], feed.shape)

    hidden = dot(low[...], w_up[...]) + b_up[...]
    c = 0.7978845608028654
    h2 = hidden * hidden
    th = jnp.tanh(hidden * (c + (c * 0.044715) * h2))
    half = 0.5 + 0.5 * th
    active = (hidden * half).astype(BF)
    slope = half + (0.5 * hidden) * (1.0 - th * th) * (c + (3 * c * 0.044715) * h2)
    feed[...] += dot(active, w_down[...])
    grad_h = (dot(gfeed[...], w_down[...], 1, 1) * slope).astype(BF)
    bu = jnp.sum(grad_h.astype(F32), axis=0, keepdims=True)
    gd = dot(gfeed_t[...], active).astype(BF).T
    gu = dot(low_t[...], grad_h)
    gm[...] += dot(grad_h, w_up[...], 1, 1)
    for b in range(FB // 128):
        for a in range(2):
            put_slot(me, keep, send, (FB // 64) * f + 2 * b + a, 0, 256,
                     gu[a * 256:(a + 1) * 256, b * 128:(b + 1) * 128].astype(BF))
        bias_up[(FB // 128) * f + b] = bu[:, b * 128:(b + 1) * 128]
    for lb in range(4):
        for a in range(FB // 256):
            put_slot(me, keep, send, lb * 8 + (FB // 256) * f + a, 256, 256,
                     gd[a * 256:(a + 1) * 256, lb * 128:(lb + 1) * 128])

    @pl.when(f == NF - 1)
    def _():
        low[...] = (middle[...] + a1 * feed[...]).astype(BF)
        def put(k, row, val):
            (o0, o1, o2, o3)[k][row:row + SUB, :] = val

        scatter_rows(dst, low, put)
        g = cot[...].astype(F32)
        s1 = jnp.sum(feed[...] * g)
        s0 = jnp.sum(branch[...] * gm[...])
        bd = jnp.sum(gfeed[...].astype(F32), axis=0, keepdims=True)
        gb = (a0 * gm[...]).astype(BF)
        bo = jnp.sum(gb.astype(F32), axis=0, keepdims=True)
        go = dot(att[...], gb, 0, 0)
        do_out[...] = dot(gb, w_out[...], 1, 1).astype(BF)
        dt = dot(w_out[...], gb, 1, 1).astype(BF)
        dott[...] = dt
        for h in range(HEADS):
            hs = slice(h * HD, (h + 1) * HD)
            inner[h] = jnp.sum(ot[hs, :] * dt[hs, :].astype(F32), axis=0, keepdims=True)
        nr = (n_dev + 127) // 128
        row = lax.broadcasted_iota(jnp.int32, (SLOTS, 128), 0)
        lane = lax.broadcasted_iota(jnp.int32, (SLOTS, 128), 1)
        mine_row, mine_lane = me[3] // 128, me[3] % 128
        small = jnp.zeros((SLOTS, 128), F32)
        for k, total in enumerate((s0, s1)):
            rest = jnp.full((SLOTS, 128), total, F32)
            for t in range(3):
                piece = rest.astype(BF).astype(F32)
                rest = rest - piece
                here = (row == (3 * k + t) * nr + mine_row) & (lane == mine_lane)
                small = jnp.where(here, piece, small)
        zero = jnp.zeros((1, 128), F32)
        for s in range(SLOTS):
            lb, a = s // 8, s % 8
            put_slot(me, keep, send, s, 512, 64, go[a * 64:a * 64 + 64, lb * 128:(lb + 1) * 128].astype(BF))
            if s < 16:
                first = bias_up[s]
            elif s < 24:
                first = (bd if s < 20 else bo)[:, (s % 4) * 128:(s % 4 + 1) * 128]
            else:
                first = zero
            put_slot(me, keep, send, s, 576, 16, top_rows(first, small[s:s + 1]))


def ffn(n_dev, dst, me, alphas, cots, xs, att, ot, w_out, b_out, w_up, b_up, w_down, b_down):
    s = jax.ShapeDtypeStruct
    anyspec = pl.BlockSpec(memory_space=pl.ANY)
    smem = pl.BlockSpec(memory_space=pltpu.SMEM)
    vmem = pl.BlockSpec(memory_space=pltpu.VMEM)
    v = pltpu.VMEM
    half = s((HALF, R1, 128), BF)
    return pl.pallas_call(
        functools.partial(ffn_body, n_dev),
        grid=(NF,),
        out_shape=(s((256, D), BF),) * 4 + (s((T, D), F32), s((T, D), BF), s((D, T), BF),
                                            s((HEADS, 1, T), F32), half, half),
        in_specs=[smem, smem, smem] + [vmem] * 9 + [
            pl.BlockSpec((D, FB), lambda f: (0, f)),
            pl.BlockSpec((1, FB), lambda f: (0, f)),
            pl.BlockSpec((FB, D), lambda f: (f, 0)),
            vmem,
        ],
        out_specs=(vmem,) * 10,
        scratch_shapes=[v((T, D), BF), v((T, D), F32), v((T, D), F32), v((T, D), BF), v((D, T), BF), v((T, D), BF),
                        v((D, T), BF), v((T, D), F32), v((16, 1, 128), F32)],
        compiler_params=params(40),
        cost_estimate=pl.CostEstimate(flops=1875000000, bytes_accessed=2500000, transcendentals=0),
        name="ffn",
    )(dst, me, alphas, *cots, xs, att, ot, w_out, b_out, w_up, b_up, w_down, b_down)


def attn_bwd_body(bias, mask, q_in, k_in, v_in, qt, kt, do_in, dott, lse, inner, after, dqo, dko, dvo, token):
    token[...] = jnp.zeros_like(token)
    dq2, dk2, dv2 = [], [], []
    for h in range(2):
        hr = pl.ds(h * HD, HD)
        dk = [None] * NQ
        dv = [None] * NQ
        dq = []
        for i in range(NQ):
            cols = pl.ds(i * QB, QB)
            q, do = one_head(qt[:, cols], h), one_head(dott[:, cols], h)
            q_rows, do_rows = q_in[cols, :], do_in[cols, :]
            ls, inn = lse[h, :, cols], inner[h, :, cols]
            acc = None
            for j in range(i + 1):
                rows = pl.ds(j * QB, QB)
                s = dot(k_in[rows, :], q)
                if j == i:
                    p = jnp.exp(s + mask[i] - ls)
                else:
                    p = jnp.exp(s - (ls - bias[i * NQ + j]))
                dp = dot(v_in[rows, :], do)
                ds = (p * (dp - inn)).astype(BF)
                gv = dot(p.astype(BF), do_rows)
                gk = dot(ds, q_rows)
                gq = dot(kt[hr, rows], ds)
                dv[j] = gv if dv[j] is None else dv[j] + gv
                dk[j] = gk if dk[j] is None else dk[j] + gk
                acc = gq if acc is None else acc + gq
            dq.append(acc * 0.125)
        dq2.append(dq)
        dk2.append(dk)
        dv2.append(dv)
    right = lax.broadcasted_iota(jnp.int32, (QB, 2 * HD), 1) >= HD
    for i in range(NQ):
        rows = pl.ds(i * QB, QB)
        dqo[rows, :] = jnp.concatenate([dq2[0][i], dq2[1][i]], axis=0).astype(BF).T
        dko[rows, :] = jnp.where(right, dk2[1][i], dk2[0][i]).astype(BF)
        dvo[rows, :] = jnp.where(right, dv2[1][i], dv2[0][i]).astype(BF)


def attn_bwd(hp, bias, mask, q, k, v, qt, kt, do, dott, lse, inner, after):
    s = jax.ShapeDtypeStruct
    smem = pl.BlockSpec(memory_space=pltpu.SMEM)
    vmem = pl.BlockSpec(memory_space=pltpu.VMEM)
    tall = pl.BlockSpec((T, 2 * HD), lambda g: (0, hp))
    wide = pl.BlockSpec((2 * HD, T), lambda g: (hp, 0))
    line = pl.BlockSpec((2, 1, T), lambda g: (hp, 0, 0))
    return pl.pallas_call(
        attn_bwd_body,
        grid=(1,),
        out_shape=(s((T, 2 * HD), BF),) * 3 + (TOKEN,),
        in_specs=[smem, vmem, tall, tall, tall, wide, wide, tall, wide, line, line, pl.BlockSpec(memory_space=pl.ANY)],
        out_specs=(vmem,) * 4,
        compiler_params=params(20),
        cost_estimate=pl.CostEstimate(flops=625000000, bytes_accessed=625000, transcendentals=0),
        name="attn_bwd%d" % hp,
    )(bias, mask, q, k, v, qt, kt, do, dott, lse, inner, after)


def attn_dense_body(dst, me, xs, gm, w, *refs):
    parts, (d_out, keep, send, token, dx_rows) = refs[:12], refs[-5:]
    token[...] = jnp.zeros_like(token)
    grads = [jnp.concatenate([parts[3 * hp + n][...] for hp in range(4)], axis=1) for n in range(3)]
    dx = gm[...]
    for n in range(3):
        dx = dx + dot(grads[n], w[:, n * D:(n + 1) * D], 1, 1)
    dx_rows[...] = dx.astype(BF)

    def put(k, row, val):
        d_out[jnp.bitwise_xor(me[4], k), row:row + SUB, :] = val

    scatter_rows(dst, dx_rows, put)
    for n in range(3):
        g = dot(xs[...], grads[n], 0, 0)
        for s in range(SLOTS):
            lb, a = s // 8, s % 8
            put_slot(me, keep, send, s, n * 64, 64, g[a * 64:a * 64 + 64, lb * 128:(lb + 1) * 128].astype(BF))


def attn_dense(dst, me, xs, gm, w, grads, after=()):
    s = jax.ShapeDtypeStruct
    anyspec = pl.BlockSpec(memory_space=pl.ANY)
    smem = pl.BlockSpec(memory_space=pltpu.SMEM)
    vmem = pl.BlockSpec(memory_space=pltpu.VMEM)
    half = s((HALF, R2, 128), BF)
    return pl.pallas_call(
        attn_dense_body,
        out_shape=(s((4, 256, D), BF), half, half, TOKEN),
        in_specs=[smem] * 2 + [vmem] * 15 + [anyspec] * len(after),
        out_specs=(vmem,) * 4,
        scratch_shapes=[pltpu.VMEM((T, D), BF)],
        compiler_params=params(32),
        cost_estimate=pl.CostEstimate(flops=400000000, bytes_accessed=1125000, transcendentals=0),
        name="attn_dense",
    )(dst, me, xs, gm, w, *grads, *after)


DENSE = ((2, 256, 0), (8, 256, 256), (8, 64, 512))
QKV = ((8, 64, 0), (8, 64, 64), (8, 64, 128))
SMALL = 576


def finish_body(pieces, small, part, me, own, other, *refs):
    n = len(pieces)
    n_out = n + small
    stages, sem = refs[-n_out - 1:-1], refs[-1]
    outs, token = refs[-2 * n_out - 2:-n_out - 2], refs[-n_out - 2]
    token[...] = jnp.zeros_like(token)

    def each(slot, depth):
        copies = []
        for which, src in enumerate((own, other)):
            core = me[0] if which == 0 else 1 - me[0]
            s = core * HALF + jnp.bitwise_xor(slot + 8 * part, me[1 + which])
            for k, (tall, rows, row) in enumerate(pieces):
                stages[k][depth, which] = src[slot, row:row + rows, :].astype(F32)
                to = outs[k].at[pl.ds(pl.multiple_of((s % tall) * rows, rows), rows),
                                pl.ds(pl.multiple_of((s // tall) * 128, 128), 128)]
                copies.append(pltpu.make_async_copy(stages[k].at[depth, which], to, sem.at[depth, which, k]))
            if small:
                stages[n][depth, which] = src[slot, SMALL:SMALL + 16, :].astype(F32)[:8]
                to = outs[n].at[pl.ds(pl.multiple_of(s * 8, 8), 8)]
                copies.append(pltpu.make_async_copy(stages[n].at[depth, which], to, sem.at[depth, which, n]))
        return copies

    pending = [None] * 4
    for slot in range(8):
        depth = slot % 4
        if pending[depth] is not None:
            for c in pending[depth]:
                c.wait()
        pending[depth] = each(slot, depth)
        for c in pending[depth]:
            c.start()
    for group in pending:
        for c in group:
            c.wait()


def finish(pieces, part, me, got, before, after):
    anyspec = pl.BlockSpec(memory_space=pl.ANY)
    vmem = pl.BlockSpec(memory_space=pltpu.VMEM)
    s = jax.ShapeDtypeStruct
    square = s((D, D), F32)
    small = pieces is DENSE
    shapes = (s((D, FF), F32), s((FF, D), F32), square, s((SLOTS * 8, 128), F32)) if small else (square,) * 3
    n = len(shapes)
    *out, token = pl.pallas_call(
        functools.partial(finish_body, pieces, int(small), part),
        out_shape=shapes + (TOKEN,),
        in_specs=[pl.BlockSpec(memory_space=pltpu.SMEM)] + [vmem] * 2 + [anyspec] * (len(before) + len(after)),
        out_specs=(anyspec,) * n + (vmem,),
        scratch_shapes=[pltpu.VMEM((4, 2, rows, 128), F32) for _, rows, _ in pieces]
        + [pltpu.VMEM((4, 2, 8, 128), F32)] * small + [pltpu.SemaphoreType.DMA((4, 2, n))],
        input_output_aliases={3 + k: k for k in range(len(before))},
        compiler_params=params(20),
        cost_estimate=pl.CostEstimate(flops=1_000_000, bytes_accessed=4_000_000, transcendentals=0),
        name="finish%d_%d" % (n, part),
    )(me, *got, *before, *after)
    return tuple(out), token


def pairs(size, bit):
    return [(a, a ^ bit) for a in range(size)]


def add(a, b):
    return (a.astype(F32) + b.astype(F32)).astype(BF)


def halve_body(keep_lo, keep_hi, got_lo, got_hi, *refs):
    lo, hi, token = refs[-3:]
    lo[...] = add(keep_lo[...], got_lo[...])
    hi[...] = add(keep_hi[...], got_hi[...])
    token[...] = jnp.zeros_like(token)


def halve(keep, got, after=()):
    m, rows = keep.shape[0] // 2, keep.shape[1]
    steps = max(1, m // 2)
    lo = pl.BlockSpec((m // steps, rows, 128), lambda g: (g, 0, 0))
    hi = pl.BlockSpec((m // steps, rows, 128), lambda g: (g + steps, 0, 0))
    half = jax.ShapeDtypeStruct((m, rows, 128), BF)
    return pl.pallas_call(
        halve_body,
        grid=(steps,),
        out_shape=(half, half, TOKEN),
        in_specs=[lo, hi, lo, hi] + [pl.BlockSpec(memory_space=pl.ANY)] * len(after),
        out_specs=(lo, lo, pl.BlockSpec(memory_space=pltpu.VMEM)),
        compiler_params=params(12),
        cost_estimate=pl.CostEstimate(flops=m * rows * 32, bytes_accessed=m * rows * 200, transcendentals=0),
        name="halve%d_%d" % (m, rows),
    )(keep, keep, got, got, *after)


def plus_body(a, b, *refs):
    out, token = refs[-2:]
    out[...] = add(a[...], b[...])
    token[...] = jnp.zeros_like(token)


def plus(a, b, after=(), twist=0):
    rows = a.shape[1]
    one = pl.BlockSpec((1, rows, 128), lambda g: (g, 0, 0))
    other = pl.BlockSpec((1, rows, 128), lambda g: (jnp.bitwise_xor(g, twist), 0, 0))
    return pl.pallas_call(
        plus_body,
        grid=(a.shape[0],),
        out_shape=(jax.ShapeDtypeStruct(a.shape, BF), TOKEN),
        in_specs=[one, other] + [pl.BlockSpec(memory_space=pl.ANY)] * len(after),
        out_specs=(one, pl.BlockSpec(memory_space=pltpu.VMEM)),
        compiler_params=params(8),
        cost_estimate=pl.CostEstimate(flops=a.shape[0] * rows * 32, bytes_accessed=a.shape[0] * rows * 100, transcendentals=0),
        name="plus%d_%d" % (a.shape[0], rows),
    )(a, b, *after)


def join_body(n, *refs):
    out, token = refs[-2:]
    row = 0
    for a, b in zip(refs[0:2 * n:2], refs[1:2 * n:2]):
        m, rows = a.shape[:2]
        out[:m, row:row + rows] = a[...]
        out[m:, row:row + rows] = b[...]
        row += rows
    token[...] = jnp.zeros_like(token)


def join(parts, after=()):
    m, rows = parts[0].shape[0], sum(p.shape[1] for p in parts[::2])
    vmem = pl.BlockSpec(memory_space=pltpu.VMEM)
    return pl.pallas_call(
        functools.partial(join_body, len(parts) // 2),
        out_shape=(jax.ShapeDtypeStruct((2 * m, rows, 128), BF), TOKEN),
        in_specs=[vmem] * len(parts) + [pl.BlockSpec(memory_space=pl.ANY)] * len(after),
        out_specs=(vmem, vmem),
        compiler_params=params(12),
        cost_estimate=pl.CostEstimate(flops=1000, bytes_accessed=m * rows * 100, transcendentals=0),
        name="join%d_%d" % (m, rows),
    )(*parts, *after)


def pos_rows(v):
    left = lax.broadcasted_iota(jnp.int32, (1, 128), 1) < SUB
    out = []
    for r in range(v.shape[0]):
        high, rest = v[r:r + 1] >> 5, v[r:r + 1] & 31
        out.append(jnp.where(left, high, pltpu.roll(rest, SUB, 1)))
        out.append(jnp.where(left, pltpu.roll(high, SUB, 1), rest))
    return jnp.concatenate(out, axis=0)


def pick_body(with_pos, me, short, long, *refs):
    outs, sem = refs[-5:-1], refs[-1]
    waits = []
    for k in range(4):
        j = jnp.bitwise_xor(me[4], k)
        to = outs[k].at[pl.ds(0, 256)]

        @pl.when(j == 0)
        def _():
            pltpu.make_async_copy(short, to, sem.at[k]).start()

        @pl.when(j > 0)
        def _():
            pltpu.make_async_copy(long.at[jnp.maximum(j - 1, 0)], to, sem.at[k]).start()

        waits.append(pltpu.make_async_copy(short, to, sem.at[k]))
    if with_pos:
        of_short = pos_rows(jnp.concatenate([refs[0][...], refs[0][...] + 512], axis=0))
        of_long = pos_rows(refs[1][...])
        for k in range(4):
            tile = jnp.where(jnp.bitwise_xor(me[4], k) == 0, of_short, of_long).astype(F32)
            tile = jnp.concatenate([tile, jnp.zeros((12, 128), F32)], axis=0).astype(BF)
            outs[k][256:272, :] = jnp.concatenate([tile, jnp.zeros((16, D - 128), BF)], axis=1)
    for c in waits:
        c.wait()


def pick(me, short, long, pos=(), after=()):
    anyspec = pl.BlockSpec(memory_space=pl.ANY)
    vmem = pl.BlockSpec(memory_space=pltpu.VMEM)
    out = jax.ShapeDtypeStruct((272 if pos else 256, D), BF)
    return pl.pallas_call(
        functools.partial(pick_body, bool(pos)),
        out_shape=(out,) * 4,
        in_specs=[pl.BlockSpec(memory_space=pltpu.SMEM)] + [anyspec] * 2 + [vmem] * len(pos) + [anyspec] * len(after),
        out_specs=(vmem,) * 4,
        scratch_shapes=[pltpu.SemaphoreType.DMA((4,))],
        compiler_params=params(56 if pos else 8),
        cost_estimate=pl.CostEstimate(flops=1000, bytes_accessed=500_000, transcendentals=0),
        name="pick%d" % len(pos),
    )(me, short.reshape(256, D), long, *pos, *after)


def widen_body(first, other, after, short, long):
    @pl.when(pl.program_id(0) == 0)
    def _():
        short[...] = first[0].astype(F32)

    long[...] = other[...].astype(F32)


def widen(rows, after):
    s = jax.ShapeDtypeStruct
    return pl.pallas_call(
        widen_body,
        grid=(3,),
        out_shape=(s((256, D), F32), s((3, 256, D), F32)),
        in_specs=[pl.BlockSpec((1, 256, D), lambda g: (0, 0, 0)), pl.BlockSpec((1, 256, D), lambda g: (g + 1, 0, 0)),
                  pl.BlockSpec(memory_space=pl.ANY)],
        out_specs=(pl.BlockSpec((256, D), lambda g: (0, 0)), pl.BlockSpec((1, 256, D), lambda g: (g, 0, 0))),
        compiler_params=params(8),
        cost_estimate=pl.CostEstimate(flops=1000, bytes_accessed=400_000, transcendentals=0),
        name="widen",
    )(rows, rows, after)


class Sums:
    def __init__(self, n_dp, n_seq):
        self.n_dp, self.n_seq = n_dp, n_seq
        self.core = pairs(n_dp, 1)
        self.first = [(a, a ^ (4 if a & 1 else 2)) for a in range(n_dp)]
        self.second = [(a, a ^ (2 if a & 1 else 4)) for a in range(n_dp)]

    def dp(self, v, perm):
        return lax.ppermute(v, "dp", perm)

    def seq(self, v, bit):
        return lax.ppermute(v, "seq", pairs(self.n_seq, bit))

    def rest(self, v):
        bit = 8
        while bit < self.n_dp:
            v = add(v, self.dp(v, pairs(self.n_dp, bit)))
            bit *= 2
        return v


def tie(a, b):
    return lax.optimization_barrier((a, b))


def per_device(n_dp, n_seq, x_short, order_short, x_long, order_long, w_query, w_key, w_value, w_out, b_out, alphas,
               w_up, b_up, w_down, b_down, cot_short, cot_long):
    i = lax.axis_index("seq")
    d = lax.axis_index("dp")
    n_dev = n_dp * n_seq

    def give_back(mine):
        return [mine[0]] + [lax.ppermute(mine[k], "seq", pairs(n_seq, k)) for k in range(1, n_seq)]

    def home(got):
        def chunk(j):
            k = jnp.bitwise_xor(i, j)
            v = jnp.where(k < 2, jnp.where(k == 0, got[0], got[1]), jnp.where(k == 2, got[2], got[3]))
            return v
        return chunk(0).reshape(2, 128, D), jnp.stack([chunk(j) for j in range(1, n_seq)])

    def give_back(mine):
        return [mine[0]] + [lax.ppermute(mine[k], "seq", pairs(n_seq, k)) for k in range(1, n_seq)]

    c, bx, by = d & 1, (d >> 1) & 1, (d >> 2) & 1
    z = (i & 1) * 2 + (i >> 1)
    x_first, y_first = bx * 8 + by * 4 + z, by * 8 + bx * 4 + z
    at = jnp.arange(8)
    me = jnp.where(at == 0, c, jnp.where(at == 1, jnp.where(c == 0, x_first, y_first), jnp.where(
        at == 2, jnp.where(c == 0, y_first, x_first), jnp.where(at == 3, d * n_seq + i, i)))).astype(jnp.int32)
    xs = give_back(pick(me, x_short, x_long, (order_short.reshape(1, 128), order_long.reshape(2, 128))))
    w = jnp.concatenate([w_query, w_key, w_value], axis=1)
    wt = w.T
    cots = give_back(pick(me, cot_short, cot_long, (), tuple(xs[1:])))
    rows, q, k, v_rows, qt, kt, ot, att, lse, mask, dst, bias = attn_fwd(me, xs, w, wt)
    o0, o1, o2, o3, gm, do, dott, inner, keep, send = ffn(
        n_dev, dst, me, alphas, cots, rows, att, ot, w_out, b_out.reshape(1, D), w_up, b_up.reshape(1, FF),
        w_down, b_down.reshape(1, D))
    net = Sums(n_dp, n_seq)

    def bwd(hp, after):
        *g, token = attn_bwd(hp, bias, mask, q, k, v_rows, qt, kt, do, dott, lse, inner, after)
        return g, token

    got = net.dp(send, net.core)
    outs = give_back((o0, o1, o2, o3))
    g0, token = bwd(0, lse)
    lo, hi, token = halve(keep, got, (token,))
    got = net.dp(hi, net.first)
    g1, token = bwd(1, token)
    g2, token = bwd(2, token)
    g3, token = bwd(3, token)
    lo, hi, token = halve(lo, got, (token,))
    got = net.dp(hi, net.second)
    d_rows, keep2, send2, token = attn_dense(
        dst, me, rows, gm, w, g0 + g1 + g2 + g3, (token,))
    out_short, out_long = home(outs)
    lo, hi, token = halve(lo, got, (token, out_short, out_long))
    got = net.seq(hi, 1)
    got2 = net.dp(send2, net.core)
    lo, hi, token = halve(lo, got, (token,))
    got = net.seq(hi, 2)
    lo2, hi2, token = halve(keep2, got2, (token,))
    got2 = net.dp(hi2, net.first)
    v, token = plus(lo, got, (token,))
    v = net.rest(v)
    got = net.seq(v, 2)
    lo2, hi2, token = halve(lo2, got2, (token,))
    got2 = net.dp(hi2, net.second)
    v, token = join((v, got), (token,))
    got = net.seq(v, 1)
    u, token = plus(lo2, got2, (token,))
    got2 = net.seq(u, 1)
    v, token = join((v, got), (token,))
    got = net.dp(v, net.second)
    u, token = plus(u, got2, (token,), 2)
    got2 = net.seq(u, 2)
    v, token = join((v, got), (token,))
    far = net.dp(v, net.first)
    near = net.dp(v, net.core)
    first, token = finish(DENSE, 0, me, (v, near), (), (token,))
    d_rows, _ = tie(d_rows, token)
    dxs = lax.all_to_all(d_rows, "seq", 0, 0)
    u, token = plus(u, got2, (token,), 1)
    u = net.rest(u)
    got2 = net.dp(u, net.second)
    u, token = join((u, got2), (token,))
    far2 = net.dp(u, net.first)
    near2 = net.dp(u, net.core)
    (g_up, g_down, g_out, small), token = finish(DENSE, 1, me, (far, net.dp(far, net.core)), first, (token,))
    first2, token = finish(QKV, 0, me, (u, near2), (), (token,))
    (g_query, g_key, g_value), token = finish(QKV, 1, me, (far2, net.dp(far2, net.core)), first2, (token,))
    dx_short, dx_long = widen(dxs, token)
    dx_short = dx_short.reshape(2, 128, D)
    small = small.reshape(SLOTS, 8, 128)
    flat = small[:24, 0].reshape(-1)
    nr = (n_dev + 127) // 128
    g_alphas = jnp.sum(small[:6 * nr, 1].reshape(2, 3 * nr * 128), axis=1)
    return (out_short, out_long, dx_short, dx_long, g_query, g_key, g_value, g_out, flat[2560:3072], g_alphas,
            g_up, flat[:2048], g_down, flat[2048:2560])


def solution(mesh):
    split = P("dp", "seq", None)
    whole = P()
    return jax.shard_map(
        functools.partial(per_device, mesh.shape["dp"], mesh.shape["seq"]),
        mesh=mesh,
        in_specs=(split, P("seq"), split, P("seq")) + (whole,) * 10 + (split, split),
        out_specs=(split,) * 4 + (whole,) * 10,
        check_vma=False,
    )
```
